128 devices in a mesh: pde: 16 (over z_lo, y, core), sketch: 8 (over z_hi, x).
Axes of the slice: x: 4, y: 4, z: 4 (z_hi: 2, z_lo: 2; z = z_hi * 2 + z_lo), core: 2. Of those that a mesh axis runs over, the one named last changes fastest.
Arguments:
- probes: float32 [8, 32, 512, 512], P('sketch', 'pde'), may hold values from -6 to 6
- ply_labels: int32 [32, 512, 512], P('pde'), may hold values from 0 to 7
- conductivity: float32 [8], replicated, may hold values from 0.5 to 2
- sensors: int32 [32768], P('pde'), may hold values from 0 to 524287, as said below
- sensor_weight: float32 [32768], P('pde'), may hold values from 1 to 10
Outputs:
- basis: float32 [8, 32, 512, 512], P('sketch', 'pde')
- factor: float32 [8, 8], replicated
The draws below stay inside these ranges and needn't reach their ends.
Inputs may be any that keep to these rules, and one draw needn't show every extreme that they name: In the sensors of every slab the first index is 0 and the second is the slab's last cell.
All inputs are finite; a program needn't handle non-finite values.
Results may differ from the reference program's by a relative error of at most 0.0003.
Values sent between devices are 32-bit elements; how exact they have to be, the bound alone decides.
No kernel may reach another device: no remote copies, remote signals or barrier semaphores. Data moves between devices by JAX's collectives and lax.ppermute only.
A program may use at most 128 MiB of HBM per device.

```python
import math
import jax
import jax.numpy as jnp
from jax import lax

SX = 2
NY = 512
NZ = 512
SENS_DEV = 2048
STEPS = 4
PLIES = 8
NX = 32
PROBES = 8
SENSORS = 32768


def draw_sensors(key, part):
    key = jax.random.fold_in(key, 7)
    slab_cells = SX * NY * NZ
    picked = jax.random.randint(key, (SENSORS // SENS_DEV, SENS_DEV), 0, slab_cells)
    picked = picked.at[:, 0].set(0)
    picked = picked.at[:, 1].set(slab_cells - 1)
    return picked.reshape(-1).astype(jnp.int32)


def set_ends(result, key, least, high):
    spot = [jax.random.randint(jax.random.fold_in(key, axis), (), 0, length) for axis, length in enumerate(result.shape)]
    main_axis = result.shape.index(max(result.shape))
    next_to = spot[:main_axis] + [(spot[main_axis] + 1) % result.shape[main_axis]] + spot[main_axis + 1:]
    return result.at[tuple(spot)].set(least).at[tuple(next_to)].set(high)


def block_scale(stream_key, extent, split, least, top_value):
    def one(axis_at, parts):
        heights = jax.random.uniform(jax.random.fold_in(jax.random.fold_in(stream_key, 6), axis_at), (parts,), jnp.float32, least / len(split), top_value / len(split))
        return jnp.repeat(jnp.exp(heights), extent[axis_at] // parts).reshape((-1,) + (1,) * (len(extent) - axis_at - 1))

    gain = one(*split[0])
    for cut in split[1:]:
        gain = gain * one(*cut)
    return gain


def gaussian(stream_key, extent, scale, most, cuts=(), kind=jnp.bfloat16):
    values = jax.random.normal(stream_key, extent, jnp.float32) * scale
    if len(cuts) > 0:
        values = block_scale(stream_key, extent, cuts, -0.22, 0.18) * values
    return jnp.clip(values, min=-most, max=most).astype(kind)


def setup_inputs(seed: int = 0) -> dict:
    key_list = jax.random.split(jax.random.key(seed), 6)
    probes = gaussian(key_list[0], (PROBES, NX, NY, NZ), 1.0, 6.0, ((0, 8), (1, 16)), jnp.float32)
    ply_labels = set_ends(jax.random.randint(key_list[1], (NX, NY, NZ), 0, PLIES), jax.random.fold_in(key_list[1], 1), 0, PLIES - 1).astype(jnp.int32)
    conductivity = jnp.clip(jnp.exp(jax.random.uniform(key_list[2], (PLIES,), jnp.float32, math.log(0.5), math.log(2.0))), 0.5, 2.0)
    sensors = draw_sensors(jax.random.fold_in(key_list[5], 71), 0)
    sensor_weight = jnp.clip(jnp.exp(math.log(10.0) - 2.3025851 * jax.random.uniform(key_list[4], (SENSORS,), jnp.float32) ** block_scale(key_list[4], (SENSORS,), ((0, 16),), -0.2, 0.2)), 1.0, 10.0)
    return dict(probes=probes, ply_labels=ply_labels, conductivity=conductivity, sensors=sensors, sensor_weight=sensor_weight)


TIME_STEP = 0.15
PRIOR_WEIGHT = 0.1

def harmonic(left, right):
    return 2.0 * left * right / (left + right)

def face_values(padded_first, conduct):
    along_first = harmonic(padded_first[1:], padded_first[:-1])
    second_pad = jnp.pad(conduct, ((0, 0), (1, 1), (0, 0)))
    along_second = harmonic(second_pad[:, 1:], second_pad[:, :-1])
    third_pad = jnp.pad(conduct, ((0, 0), (0, 0), (1, 1)))
    along_third = harmonic(third_pad[:, :, 1:], third_pad[:, :, :-1])
    return (along_first, along_second, along_third)

def advance(fields, padded_first, faces):
    along_first, along_second, along_third = faces
    lead = [(0, 0)] * (fields.ndim - 3)
    flow = along_first * (padded_first[..., 1:, :, :] - padded_first[..., :-1, :, :])
    change = flow[..., 1:, :, :] - flow[..., :-1, :, :]
    second_pad = jnp.pad(fields, lead + [(0, 0), (1, 1), (0, 0)])
    flow = along_second * (second_pad[..., :, 1:, :] - second_pad[..., :, :-1, :])
    change = change + flow[..., :, 1:, :] - flow[..., :, :-1, :]
    third_pad = jnp.pad(fields, lead + [(0, 0), (0, 0), (1, 1)])
    flow = along_third * (third_pad[..., :, :, 1:] - third_pad[..., :, :, :-1])
    change = change + flow[..., :, :, 1:] - flow[..., :, :, :-1]
    return fields + TIME_STEP * change

def lookup(ply_labels, conductivity):
    kinds = jnp.arange(conductivity.shape[0], dtype=jnp.int32)
    chosen = ply_labels[None] == kinds[:, None, None, None]
    return jnp.sum(jnp.where(chosen, conductivity[:, None, None, None], jnp.zeros((), conductivity.dtype)), axis=0)

def lower_inverse(lower_factor):
    count = lower_factor.shape[0]
    identity = jnp.eye(count, dtype=lower_factor.dtype)

    def one_row(row, inverse):
        line = lax.dynamic_slice_in_dim(lower_factor, row, 1, 0)
        target = lax.dynamic_slice_in_dim(identity, row, 1, 0)
        pivot = jnp.sum(line * target)
        carried = jnp.dot(line, inverse, precision=lax.Precision.HIGHEST)
        return lax.dynamic_update_slice_in_dim(inverse, (target - carried) / pivot, row, 0)
    return lax.fori_loop(0, count, one_row, jnp.zeros_like(lower_factor))

def reference(probes, ply_labels, conductivity, sensors, sensor_weight):
    conduct = lookup(ply_labels, conductivity)
    faces = face_values(jnp.pad(conduct, ((1, 1), (0, 0), (0, 0))), conduct)
    slab_cells = SX * NY * NZ
    sensor_cells = sensors + jnp.arange(SENSORS, dtype=jnp.int32) // SENS_DEV * slab_cells

    def apply_one(probe):
        state = probe
        for repeat in range(STEPS):
            state = advance(state, jnp.pad(state, ((1, 1), (0, 0), (0, 0))), faces)
        flattened = state.reshape(-1)
        misfit = flattened[sensor_cells] * sensor_weight
        source = jnp.zeros_like(flattened).at[sensor_cells].add(misfit).reshape(probe.shape)
        for repeat in range(STEPS):
            source = advance(source, jnp.pad(source, ((1, 1), (0, 0), (0, 0))), faces)
        return source + PRIOR_WEIGHT * probe
    products = lax.map(apply_one, probes)
    flattened = products.reshape(PROBES, -1)
    gram_matrix = jnp.dot(flattened.astype(jnp.float32), flattened.T.astype(jnp.float32), precision=lax.Precision.HIGHEST, preferred_element_type=jnp.float32) / (NX * NY * NZ)
    lower_factor = jnp.linalg.cholesky(gram_matrix)
    inverse = lower_inverse(lower_factor)
    basis = jnp.dot(inverse.astype(jnp.float32), flattened.astype(jnp.float32), precision=lax.Precision.HIGHEST, preferred_element_type=jnp.float32)
    return (basis.reshape(products.shape), lower_factor.T)
```

```python
import functools

import jax
import jax.numpy as jnp
from jax import lax
from jax.experimental import pallas as pl
from jax.experimental.pallas import tpu as pltpu
from jax.sharding import PartitionSpec as P

STEPS = 4
TIME_STEP = 0.15
PRIOR_WEIGHT = 0.1

F32 = jnp.float32
BF16 = jnp.bfloat16
LANES = 128
NP = 8
NS = 16
NY = 512
NZ = 512
NU = 64
HALO = 8
ROWS = 48
COLS = 80
CORE_R = 32
CORE_C = 64
BLOCK = 64
VMEM = pltpu.MemorySpace.VMEM
VMEM_LIMIT = 60 * 1024 * 1024


def params(**kw):
    return pltpu.CompilerParams(vmem_limit_bytes=VMEM_LIMIT, **kw)


def lane_iota(shape=(8, LANES)):
    return lax.broadcasted_iota(jnp.int32, shape, len(shape) - 1)


def block_transpose(parts):
    lanes = lane_iota()
    parts = list(parts)
    for bit in range(4):
        shift = HALO << bit
        upper = (lanes & shift) != 0
        for m in range(16):
            if m & (1 << bit):
                continue
            a, b = parts[m], parts[m | (1 << bit)]
            parts[m] = jnp.where(upper, pltpu.roll(b, shift, 1), a)
            parts[m | (1 << bit)] = jnp.where(upper, b, pltpu.roll(a, LANES - shift, 1))
    return parts


def pack_probes_kernel(x_ref, o_ref, u_ref):
    step = pl.program_id(0)
    cols = NU

    @pl.when(step == 0)
    def _():
        u_ref[0:cols, :] = jnp.zeros((cols, LANES), F32)
        u_ref[cols * (NU + 1) : cols * (NU + 4), :] = jnp.zeros((3 * cols, LANES), F32)

    def group(g, carry):
        parts = [
            x_ref[0, p, pl.ds(g * 64 + r, 8, stride=8), :] for p in range(2) for r in range(8)
        ]
        for uc, part in enumerate(block_transpose(parts)):
            u_ref[pl.ds((1 + 8 * g) * cols + 16 * step + uc, 8, stride=cols), :] = part
        return carry

    lax.fori_loop(0, 8, group, 0)

    @pl.when(step == 3)
    def _():
        for b in range(8):

            def tile(a, carry, b=b):
                out = (b * NS + a) * BLOCK
                for i in range(6):
                    o_ref[pl.ds(out + 8 * i, 8), :] = u_ref[
                        pl.ds(pl.multiple_of((4 * a + i) * cols + 8 * b, 8), 8), :
                    ]
                if b > 0:
                    left = u_ref[pl.ds(4 * a * cols + 8 * b - 1, 8, stride=cols), :]
                else:
                    left = jnp.zeros((8, LANES), F32)
                o_ref[pl.ds(out + 48, 8), :] = left
                if b < 7:
                    right = u_ref[pl.ds(4 * a * cols + 8 * b + 8, 8, stride=cols), :]
                else:
                    right = jnp.zeros((8, LANES), F32)
                o_ref[pl.ds(out + 56, 8), :] = right
                return carry

            lax.fori_loop(0, NS, tile, 0)


def pack_probes(probes):
    return pl.pallas_call(
        pack_probes_kernel,
        grid=(4,),
        in_specs=[pl.BlockSpec((1, 2, NY, LANES), lambda j: (0, 0, 0, j))],
        out_specs=pl.BlockSpec((128 * BLOCK, LANES), lambda j: (0, 0)),
        out_shape=jax.ShapeDtypeStruct((128 * BLOCK, LANES), F32),
        scratch_shapes=[pltpu.VMEM((NU * (NU + 4), LANES), F32)],
        compiler_params=params(),
        cost_estimate=pl.CostEstimate(flops=8_000_000, bytes_accessed=12_000_000, transcendentals=0),
        name="pack_probes",
    )(probes)


CHUNK = 512


def pack_fields_kernel(kinds_ref, label_ref, sensor_ref, weight_ref, o_ref, cond_ref, dense_ref, u_ref):
    k = lax.axis_index("sketch")
    lanes = lane_iota()
    odd = lax.rem(k, 2)
    shift = 8 + 64 * odd
    first = lax.div(k + 1, 2) - 1
    first_at = pl.multiple_of(jnp.maximum(first, 0) * LANES, LANES)
    second_at = pl.multiple_of(jnp.minimum(first + 1, 3) * LANES, LANES)
    from_first = lanes < shift
    outside = (from_first & (first < 0)) | ((lanes >= shift) & (first + 1 > 3))

    def window(i, carry):
        for p in range(2):
            rows = pl.ds(pl.multiple_of(i * 8, 8), 8)
            a = label_ref[p, rows, pl.ds(first_at, LANES)]
            b = label_ref[p, rows, pl.ds(second_at, LANES)]
            label = jnp.where(from_first, pltpu.roll(a, shift, 1), pltpu.roll(b, shift, 1))
            cond = jnp.zeros((8, LANES), F32)
            for kind in range(8):
                cond = jnp.where(label == kind, kinds_ref[kind], cond)
            cond_ref[p, rows, :] = jnp.where(outside, 0.0, cond)
        return carry

    lax.fori_loop(0, NU, window, 0)

    dense_ref[...] = jnp.zeros_like(dense_ref)

    def chunk(j, carry):
        at = pl.ds(pl.multiple_of(j * CHUNK, CHUNK), CHUNK)
        cell = sensor_ref[:, at]
        weight = weight_ref[:, at]
        row = lax.shift_right_logical(cell, 9)
        col = (cell & (NZ - 1)) - (64 * k - HALO)
        by_row = (lax.broadcasted_iota(jnp.int32, (2 * NY, CHUNK), 0) == row).astype(F32).astype(BF16)
        hit = lax.broadcasted_iota(jnp.int32, (LANES, CHUNK), 0) == col
        part1 = weight.astype(BF16).astype(F32)
        rest = weight - part1
        part2 = rest.astype(BF16).astype(F32)
        part3 = rest - part2
        by_col = jnp.concatenate(
            [jnp.where(hit, part, 0.0).astype(BF16) for part in (part1, part2, part3)], axis=0
        )
        got = lax.dot_general(by_row, by_col, (((1,), (1,)), ((), ())), preferred_element_type=F32)
        got = (got[:, 0:LANES] + got[:, LANES : 2 * LANES]) + got[:, 2 * LANES :]
        dense_ref[...] += got.reshape(2, NY, LANES)
        return carry

    lax.fori_loop(0, 2048 // CHUNK, chunk, 0)

    cols = 16
    for f, src in enumerate((cond_ref, dense_ref)):
        u_ref[0:cols, :] = jnp.zeros((cols, LANES), F32)
        u_ref[cols * (NU + 1) : cols * (NU + 4), :] = jnp.zeros((3 * cols, LANES), F32)

        def group(g, carry, src=src):
            parts = [src[p, pl.ds(g * 64 + r, 8, stride=8), :] for p in range(2) for r in range(8)]
            for uc, part in enumerate(block_transpose(parts)):
                if uc < 10:
                    slot = (uc - 1) % 16
                    u_ref[pl.ds((1 + 8 * g) * cols + slot, 8, stride=cols), :] = part
            return carry

        lax.fori_loop(0, 8, group, 0)

        def tile(a, carry, f=f):
            out = (a * 2 + f) * BLOCK
            for i in range(6):
                o_ref[pl.ds(out + 8 * i, 8), :] = u_ref[
                    pl.ds(pl.multiple_of((4 * a + i) * cols, 8), 8), :
                ]
            o_ref[pl.ds(out + 48, 8), :] = u_ref[pl.ds(4 * a * cols + 15, 8, stride=cols), :]
            o_ref[pl.ds(out + 56, 8), :] = u_ref[pl.ds(4 * a * cols + 8, 8, stride=cols), :]
            return carry

        lax.fori_loop(0, NS, tile, 0)


def pack_fields(conductivity, labels, sensors, weights):
    return pl.pallas_call(
        pack_fields_kernel,
        in_specs=[pl.BlockSpec(memory_space=pltpu.SMEM)] + [pl.BlockSpec(memory_space=VMEM)] * 3,
        out_specs=pl.BlockSpec(memory_space=VMEM),
        out_shape=jax.ShapeDtypeStruct((NS * 2 * BLOCK, LANES), F32),
        scratch_shapes=[
            pltpu.VMEM((2, NY, LANES), F32),
            pltpu.VMEM((2, NY, LANES), F32),
            pltpu.VMEM((16 * (NU + 4), LANES), F32),
        ],
        compiler_params=params(),
        cost_estimate=pl.CostEstimate(flops=8_000_000, bytes_accessed=12_000_000, transcendentals=0),
        name="pack_fields",
    )(conductivity, labels, sensors.reshape(1, -1), weights.reshape(1, -1))


def unit_place(row):
    if row < 48:
        return row // 8, HALO + 8 * (row % 8)
    if row < 56:
        return row - 48, 0
    return row - 56, HALO + CORE_C


UNIT_ROWS = [row for row in range(BLOCK) if row % 8 < 6 or row < 48]


def harmonic(left, right):
    total = jnp.maximum(left + right, 1e-30)
    return (2.0 * TIME_STEP) * left * right / total


def fields_kernel(r_ref, fr_ref, fc_ref, fp_ref, d_ref, cond_ref):
    zero8 = jnp.zeros((8, LANES), F32)
    for p in range(2):

        def clear(i, carry, p=p):
            cond_ref[p, i, COLS : COLS + 8, :] = zero8
            fc_ref[p, i, 0:8, :] = zero8
            return carry

        lax.fori_loop(0, ROWS, clear, 0)

    def unpack(f, ref, row, ur, col):
        block = r_ref[pl.ds(f * BLOCK + row, NS, stride=2 * BLOCK), :]
        turned = jnp.concatenate([block] * NP, axis=0).T
        for p in range(2):
            for r in range(8):
                at = (p * 8 + r) * 8
                ref[p, ur * 8 + r, pl.ds(col, 8), :] = turned[at : at + 8]

    for f, ref in ((0, cond_ref), (1, d_ref)):

        def rows(ur, carry, f=f, ref=ref):
            for uc in range(8):
                unpack(f, ref, ur * 8 + uc, ur, HALO + 8 * uc)
            unpack(f, ref, 48 + ur, ur, 0)
            unpack(f, ref, 56 + ur, ur, HALO + CORE_C)
            return carry

        lax.fori_loop(0, 6, rows, 0)

    last_slab = (lane_iota() & (NS - 1)) == NS - 1

    def faces(i, carry):
        nxt = jnp.minimum(i + 1, ROWS - 1)
        for cb in range(10):
            at = pl.ds(8 * cb, 8)
            c0, c1 = cond_ref[0, i, at, :], cond_ref[1, i, at, :]
            fr_ref[0, i, at, :] = harmonic(c0, cond_ref[0, nxt, at, :])
            fr_ref[1, i, at, :] = harmonic(c1, cond_ref[1, nxt, at, :])
            aside = pl.ds(8 * cb + 1, 8)
            fc_ref[0, i, pl.ds(8 + 8 * cb, 8), :] = harmonic(c0, cond_ref[0, i, aside, :])
            fc_ref[1, i, pl.ds(8 + 8 * cb, 8), :] = harmonic(c1, cond_ref[1, i, aside, :])
            fp_ref[0, i, at, :] = harmonic(c0, c1)
            beyond = pltpu.roll(c0, LANES - 1, 1)
            fp_ref[1, i, at, :] = jnp.where(last_slab, 0.0, harmonic(c1, beyond))
        return carry

    lax.fori_loop(0, ROWS, faces, 0)


def make_fields(received):
    wide = jax.ShapeDtypeStruct((2, ROWS, COLS, LANES), F32)
    wider = jax.ShapeDtypeStruct((2, ROWS, COLS + 8, LANES), F32)
    return pl.pallas_call(
        fields_kernel,
        in_specs=[pl.BlockSpec(memory_space=VMEM)],
        out_specs=[pl.BlockSpec(memory_space=VMEM)] * 4,
        out_shape=[wide, wider, wide, wide],
        scratch_shapes=[pltpu.VMEM((2, ROWS, COLS + 8, LANES), F32)],
        compiler_params=params(),
        cost_estimate=pl.CostEstimate(flops=40_000_000, bytes_accessed=30_000_000, transcendentals=0),
        name="make_fields",
    )(received)


def solve_kernel(
    r_hbm, fr_hbm, fc_hbm, fp_hbm, d_hbm, prod_ref, gram_ref, r_ref, fr_ref, fc_ref, fp_ref, d_ref, ua_ref, ub_ref, sems
):
    copies = [
        pltpu.make_async_copy(src, dst, sems.at[i])
        for i, (src, dst) in enumerate(
            ((r_hbm, r_ref), (fr_hbm, fr_ref), (fc_hbm, fc_ref), (fp_hbm, fp_ref), (d_hbm, d_ref))
        )
    ]
    for copy in copies:
        copy.start()
    zero8 = jnp.zeros((8, LANES), F32)
    for ref in (ua_ref, ub_ref):
        for p in range(2):

            def clear(i, carry, p=p, ref=ref):
                ref[p, i, 0:8, :] = zero8
                ref[p, i, 8 + COLS : 16 + COLS, :] = zero8
                return carry

            lax.fori_loop(0, ROWS, clear, 0)
    copies[0].wait()

    def unpack(row, ur, col):
        turned = r_ref[pl.ds(row, LANES, stride=BLOCK), :].T
        for p in range(2):
            for r in range(8):
                at = (p * 8 + r) * 8
                ua_ref[p, ur * 8 + r, pl.ds(8 + col, 8), :] = turned[at : at + 8]
        return turned

    def rows(ur, carry):
        for uc in range(8):
            unpack(ur * 8 + uc, ur, HALO + 8 * uc)
        unpack(48 + ur, ur, 0)
        unpack(56 + ur, ur, HALO + CORE_C)
        return carry

    lax.fori_loop(0, 6, rows, 0)

    def keep(i, carry):
        for p in range(2):
            for cb in range(8):
                prod_ref[p, i, pl.ds(8 * cb, 8), :] = (
                    PRIOR_WEIGHT * ua_ref[p, i + HALO, pl.ds(8 + HALO + 8 * cb, 8), :]
                )
        return carry

    lax.fori_loop(0, CORE_R, keep, 0)
    for copy in copies[1:]:
        copy.wait()

    def advance(src, dst, step):
        last = step == 2 * STEPS
        blocks = range(1, 9) if last else range(10)

        def flow(p, i, cb):
            at = pl.ds(8 + 8 * cb, 8)
            return fr_ref[p, i, pl.ds(8 * cb, 8), :] * (src[p, i + 1, at, :] - src[p, i, at, :])

        def one_row(i, carry):
            flows, grams = carry
            new_flows = []
            for n, cb in enumerate(blocks):
                at = pl.ds(8 * cb, 8)
                mid = pl.ds(8 + 8 * cb, 8)
                right = pl.ds(9 + 8 * cb, 8)
                left = pl.ds(7 + 8 * cb, 8)
                u = [src[p, i, mid, :] for p in range(2)]
                new = []
                for p in range(2):
                    row_flow = fr_ref[p, i, at, :] * (src[p, i + 1, mid, :] - u[p])
                    change = row_flow - flows[2 * n + p]
                    new_flows.append(row_flow)
                    change += fc_ref[p, i, mid, :] * (src[p, i, right, :] - u[p])
                    change += fc_ref[p, i, left, :] * (src[p, i, left, :] - u[p])
                    new.append(u[p] + change)
                inner = fp_ref[0, i, at, :] * (u[1] - u[0])
                outer = fp_ref[1, i, at, :] * (pltpu.roll(u[0], LANES - 1, 1) - u[1])
                new[0] = new[0] + (inner - pltpu.roll(outer, 1, 1))
                new[1] = new[1] + (outer - inner)
                for p in range(2):
                    if step == STEPS:
                        new[p] = new[p] * d_ref[p, i, at, :]
                    if last:
                        core = pl.ds(8 * (cb - 1), 8)
                        x = prod_ref[p, i - HALO, core, :] + new[p]
                        prod_ref[p, i - HALO, core, :] = x
                        grams = tuple(
                            g + x * (x if d == 0 else pltpu.roll(x, NS * d, 1)) for d, g in enumerate(grams)
                        )
                    else:
                        dst[p, i, mid, :] = new[p]
            return tuple(new_flows), grams

        start = tuple(flow(p, step - 1, cb) for cb in blocks for p in range(2))
        grams = tuple(zero8 for d in range(5)) if last else ()
        return lax.fori_loop(step, ROWS - step, one_row, (start, grams))[1]

    refs = (ua_ref, ub_ref)
    for step in range(1, 2 * STEPS + 1):
        grams = advance(refs[(step - 1) % 2], refs[step % 2], step)

    lanes = lane_iota()
    packed = zero8
    for d in range(5):
        total = jnp.broadcast_to(jnp.sum(grams[d], axis=0, keepdims=True), (8, LANES))
        for shift in (8, 4, 2, 1):
            total = total + pltpu.roll(total, LANES - shift, 1)
        packed = jnp.where((lanes & (NS - 1)) == d, pltpu.roll(total, d, 1) if d else total, packed)
    gram_ref[...] = jnp.concatenate([packed] * (LANES // 8), axis=0)


def solve(received, faces):
    hbm = pl.BlockSpec(memory_space=pl.ANY)
    wide = pltpu.VMEM((2, ROWS, COLS, LANES), F32)
    return pl.pallas_call(
        solve_kernel,
        in_specs=[hbm] * 5,
        out_specs=[pl.BlockSpec(memory_space=VMEM)] * 2,
        out_shape=[
            jax.ShapeDtypeStruct((2, CORE_R, CORE_C, LANES), F32),
            jax.ShapeDtypeStruct((LANES, LANES), F32),
        ],
        scratch_shapes=[
            pltpu.VMEM((128 * BLOCK, LANES), F32),
            wide,
            pltpu.VMEM((2, ROWS, COLS + 8, LANES), F32),
            wide,
            wide,
            pltpu.VMEM((2, ROWS, COLS + 16, LANES), F32),
            pltpu.VMEM((2, ROWS, COLS + 16, LANES), F32),
            pltpu.SemaphoreType.DMA((5,)),
        ],
        compiler_params=params(),
        cost_estimate=pl.CostEstimate(flops=100_000_000, bytes_accessed=30_000_000, transcendentals=0),
        name="solve",
    )(received, *faces)


def basis_kernel(gram_ref, prod_ref, o_ref, factor_ref, *, cells):
    lanes = lane_iota()
    sublanes = lax.broadcasted_iota(jnp.int32, (8, LANES), 0)
    total = gram_ref[0:8, :]
    for i in range(1, LANES // 8):
        total = total + gram_ref[8 * i : 8 * i + 8, :]
    row = jnp.broadcast_to(jnp.sum(total, axis=0, keepdims=True), (8, LANES)) / cells

    def entry(i, j):
        d = (i - j) % NP
        at = i * NS + d if d <= 4 else j * NS + (NP - d)
        return jnp.broadcast_to(row[:, at : at + 1], (8, LANES))

    lower = {}
    inv_diag = []
    for j in range(NP):
        pivot = entry(j, j)
        for m in range(j):
            pivot = pivot - lower[j, m] * lower[j, m]
        lower[j, j] = jnp.sqrt(pivot)
        inv_diag.append(1.0 / lower[j, j])
        for i in range(j + 1, NP):
            value = entry(i, j)
            for m in range(j):
                value = value - lower[i, m] * lower[j, m]
            lower[i, j] = value * inv_diag[j]
    inverse = {}
    for i in range(NP):
        inverse[i, i] = inv_diag[i]
        for j in range(i):
            carried = lower[i, j] * inverse[j, j]
            for m in range(j + 1, i):
                carried = carried + lower[i, m] * inverse[m, j]
            inverse[i, j] = -carried * inv_diag[i]

    factor = jnp.zeros((8, LANES), F32)
    for (i, j), value in lower.items():
        factor = jnp.where((sublanes == j) & (lanes == i), value, factor)
    factor_ref[...] = factor

    probe = lax.shift_right_logical(lanes, 4)
    coefs = []
    for d in range(NP):
        coef = jnp.zeros((8, LANES), F32)
        for i in range(d, NP):
            coef = jnp.where(probe == i, inverse[i, i - d], coef)
        coefs.append(coef)

    def units(ur, carry):
        for uc in range(8):
            parts = []
            for p in range(2):
                for r in range(8):
                    x = prod_ref[p, ur * 8 + r, pl.ds(8 * uc, 8), :]
                    y = coefs[0] * x
                    for d in range(1, NP):
                        y = y + coefs[d] * pltpu.roll(x, NS * d, 1)
                    parts.append(y)
            o_ref[pl.ds(ur * 8 + uc, LANES, stride=32), :] = jnp.concatenate(parts, axis=0).T
        return carry

    lax.fori_loop(0, 4, units, 0)


def make_basis(grams, products):
    cells = float(2 * NS * NY * NZ)
    return pl.pallas_call(
        functools.partial(basis_kernel, cells=cells),
        in_specs=[pl.BlockSpec(memory_space=VMEM)] * 2,
        out_specs=[pl.BlockSpec(memory_space=VMEM)] * 2,
        out_shape=[
            jax.ShapeDtypeStruct((128 * 32, LANES), F32),
            jax.ShapeDtypeStruct((8, LANES), F32),
        ],
        compiler_params=params(),
        cost_estimate=pl.CostEstimate(flops=10_000_000, bytes_accessed=4_000_000, transcendentals=0),
        name="make_basis",
    )(grams, products)


def unpack_kernel(r_ref, o_ref):
    def group(g, carry):
        parts = [
            r_ref[pl.ds(b * 512 + g * 64 + uc, 8, stride=8), :] for b in range(2) for uc in range(8)
        ]
        turned = block_transpose(parts)
        for p in range(2):
            for r in range(8):
                o_ref[0, p, pl.ds(g * 64 + r, 8, stride=8), :] = turned[p * 8 + r]
        return carry

    lax.fori_loop(0, 8, group, 0)


def unpack_basis(received):
    return pl.pallas_call(
        unpack_kernel,
        grid=(4,),
        in_specs=[pl.BlockSpec((1024, LANES), lambda j: (j, 0))],
        out_specs=pl.BlockSpec((1, 2, NY, LANES), lambda j: (0, 0, 0, j)),
        out_shape=jax.ShapeDtypeStruct((1, 2, NY, NZ), F32),
        compiler_params=params(),
        cost_estimate=pl.CostEstimate(flops=8_000_000, bytes_accessed=4_000_000, transcendentals=0),
        name="unpack_basis",
    )(received)


def exchange(rows, axes):
    return lax.all_to_all(rows, axes, split_axis=0, concat_axis=0, tiled=True)


def on_device(probes, ply_labels, conductivity, sensors, sensor_weight):
    every = ("sketch", "pde")
    fields = exchange(pack_fields(conductivity, ply_labels, sensors, sensor_weight), "pde")
    tiles = exchange(pack_probes(probes), every)
    products, gram = solve(tiles, make_fields(fields))
    grams = exchange(gram, every)
    columns, factor = make_basis(grams, products)
    basis = unpack_basis(exchange(columns, every))
    return (basis, factor[:, :NP])


def solution(mesh):
    placed = (P("sketch", "pde", None, None), P("pde", None, None), P(), P("pde"), P("pde"))
    return jax.shard_map(
        on_device,
        mesh=mesh,
        in_specs=placed,
        out_specs=(P("sketch", "pde", None, None), P()),
        check_vma=False,
    )
```

```python
import functools

import jax
import jax.numpy as jnp
from jax import lax
from jax.experimental import pallas as pl
from jax.experimental.pallas import tpu as pltpu
from jax.sharding import PartitionSpec as P

STEPS = 4
TIME_STEP = 0.15
PRIOR_WEIGHT = 0.1

F32 = jnp.float32
BF16 = jnp.bfloat16
LANES = 128
NP = 8
NS = 16
NY = 512
NZ = 512
NU = 64
HALO = 8
ROWS = 48
COLS = 80
CORE_R = 32
CORE_C = 64
BLOCK = 64
VMEM = pltpu.MemorySpace.VMEM
VMEM_LIMIT = 60 * 1024 * 1024
UNROLL = 2


def params(**kw):
    return pltpu.CompilerParams(vmem_limit_bytes=VMEM_LIMIT, **kw)


def lane_iota(shape=(8, LANES)):
    return lax.broadcasted_iota(jnp.int32, shape, len(shape) - 1)


def scatter_groups(parts):
    group = lax.shift_right_logical(lane_iota(), 3)
    parts = [pltpu.roll(part, 8 * m, 1) if m else part for m, part in enumerate(parts)]
    for bit in range(4):
        ahead = (group & (1 << bit)) != 0
        parts = [jnp.where(ahead, parts[(i + (1 << bit)) % 16], parts[i]) for i in range(16)]
    return [parts[(-u) % 16] for u in range(16)]


def gather_groups(parts):
    group = lax.shift_right_logical(lane_iota(), 3)
    parts = [parts[(-i) % 16] for i in range(16)]
    for bit in range(4):
        behind = (group & (1 << bit)) != 0
        parts = [jnp.where(behind, parts[(i - (1 << bit)) % 16], parts[i]) for i in range(16)]
    return [pltpu.roll(part, LANES - 8 * m, 1) if m else part for m, part in enumerate(parts)]


def pack_probes_kernel(x_ref, o_ref, u_ref):
    step = pl.program_id(0)
    cols = NU

    @pl.when(step == 0)
    def _():
        u_ref[0:cols, :] = jnp.zeros((cols, LANES), F32)
        u_ref[cols * (NU + 1) : cols * (NU + 4), :] = jnp.zeros((3 * cols, LANES), F32)

    def group(g, carry):
        parts = [
            x_ref[0, p, pl.ds(g * 64 + r, 8, stride=8), :] for p in range(2) for r in range(8)
        ]
        for uc, part in enumerate(scatter_groups(parts)):
            u_ref[pl.ds((1 + 8 * g) * cols + 16 * step + uc, 8, stride=cols), :] = part
        return carry

    lax.fori_loop(0, 8, group, 0)

    @pl.when(step == 3)
    def _():
        for b in range(8):

            def tile(a, carry, b=b):
                out = (b * NS + a) * BLOCK
                for i in range(6):
                    o_ref[pl.ds(out + 8 * i, 8), :] = u_ref[
                        pl.ds(pl.multiple_of((4 * a + i) * cols + 8 * b, 8), 8), :
                    ]
                if b > 0:
                    left = u_ref[pl.ds(4 * a * cols + 8 * b - 1, 8, stride=cols), :]
                else:
                    left = jnp.zeros((8, LANES), F32)
                o_ref[pl.ds(out + 48, 8), :] = left
                if b < 7:
                    right = u_ref[pl.ds(4 * a * cols + 8 * b + 8, 8, stride=cols), :]
                else:
                    right = jnp.zeros((8, LANES), F32)
                o_ref[pl.ds(out + 56, 8), :] = right
                return carry

            lax.fori_loop(0, NS, tile, 0)


def pack_probes(probes):
    return pl.pallas_call(
        pack_probes_kernel,
        grid=(4,),
        in_specs=[pl.BlockSpec((1, 2, NY, LANES), lambda j: (0, 0, 0, j))],
        out_specs=pl.BlockSpec((128 * BLOCK, LANES), lambda j: (0, 0)),
        out_shape=jax.ShapeDtypeStruct((128 * BLOCK, LANES), F32),
        scratch_shapes=[pltpu.VMEM((NU * (NU + 4), LANES), F32)],
        compiler_params=params(),
        cost_estimate=pl.CostEstimate(flops=8_000_000, bytes_accessed=12_000_000, transcendentals=0),
        name="pack_probes",
    )(probes)


CHUNK = 512


def pack_fields_kernel(kinds_ref, label_ref, sensor_ref, weight_ref, o_ref, cond_ref, dense_ref, u_ref):
    k = lax.axis_index("sketch")
    lanes = lane_iota()
    odd = lax.rem(k, 2)
    shift = 8 + 64 * odd
    first = lax.div(k + 1, 2) - 1
    first_at = pl.multiple_of(jnp.maximum(first, 0) * LANES, LANES)
    second_at = pl.multiple_of(jnp.minimum(first + 1, 3) * LANES, LANES)
    from_first = lanes < shift
    outside = (from_first & (first < 0)) | ((lanes >= shift) & (first + 1 > 3))

    def window(i, carry):
        for p in range(2):
            rows = pl.ds(pl.multiple_of(i * 8, 8), 8)
            a = label_ref[p, rows, pl.ds(first_at, LANES)]
            b = label_ref[p, rows, pl.ds(second_at, LANES)]
            label = jnp.where(from_first, pltpu.roll(a, shift, 1), pltpu.roll(b, shift, 1))
            cond = jnp.zeros((8, LANES), F32)
            for kind in range(8):
                cond = jnp.where(label == kind, kinds_ref[kind], cond)
            cond_ref[p, rows, :] = jnp.where(outside, 0.0, cond)
        return carry

    lax.fori_loop(0, NU, window, 0)

    dense_ref[...] = jnp.zeros_like(dense_ref)

    def chunk(j, carry):
        at = pl.ds(pl.multiple_of(j * CHUNK, CHUNK), CHUNK)
        cell = sensor_ref[:, at]
        weight = weight_ref[:, at]
        row = lax.shift_right_logical(cell, 9)
        col = (cell & (NZ - 1)) - (64 * k - HALO)
        by_row = (lax.broadcasted_iota(jnp.int32, (2 * NY, CHUNK), 0) == row).astype(F32).astype(BF16)
        hit = lax.broadcasted_iota(jnp.int32, (LANES, CHUNK), 0) == col
        part1 = weight.astype(BF16).astype(F32)
        rest = weight - part1
        by_col = jnp.concatenate([jnp.where(hit, part, 0.0).astype(BF16) for part in (part1, rest)], axis=0)
        got = lax.dot_general(by_row, by_col, (((1,), (1,)), ((), ())), preferred_element_type=F32)
        got = got[:, 0:LANES] + got[:, LANES:]
        dense_ref[...] += got.reshape(2, NY, LANES)
        return carry

    lax.fori_loop(0, 2048 // CHUNK, chunk, 0)

    cols = 16
    for f, src in enumerate((cond_ref, dense_ref)):
        u_ref[0:cols, :] = jnp.zeros((cols, LANES), F32)
        u_ref[cols * (NU + 1) : cols * (NU + 4), :] = jnp.zeros((3 * cols, LANES), F32)

        def group(g, carry, src=src):
            parts = [src[p, pl.ds(g * 64 + r, 8, stride=8), :] for p in range(2) for r in range(8)]
            for uc, part in enumerate(scatter_groups(parts)):
                if uc < 10:
                    slot = (uc - 1) % 16
                    u_ref[pl.ds((1 + 8 * g) * cols + slot, 8, stride=cols), :] = part
            return carry

        lax.fori_loop(0, 8, group, 0)

        def tile(a, carry, f=f):
            out = (a * 2 + f) * BLOCK
            for i in range(6):
                o_ref[pl.ds(out + 8 * i, 8), :] = u_ref[
                    pl.ds(pl.multiple_of((4 * a + i) * cols, 8), 8), :
                ]
            o_ref[pl.ds(out + 48, 8), :] = u_ref[pl.ds(4 * a * cols + 15, 8, stride=cols), :]
            o_ref[pl.ds(out + 56, 8), :] = u_ref[pl.ds(4 * a * cols + 8, 8, stride=cols), :]
            return carry

        lax.fori_loop(0, NS, tile, 0)


def pack_fields(conductivity, labels, sensors, weights):
    return pl.pallas_call(
        pack_fields_kernel,
        in_specs=[pl.BlockSpec(memory_space=pltpu.SMEM)] + [pl.BlockSpec(memory_space=VMEM)] * 3,
        out_specs=pl.BlockSpec(memory_space=VMEM),
        out_shape=jax.ShapeDtypeStruct((NS * 2 * BLOCK, LANES), F32),
        scratch_shapes=[
            pltpu.VMEM((2, NY, LANES), F32),
            pltpu.VMEM((2, NY, LANES), F32),
            pltpu.VMEM((16 * (NU + 4), LANES), F32),
        ],
        compiler_params=params(),
        cost_estimate=pl.CostEstimate(flops=8_000_000, bytes_accessed=12_000_000, transcendentals=0),
        name="pack_fields",
    )(conductivity, labels, sensors.reshape(1, -1), weights.reshape(1, -1))


def unit_place(row):
    if row < 48:
        return row // 8, HALO + 8 * (row % 8)
    if row < 56:
        return row - 48, 0
    return row - 56, HALO + CORE_C


UNIT_ROWS = [row for row in range(BLOCK) if row % 8 < 6 or row < 48]


def harmonic(left, right):
    total = jnp.maximum(left + right, 1e-30)
    return (2.0 * TIME_STEP) * left * right / total


def fields_kernel(r_ref, fr_ref, fc_ref, fp_ref, d_ref, cond_ref):
    zero8 = jnp.zeros((8, LANES), F32)
    for p in range(2):

        def clear(i, carry, p=p):
            cond_ref[p, i, COLS : COLS + 8, :] = zero8
            fc_ref[p, i, 0:8, :] = zero8
            return carry

        lax.fori_loop(0, ROWS, clear, 0)

    def unpack(f, ref, row, ur, col):
        block = r_ref[pl.ds(f * BLOCK + row, NS, stride=2 * BLOCK), :]
        turned = jnp.concatenate([block] * NP, axis=0).T
        for g in range(16):
            m = (g - col // 8) % 16
            ref[m // 8, ur * 8 + m % 8, pl.ds(col, 8), :] = turned[8 * g : 8 * g + 8]

    for f, ref in ((0, cond_ref), (1, d_ref)):

        def rows(ur, carry, f=f, ref=ref):
            for uc in range(8):
                unpack(f, ref, ur * 8 + uc, ur, HALO + 8 * uc)
            unpack(f, ref, 48 + ur, ur, 0)
            unpack(f, ref, 56 + ur, ur, HALO + CORE_C)
            return carry

        lax.fori_loop(0, 6, rows, 0)

    last_slab = (lane_iota() & (NS - 1)) == NS - 1

    def faces(i, carry):
        nxt = jnp.minimum(i + 1, ROWS - 1)
        for cb in range(10):
            at = pl.ds(8 * cb, 8)
            c0, c1 = cond_ref[0, i, at, :], cond_ref[1, i, at, :]
            fr_ref[0, i, at, :] = harmonic(c0, cond_ref[0, nxt, at, :])
            fr_ref[1, i, at, :] = harmonic(c1, cond_ref[1, nxt, at, :])
            aside = pl.ds(8 * cb + 1, 8)
            fc_ref[0, i, pl.ds(8 + 8 * cb, 8), :] = harmonic(c0, cond_ref[0, i, aside, :])
            fc_ref[1, i, pl.ds(8 + 8 * cb, 8), :] = harmonic(c1, cond_ref[1, i, aside, :])
            fp_ref[0, i, at, :] = harmonic(c0, c1)
            beyond = pltpu.roll(c0, LANES - 1, 1)
            outer = jnp.where(last_slab, 0.0, harmonic(c1, beyond))
            fp_ref[1, i, at, :] = outer
            fp_ref[2, i, at, :] = pltpu.roll(outer, 1, 1)
        return carry

    lax.fori_loop(0, ROWS, faces, 0)


def make_fields(received):
    wide = jax.ShapeDtypeStruct((2, ROWS, COLS, LANES), F32)
    wider = jax.ShapeDtypeStruct((2, ROWS, COLS + 8, LANES), F32)
    return pl.pallas_call(
        fields_kernel,
        in_specs=[pl.BlockSpec(memory_space=VMEM)],
        out_specs=[pl.BlockSpec(memory_space=VMEM)] * 4,
        out_shape=[wide, wider, jax.ShapeDtypeStruct((3, ROWS, COLS, LANES), F32), wide],
        scratch_shapes=[pltpu.VMEM((2, ROWS, COLS + 8, LANES), F32)],
        compiler_params=params(),
        cost_estimate=pl.CostEstimate(flops=40_000_000, bytes_accessed=30_000_000, transcendentals=0),
        name="make_fields",
    )(received)


PADDED = BLOCK + 8


def solve_kernel(
    r_hbm, fr_hbm, fc_hbm, fp_hbm, d_hbm, y_ref, gram_ref, r_ref, fr_ref, fc_ref, fp_ref, d_ref, ua_ref, ub_ref, prod_ref, sems
):
    copies = [
        pltpu.make_async_copy(src, dst, sems.at[i])
        for i, (src, dst) in enumerate(
            (
                (r_hbm, r_ref.at[:, 0:BLOCK, :]),
                (fr_hbm, fr_ref),
                (fc_hbm, fc_ref),
                (fp_hbm, fp_ref),
                (d_hbm, d_ref),
            )
        )
    ]
    for copy in copies:
        copy.start()
    odd = lax.rem(lax.axis_index("sketch"), 2)
    zero8 = jnp.zeros((8, LANES), F32)
    for ref in (ua_ref, ub_ref):
        for p in range(2):

            def clear(i, carry, p=p, ref=ref):
                ref[p, i, 0:8, :] = zero8
                ref[p, i, 8 + COLS : 16 + COLS, :] = zero8
                return carry

            lax.fori_loop(0, ROWS, clear, 0)
    copies[0].wait()
    flat_ref = r_ref.reshape(LANES * PADDED, LANES)

    def unpack(row, ur, col):
        turned = flat_ref[pl.ds(row, LANES, stride=PADDED), :].T
        for g in range(16):
            m = (g - (col // 8 - 1)) % 16
            ua_ref[lax.rem(m // 8 + odd, 2), ur * 8 + m % 8, pl.ds(8 + col, 8), :] = turned[8 * g : 8 * g + 8]

    def rows(ur, carry):
        for uc in range(8):
            unpack(ur * 8 + uc, ur, HALO + 8 * uc)
        unpack(48 + ur, ur, 0)
        unpack(56 + ur, ur, HALO + CORE_C)
        return carry

    lax.fori_loop(0, 6, rows, 0)

    def keep(i, carry):
        for p in range(2):
            for cb in range(8):
                prod_ref[p, i, pl.ds(8 * cb, 8), :] = (
                    PRIOR_WEIGHT * ua_ref[p, i + HALO, pl.ds(8 + HALO + 8 * cb, 8), :]
                )
        return carry

    lax.fori_loop(0, CORE_R, keep, 0)
    for copy in copies[1:]:
        copy.wait()

    def advance(src, dst, step):
        last = step == 2 * STEPS
        blocks = range(1, 9) if last else range(10)

        def flow(p, i, cb):
            at = pl.ds(8 + 8 * cb, 8)
            return fr_ref[p, i, pl.ds(8 * cb, 8), :] * (src[p, i + 1, at, :] - src[p, i, at, :])

        def one_row(i, flows):
            mids = [pl.ds(8 + 8 * cb, 8) for cb in blocks]
            beyond = [
                (pltpu.roll(src[0, i, mid, :], LANES - 1, 1), pltpu.roll(src[1, i, mid, :], 1, 1)) for mid in mids
            ]
            new_flows = []
            new = []
            for n, (cb, mid) in enumerate(zip(blocks, mids)):
                at = pl.ds(8 * cb, 8)
                right = pl.ds(9 + 8 * cb, 8)
                left = pl.ds(7 + 8 * cb, 8)
                for p in range(2):
                    u = src[p, i, mid, :]
                    row_flow = fr_ref[p, i, at, :] * (src[p, i + 1, mid, :] - u)
                    change = row_flow - flows[2 * n + p]
                    new_flows.append(row_flow)
                    change += fc_ref[p, i, mid, :] * (src[p, i, right, :] - u)
                    change += fc_ref[p, i, left, :] * (src[p, i, left, :] - u)
                    new.append(u + change)
            for n, (cb, mid) in enumerate(zip(blocks, mids)):
                at = pl.ds(8 * cb, 8)
                u = [src[p, i, mid, :] for p in range(2)]
                inner = fp_ref[0, i, at, :] * (u[1] - u[0])
                below = fp_ref[2, i, at, :] * (beyond[n][1] - u[0])
                above = fp_ref[1, i, at, :] * (beyond[n][0] - u[1])
                both = [new[2 * n] + (below + inner), new[2 * n + 1] + (above - inner)]
                for p in range(2):
                    if step == STEPS:
                        both[p] = both[p] * d_ref[p, i, at, :]
                    if last:
                        core = pl.ds(8 * (cb - 1), 8)
                        prod_ref[p, i - HALO, core, :] += both[p]
                    else:
                        dst[p, i, mid, :] = both[p]
            return tuple(new_flows)

        start = tuple(flow(p, step - 1, cb) for cb in blocks for p in range(2))
        lax.fori_loop(step, ROWS - step, one_row, start, unroll=UNROLL)

    refs = (ua_ref, ub_ref)
    for step in range(1, 2 * STEPS + 1):
        advance(refs[(step - 1) % 2], refs[step % 2], step)

    def units(ur, gram):
        for uc in range(8):
            parts = []
            for g in range(16):
                m = (g - uc) % 16
                parts.append(prod_ref[lax.rem(m // 8 + odd, 2), ur * 8 + m % 8, pl.ds(8 * uc, 8), :])
            turned = jnp.concatenate(parts, axis=0).T
            y_ref[ur * 8 + uc] = turned
            gram = gram + lax.dot_general(
                turned,
                turned,
                (((1,), (1,)), ((), ())),
                precision=lax.Precision.HIGHEST,
                preferred_element_type=F32,
            )
        return gram

    gram = lax.fori_loop(0, 4, units, jnp.zeros((LANES, LANES), F32))
    slab_of_row = lax.broadcasted_iota(jnp.int32, (LANES, LANES), 0) & (NS - 1)
    slab_of_lane = lax.broadcasted_iota(jnp.int32, (LANES, LANES), 1) & (NS - 1)
    gram = jnp.where(slab_of_row == slab_of_lane, gram, 0.0)
    by_probe = jnp.sum(gram.reshape(NP, NS, LANES), axis=1)
    same = (
        lax.shift_right_logical(lax.broadcasted_iota(jnp.int32, (LANES, LANES), 0), 4)
        == lax.shift_right_logical(lax.broadcasted_iota(jnp.int32, (LANES, LANES), 1), 4)
    ).astype(F32)
    by_probe = jnp.dot(by_probe, same, precision=lax.Precision.HIGHEST, preferred_element_type=F32)
    own = (lane_iota() & (NS - 1)) == lax.broadcasted_iota(jnp.int32, (8, LANES), 0)
    row = jnp.sum(jnp.where(own, by_probe, 0.0), axis=0, keepdims=True)
    gram_ref[...] = jnp.broadcast_to(row, (LANES, LANES))


def solve(received, faces):
    hbm = pl.BlockSpec(memory_space=pl.ANY)
    wide = pltpu.VMEM((2, ROWS, COLS, LANES), F32)
    return pl.pallas_call(
        solve_kernel,
        in_specs=[hbm] * 5,
        out_specs=[pl.BlockSpec(memory_space=VMEM)] * 2,
        out_shape=[
            jax.ShapeDtypeStruct((32, LANES, LANES), F32),
            jax.ShapeDtypeStruct((LANES, LANES), F32),
        ],
        scratch_shapes=[
            pltpu.VMEM((LANES, PADDED, LANES), F32),
            wide,
            pltpu.VMEM((2, ROWS, COLS + 8, LANES), F32),
            pltpu.VMEM((3, ROWS, COLS, LANES), F32),
            wide,
            pltpu.VMEM((2, ROWS, COLS + 16, LANES), F32),
            pltpu.VMEM((2, ROWS, COLS + 16, LANES), F32),
            pltpu.VMEM((2, CORE_R, CORE_C, LANES), F32),
            pltpu.SemaphoreType.DMA((5,)),
        ],
        compiler_params=params(),
        cost_estimate=pl.CostEstimate(flops=100_000_000, bytes_accessed=30_000_000, transcendentals=0),
        name="solve",
    )(received.reshape(LANES, BLOCK, LANES), *faces)


def basis_kernel(gram_ref, y_ref, o_ref, factor_ref, *, cells):
    lanes = lane_iota()
    sublanes = lax.broadcasted_iota(jnp.int32, (8, LANES), 0)
    total = gram_ref[0:8, :]
    for i in range(1, LANES // 8):
        total = total + gram_ref[8 * i : 8 * i + 8, :]
    row = jnp.broadcast_to(jnp.sum(total, axis=0, keepdims=True), (8, LANES)) / cells

    def entry(i, j):
        at = j * NS + i
        return jnp.broadcast_to(row[:, at : at + 1], (8, LANES))

    lower = {}
    inv_diag = []
    for j in range(NP):
        pivot = entry(j, j)
        for m in range(j):
            pivot = pivot - lower[j, m] * lower[j, m]
        lower[j, j] = jnp.sqrt(pivot)
        inv_diag.append(1.0 / lower[j, j])
        for i in range(j + 1, NP):
            value = entry(i, j)
            for m in range(j):
                value = value - lower[i, m] * lower[j, m]
            lower[i, j] = value * inv_diag[j]
    inverse = {}
    for i in range(NP):
        inverse[i, i] = inv_diag[i]
        for j in range(i):
            carried = lower[i, j] * inverse[j, j]
            for m in range(j + 1, i):
                carried = carried + lower[i, m] * inverse[m, j]
            inverse[i, j] = -carried * inv_diag[i]

    factor = jnp.zeros((8, LANES), F32)
    for (i, j), value in lower.items():
        factor = jnp.where((sublanes == j) & (lanes == i), value, factor)
    factor_ref[...] = factor

    probe = lax.shift_right_logical(lanes, 4)
    mix = []
    for i in range(NP):
        coef = jnp.zeros((8, LANES), F32)
        for j in range(i + 1):
            coef = jnp.where(probe == j, inverse[i, j], coef)
        for half in range(2):
            mix.append(jnp.where((lanes & (NS - 1)) == sublanes + 8 * half, coef, 0.0))
    mix = jnp.concatenate(mix, axis=0)

    def units(ur, carry):
        for uc in range(8):
            o_ref[pl.ds(ur * 8 + uc, LANES, stride=32), :] = jnp.dot(
                mix, y_ref[ur * 8 + uc], precision=lax.Precision.HIGHEST, preferred_element_type=F32
            )
        return carry

    lax.fori_loop(0, 4, units, 0)


def make_basis(grams, products):
    cells = float(2 * NS * NY * NZ)
    return pl.pallas_call(
        functools.partial(basis_kernel, cells=cells),
        in_specs=[pl.BlockSpec(memory_space=VMEM)] * 2,
        out_specs=[pl.BlockSpec(memory_space=VMEM)] * 2,
        out_shape=[
            jax.ShapeDtypeStruct((128 * 32, LANES), F32),
            jax.ShapeDtypeStruct((8, LANES), F32),
        ],
        compiler_params=params(),
        cost_estimate=pl.CostEstimate(flops=10_000_000, bytes_accessed=4_000_000, transcendentals=0),
        name="make_basis",
    )(grams, products)


def unpack_kernel(r_ref, o_ref):
    def group(g, carry):
        parts = [
            r_ref[pl.ds(b * 512 + g * 64 + uc, 8, stride=8), :] for b in range(2) for uc in range(8)
        ]
        turned = gather_groups(parts)
        for p in range(2):
            for r in range(8):
                o_ref[0, p, pl.ds(g * 64 + r, 8, stride=8), :] = turned[p * 8 + r]
        return carry

    lax.fori_loop(0, 8, group, 0)


def unpack_basis(received):
    return pl.pallas_call(
        unpack_kernel,
        grid=(4,),
        in_specs=[pl.BlockSpec((1024, LANES), lambda j: (j, 0))],
        out_specs=pl.BlockSpec((1, 2, NY, LANES), lambda j: (0, 0, 0, j)),
        out_shape=jax.ShapeDtypeStruct((1, 2, NY, NZ), F32),
        compiler_params=params(),
        cost_estimate=pl.CostEstimate(flops=8_000_000, bytes_accessed=4_000_000, transcendentals=0),
        name="unpack_basis",
    )(received)


def exchange(rows, axes):
    return lax.all_to_all(rows, axes, split_axis=0, concat_axis=0, tiled=True)


def on_device(probes, ply_labels, conductivity, sensors, sensor_weight):
    every = ("sketch", "pde")
    fields = exchange(pack_fields(conductivity, ply_labels, sensors, sensor_weight), "pde")
    tiles = exchange(pack_probes(probes), every)
    products, gram = solve(tiles, make_fields(fields))
    grams = exchange(gram, every)
    columns, factor = make_basis(grams, products)
    basis = unpack_basis(exchange(columns, every))
    return (basis, factor[:, :NP])


def solution(mesh):
    placed = (P("sketch", "pde", None, None), P("pde", None, None), P(), P("pde"), P("pde"))
    return jax.shard_map(
        on_device,
        mesh=mesh,
        in_specs=placed,
        out_specs=(P("sketch", "pde", None, None), P()),
        check_vma=False,
    )
```

```python
import functools

import jax
import jax.numpy as jnp
from jax import lax
from jax.experimental import pallas as pl
from jax.experimental.pallas import tpu as pltpu
from jax.sharding import PartitionSpec as P

STEPS = 4
TIME_STEP = 0.15
PRIOR_WEIGHT = 0.1

F32 = jnp.float32
BF16 = jnp.bfloat16
LANES = 128
NP = 8
NS = 16
NY = 512
NZ = 512
NU = 64
HALO = 8
ROWS = 48
COLS = 80
CORE_R = 32
CORE_C = 64
BLOCK = 60
FIELD_BLOCK = 64
VMEM = pltpu.MemorySpace.VMEM
UNROLL = 4
WIDTH = 10
VIA_SCRATCH = False


def params(mebibytes):
    return pltpu.CompilerParams(vmem_limit_bytes=mebibytes * 1024 * 1024)


def in_hbm(*arrays):
    return [pltpu.with_memory_space_constraint(array, pltpu.HBM) for array in arrays]


def lane_iota(shape=(8, LANES)):
    return lax.broadcasted_iota(jnp.int32, shape, len(shape) - 1)


def scatter_groups(parts):
    group = lax.shift_right_logical(lane_iota(), 3)
    parts = [pltpu.roll(part, 8 * m, 1) if m else part for m, part in enumerate(parts)]
    for bit in range(4):
        ahead = (group & (1 << bit)) != 0
        parts = [jnp.where(ahead, parts[(i + (1 << bit)) % 16], parts[i]) for i in range(16)]
    return [parts[(-u) % 16] for u in range(16)]


def gather_groups(parts):
    group = lax.shift_right_logical(lane_iota(), 3)
    parts = [parts[(-i) % 16] for i in range(16)]
    for bit in range(4):
        behind = (group & (1 << bit)) != 0
        parts = [jnp.where(behind, parts[(i - (1 << bit)) % 16], parts[i]) for i in range(16)]
    return [pltpu.roll(part, LANES - 8 * m, 1) if m else part for m, part in enumerate(parts)]


def pack_probes_kernel(x_ref, o_ref, u_ref):
    step = pl.program_id(0)
    cols = NU

    @pl.when(step == 0)
    def _():
        u_ref[0:cols, :] = jnp.zeros((cols, LANES), F32)
        u_ref[cols * (NU + 1) : cols * (NU + 4), :] = jnp.zeros((3 * cols, LANES), F32)

    def group(g, carry):
        parts = [
            x_ref[0, p, pl.ds(g * 64 + r, 8, stride=8), :] for p in range(2) for r in range(8)
        ]
        for uc, part in enumerate(scatter_groups(parts)):
            u_ref[pl.ds((1 + 8 * g) * cols + 16 * step + uc, 8, stride=cols), :] = part
        return carry

    lax.fori_loop(0, 8, group, 0)

    @pl.when(step == 3)
    def _():
        for b in range(8):

            def tile(a, carry, b=b):
                out = (b * NS + a) * BLOCK
                for i in range(6):
                    o_ref[pl.ds(out + 8 * i, 8), :] = u_ref[
                        pl.ds(pl.multiple_of((4 * a + i) * cols + 8 * b, 8), 8), :
                    ]
                if b > 0:
                    left = u_ref[pl.ds(4 * a * cols + 8 * b - 1, 6, stride=cols), :]
                else:
                    left = jnp.zeros((6, LANES), F32)
                o_ref[pl.ds(out + 48, 6), :] = left
                if b < 7:
                    right = u_ref[pl.ds(4 * a * cols + 8 * b + 8, 6, stride=cols), :]
                else:
                    right = jnp.zeros((6, LANES), F32)
                o_ref[pl.ds(out + 54, 6), :] = right
                return carry

            lax.fori_loop(0, NS, tile, 0)


def pack_probes(probes):
    return pl.pallas_call(
        pack_probes_kernel,
        grid=(4,),
        in_specs=[pl.BlockSpec((1, 2, NY, LANES), lambda j: (0, 0, 0, j))],
        out_specs=pl.BlockSpec((128 * BLOCK, LANES), lambda j: (0, 0)),
        out_shape=jax.ShapeDtypeStruct((128 * BLOCK, LANES), F32),
        scratch_shapes=[pltpu.VMEM((NU * (NU + 4), LANES), F32)],
        compiler_params=params(14),
        cost_estimate=pl.CostEstimate(flops=8_000_000, bytes_accessed=12_000_000, transcendentals=0),
        name="pack_probes",
    )(probes)


CHUNK = 256


def pack_fields_kernel(
    kinds_hbm,
    label_hbm,
    sensor_hbm,
    weight_hbm,
    o_ref,
    kinds_ref,
    sensor_ref,
    weight_ref,
    label_ref,
    cond_ref,
    dense_ref,
    u_ref,
    row_ref,
    col_ref,
    sems,
):
    k = lax.axis_index("sketch")
    lanes = lane_iota()
    shift = 8 + 64 * lax.rem(k, 2)
    first = lax.div(k + 1, 2) - 1
    start = jnp.clip(first, 0, 2)
    window_hbm = label_hbm.at[:, :, pl.ds(pl.multiple_of(start * LANES, LANES), 2 * LANES)]
    copies = [
        pltpu.make_async_copy(src, dst, sems.at[i])
        for i, (src, dst) in enumerate(
            (
                (sensor_hbm, sensor_ref),
                (weight_hbm, weight_ref),
                (kinds_hbm, kinds_ref),
                (window_hbm, label_ref),
            )
        )
    ]
    for copy in copies:
        copy.start()
    for copy in copies[:3]:
        copy.wait()

    def chunk(j, carry):
        at = pl.ds(pl.multiple_of(j * CHUNK, CHUNK), CHUNK)
        cell = sensor_ref[:, at]
        weight = weight_ref[:, at]
        plane = lax.shift_right_logical(cell, 18)
        row = lax.shift_right_logical(cell, 9) & (NY - 1)
        col = (cell & (NZ - 1)) - (64 * k - HALO)
        col = jnp.where((col >= 0) & (col < COLS), plane * LANES + col, -1)
        part = weight.astype(BF16).astype(F32)
        rest = weight - part
        index = lax.broadcasted_iota(jnp.int32, (2 * LANES, CHUNK), 0)
        for half in range(2):
            hit = index + 2 * LANES * half == row
            row_ref[pl.ds(2 * LANES * half, 2 * LANES), at] = jnp.where(hit, 1.0, 0.0).astype(BF16)
        hit = index == col
        col_ref[0 : 2 * LANES, at] = jnp.where(hit, part, 0.0).astype(BF16)
        col_ref[2 * LANES :, at] = jnp.where(hit, rest, 0.0).astype(BF16)
        return carry

    lax.fori_loop(0, 2048 // CHUNK, chunk, 0)
    got = lax.dot_general(row_ref[...], col_ref[...], (((1,), (1,)), ((), ())), preferred_element_type=F32)
    for p in range(2):
        dense_ref[p] = got[:, p * LANES : (p + 1) * LANES] + got[:, (p + 2) * LANES : (p + 3) * LANES]

    copies[3].wait()
    place = first - start
    first_at = pl.multiple_of(jnp.maximum(place, 0) * LANES, LANES)
    second_at = pl.multiple_of(jnp.minimum(place + 1, 1) * LANES, LANES)
    from_first = lanes < shift
    outside = (from_first & (first < 0)) | ((lanes >= shift) & (first + 1 > 3))

    def window(i, carry):
        for q in range(4):
            rows = pl.ds(pl.multiple_of(i * 32 + q * 8, 8), 8)
            for p in range(2):
                a = label_ref[p, rows, pl.ds(first_at, LANES)]
                b = label_ref[p, rows, pl.ds(second_at, LANES)]
                label = jnp.where(from_first, pltpu.roll(a, shift, 1), pltpu.roll(b, shift, 1))
                cond = jnp.zeros((8, LANES), F32)
                for kind in range(8):
                    cond = jnp.where(label == kind, kinds_ref[kind], cond)
                cond_ref[p, rows, :] = jnp.where(outside, 0.0, cond)
        return carry

    lax.fori_loop(0, NU // 4, window, 0)

    cols = 16
    span = cols * (NU + 4)
    for f in range(2):
        u_ref[f * span : f * span + cols, :] = jnp.zeros((cols, LANES), F32)
        u_ref[f * span + cols * (NU + 1) : (f + 1) * span, :] = jnp.zeros((3 * cols, LANES), F32)

    def group(g, carry):
        for f, src in enumerate((cond_ref, dense_ref)):
            parts = [src[p, pl.ds(g * 64 + r, 8, stride=8), :] for p in range(2) for r in range(8)]
            for uc, part in enumerate(scatter_groups(parts)):
                if uc < 10:
                    slot = (uc - 1) % 16
                    u_ref[pl.ds(f * span + (1 + 8 * g) * cols + slot, 8, stride=cols), :] = part
        return carry

    lax.fori_loop(0, 8, group, 0)

    def tile(a, carry):
        for f in range(2):
            out = (a * 2 + f) * FIELD_BLOCK
            at = f * span + 4 * a * cols
            for i in range(6):
                o_ref[pl.ds(out + 8 * i, 8), :] = u_ref[pl.ds(pl.multiple_of(at + i * cols, 8), 8), :]
            o_ref[pl.ds(out + 48, 8), :] = u_ref[pl.ds(at + 15, 8, stride=cols), :]
            o_ref[pl.ds(out + 56, 8), :] = u_ref[pl.ds(at + 8, 8, stride=cols), :]
        return carry

    lax.fori_loop(0, NS, tile, 0)


def pack_fields(conductivity, labels, sensors, weights):
    vmem = pl.BlockSpec(memory_space=VMEM)
    return pl.pallas_call(
        pack_fields_kernel,
        in_specs=[pl.BlockSpec(memory_space=pltpu.HBM)] * 4,
        out_specs=vmem,
        out_shape=jax.ShapeDtypeStruct((NS * 2 * FIELD_BLOCK, LANES), F32),
        scratch_shapes=[
            pltpu.SMEM((8,), F32),
            pltpu.VMEM((1, 2048), jnp.int32),
            pltpu.VMEM((1, 2048), F32),
            pltpu.VMEM((2, NY, 2 * LANES), jnp.int32),
            pltpu.VMEM((2, NY, LANES), F32),
            pltpu.VMEM((2, NY, LANES), F32),
            pltpu.VMEM((2 * 16 * (NU + 4), LANES), F32),
            pltpu.VMEM((NY, 2048), BF16),
            pltpu.VMEM((NY, 2048), BF16),
            pltpu.SemaphoreType.DMA((4,)),
        ],
        compiler_params=params(14),
        cost_estimate=pl.CostEstimate(flops=8_000_000, bytes_accessed=12_000_000, transcendentals=0),
        name="pack_fields",
    )(*in_hbm(conductivity, labels, sensors.reshape(1, -1), weights.reshape(1, -1)))


def harmonic(left, right):
    total = jnp.maximum(left + right, 1e-30)
    return (2.0 * TIME_STEP) * left * right / total


def fields_kernel(r_ref, fr_ref, fc_ref, fp_ref, d_ref, cond_ref):
    zero8 = jnp.zeros((8, LANES), F32)
    for p in range(2):

        def clear(i, carry, p=p):
            cond_ref[p, i, COLS : COLS + 8, :] = zero8
            fc_ref[p, i, 0:8, :] = zero8
            return carry

        lax.fori_loop(0, ROWS, clear, 0)

    def unpack(f, ref, row, ur, col):
        block = r_ref[pl.ds(f * FIELD_BLOCK + row, NS, stride=2 * FIELD_BLOCK), :]
        turned = jnp.concatenate([block] * NP, axis=0).T
        for g in range(16):
            m = (g - col // 8) % 16
            ref[m // 8, ur * 8 + m % 8, pl.ds(col, 8), :] = turned[8 * g : 8 * g + 8]

    for f, ref in ((0, cond_ref), (1, d_ref)):

        def rows(ur, carry, f=f, ref=ref):
            for uc in range(8):
                unpack(f, ref, ur * 8 + uc, ur, HALO + 8 * uc)
            unpack(f, ref, 48 + ur, ur, 0)
            unpack(f, ref, 56 + ur, ur, HALO + CORE_C)
            return carry

        lax.fori_loop(0, 6, rows, 0)

    last_slab = (lane_iota() & (NS - 1)) == NS - 1

    def faces(i, carry):
        nxt = jnp.minimum(i + 1, ROWS - 1)
        for cb in range(10):
            at = pl.ds(8 * cb, 8)
            c0, c1 = cond_ref[0, i, at, :], cond_ref[1, i, at, :]
            fr_ref[0, i, at, :] = harmonic(c0, cond_ref[0, nxt, at, :])
            fr_ref[1, i, at, :] = harmonic(c1, cond_ref[1, nxt, at, :])
            aside = pl.ds(8 * cb + 1, 8)
            fc_ref[0, i, pl.ds(8 + 8 * cb, 8), :] = harmonic(c0, cond_ref[0, i, aside, :])
            fc_ref[1, i, pl.ds(8 + 8 * cb, 8), :] = harmonic(c1, cond_ref[1, i, aside, :])
            fp_ref[0, i, at, :] = harmonic(c0, c1)
            beyond = pltpu.roll(c0, LANES - 1, 1)
            outer = jnp.where(last_slab, 0.0, harmonic(c1, beyond))
            fp_ref[1, i, at, :] = outer
            fp_ref[2, i, at, :] = pltpu.roll(outer, 1, 1)
        return carry

    lax.fori_loop(0, ROWS, faces, 0)


def make_fields(received):
    wide = jax.ShapeDtypeStruct((2, ROWS, COLS, LANES), F32)
    wider = jax.ShapeDtypeStruct((2, ROWS, COLS + 8, LANES), F32)
    return pl.pallas_call(
        fields_kernel,
        in_specs=[pl.BlockSpec(memory_space=VMEM)],
        out_specs=[pl.BlockSpec(memory_space=VMEM)] * 4,
        out_shape=[wide, wider, jax.ShapeDtypeStruct((3, ROWS, COLS, LANES), F32), wide],
        scratch_shapes=[pltpu.VMEM((2, ROWS, COLS + 8, LANES), F32)],
        compiler_params=params(10),
        cost_estimate=pl.CostEstimate(flops=40_000_000, bytes_accessed=30_000_000, transcendentals=0),
        name="make_fields",
    )(received)


def solve_kernel(
    r_hbm,
    fr_hbm,
    fc_hbm,
    fp_hbm,
    d_hbm,
    y_ref,
    gram_ref,
    r_ref,
    fr_ref,
    fc_ref,
    fp_ref,
    d_ref,
    ua_ref,
    ub_ref,
    prod_ref,
    side_ref,
    sems,
):
    copies = [
        pltpu.make_async_copy(src, dst, sems.at[i])
        for i, (src, dst) in enumerate(
            ((r_hbm, r_ref), (fr_hbm, fr_ref), (fc_hbm, fc_ref), (fp_hbm, fp_ref), (d_hbm, d_ref))
        )
    ]
    for copy in copies:
        copy.start()
    odd = lax.rem(lax.axis_index("sketch"), 2)
    zero8 = jnp.zeros((8, LANES), F32)
    for ref in (ua_ref, ub_ref):
        for p in range(2):

            def clear(i, carry, p=p, ref=ref):
                ref[p, i, 0:8, :] = zero8
                ref[p, i, 8 + COLS : 16 + COLS, :] = zero8
                return carry

            lax.fori_loop(0, ROWS, clear, 0)
    copies[0].wait()

    def unpack(row, ur, col):
        turned = r_ref[pl.ds(row, LANES, stride=BLOCK), :].T
        for g in range(16):
            m = (g - (col // 8 - 1)) % 16
            ua_ref[lax.rem(m // 8 + odd, 2), ur * 8 + m % 8, pl.ds(8 + col, 8), :] = turned[8 * g : 8 * g + 8]

    def rows(ur, carry):
        for uc in range(8):
            unpack(ur * 8 + uc, ur, HALO + 8 * uc)
        unpack(48 + ur, ur, 0)
        unpack(54 + ur, ur, HALO + CORE_C)
        return carry

    lax.fori_loop(0, 6, rows, 0)

    def keep(i, carry):
        for p in range(2):
            for cb in range(8):
                prod_ref[p, i, pl.ds(8 * cb, 8), :] = (
                    PRIOR_WEIGHT * ua_ref[p, i + HALO, pl.ds(8 + HALO + 8 * cb, 8), :]
                )
        return carry

    lax.fori_loop(0, CORE_R, keep, 0)
    for copy in copies[1:4]:
        copy.wait()

    def advance(src, dst, step, blocks):
        last = step == 2 * STEPS

        def flow(p, i, cb):
            at = pl.ds(8 + 8 * cb, 8)
            return fr_ref[p, i, pl.ds(8 * cb, 8), :] * (src[p, i + 1, at, :] - src[p, i, at, :])

        def some_rows(first, count, flows):
            mids = [pl.ds(8 + 8 * cb, 8) for cb in blocks]
            for slot in range(count):
                i = first + slot
                beyond = [
                    (pltpu.roll(src[0, i, mid, :], LANES - 1, 1), pltpu.roll(src[1, i, mid, :], 1, 1)) for mid in mids
                ]
                new_flows = []
                new = []
                for n, (cb, mid) in enumerate(zip(blocks, mids)):
                    at = pl.ds(8 * cb, 8)
                    right = pl.ds(9 + 8 * cb, 8)
                    left = pl.ds(7 + 8 * cb, 8)
                    for p in range(2):
                        u = src[p, i, mid, :]
                        row_flow = fr_ref[p, i, at, :] * (src[p, i + 1, mid, :] - u)
                        change = row_flow - flows[2 * n + p]
                        new_flows.append(row_flow)
                        to_right = fc_ref[p, i, mid, :] * (src[p, i, right, :] - u)
                        if VIA_SCRATCH:
                            side_ref[slot, p, mid, :] = to_right
                            if n == 0:
                                from_left = fc_ref[p, i, left, :] * (u - src[p, i, left, :])
                            else:
                                from_left = side_ref[slot, p, left, :]
                            change += to_right - from_left
                        else:
                            change += to_right
                            change += fc_ref[p, i, left, :] * (src[p, i, left, :] - u)
                        new.append(u + change)
                for n, (cb, mid) in enumerate(zip(blocks, mids)):
                    at = pl.ds(8 * cb, 8)
                    u = [src[p, i, mid, :] for p in range(2)]
                    inner = fp_ref[0, i, at, :] * (u[1] - u[0])
                    below = fp_ref[2, i, at, :] * (beyond[n][1] - u[0])
                    above = fp_ref[1, i, at, :] * (beyond[n][0] - u[1])
                    both = [new[2 * n] + (below + inner), new[2 * n + 1] + (above - inner)]
                    for p in range(2):
                        if step == STEPS:
                            both[p] = both[p] * d_ref[p, i, at, :]
                        if last:
                            core = pl.ds(8 * (cb - 1), 8)
                            prod_ref[p, i - HALO, core, :] += both[p]
                        else:
                            dst[p, i, mid, :] = both[p]
                flows = tuple(new_flows)
            return flows

        flows = tuple(flow(p, step - 1, cb) for cb in blocks for p in range(2))
        count = ROWS - 2 * step
        rest = count % UNROLL
        flows = lax.fori_loop(
            0, count // UNROLL, lambda t, flows: some_rows(step + t * UNROLL, UNROLL, flows), flows
        )
        if rest:
            some_rows(ROWS - step - rest, rest, flows)

    refs = (ua_ref, ub_ref)
    for step in range(1, 2 * STEPS + 1):
        if step == STEPS:
            copies[4].wait()
        first, end = (1, 9) if step == 2 * STEPS else (0, 10)
        for at in range(first, end, WIDTH):
            blocks = list(range(at, min(at + WIDTH, end)))
            advance(refs[(step - 1) % 2], refs[step % 2], step, blocks)

    def units(ur, carry):
        for uc in range(8):
            parts = []
            for g in range(16):
                m = (g - uc) % 16
                parts.append(prod_ref[lax.rem(m // 8 + odd, 2), ur * 8 + m % 8, pl.ds(8 * uc, 8), :])
            turned = jnp.concatenate(parts, axis=0).T
            high = turned.astype(BF16)
            at = pl.ds(pl.multiple_of((ur * 8 + uc) * LANES, LANES), LANES)
            y_ref[0:LANES, at] = high
            y_ref[LANES:, at] = (turned - high.astype(F32)).astype(BF16)
        return carry

    lax.fori_loop(0, 4, units, 0)
    both = lax.dot_general(y_ref[0:LANES, :], y_ref[...], (((1,), (1,)), ((), ())), preferred_element_type=F32)
    mixed = both[:, LANES:]
    gram = both[:, :LANES] + (mixed + mixed.T)
    slab_of_row = lax.broadcasted_iota(jnp.int32, (LANES, LANES), 0) & (NS - 1)
    slab_of_lane = lax.broadcasted_iota(jnp.int32, (LANES, LANES), 1) & (NS - 1)
    gram = jnp.where(slab_of_row == slab_of_lane, gram, 0.0)
    by_probe = jnp.sum(gram.reshape(NP, NS, LANES), axis=1)
    same = (
        lax.shift_right_logical(lax.broadcasted_iota(jnp.int32, (LANES, LANES), 0), 4)
        == lax.shift_right_logical(lax.broadcasted_iota(jnp.int32, (LANES, LANES), 1), 4)
    ).astype(F32)
    by_probe = jnp.dot(by_probe, same, precision=lax.Precision.HIGHEST, preferred_element_type=F32)
    own = (lane_iota() & (NS - 1)) == lax.broadcasted_iota(jnp.int32, (8, LANES), 0)
    row = jnp.sum(jnp.where(own, by_probe, 0.0), axis=0, keepdims=True)
    gram_ref[...] = jnp.broadcast_to(row, (LANES, LANES))


def solve(received, faces):
    vmem = pl.BlockSpec(memory_space=VMEM)
    return pl.pallas_call(
        solve_kernel,
        in_specs=[pl.BlockSpec(memory_space=pltpu.HBM)] * 5,
        out_specs=[vmem] * 2,
        out_shape=[
            jax.ShapeDtypeStruct((2 * LANES, 32 * LANES), BF16),
            jax.ShapeDtypeStruct((LANES, LANES), F32),
        ],
        scratch_shapes=[
            pltpu.VMEM((128 * BLOCK, LANES), F32),
            pltpu.VMEM((2, ROWS, COLS, LANES), F32),
            pltpu.VMEM((2, ROWS, COLS + 8, LANES), F32),
            pltpu.VMEM((3, ROWS, COLS, LANES), F32),
            pltpu.VMEM((2, ROWS, COLS, LANES), F32),
            pltpu.VMEM((2, ROWS, COLS + 16, LANES), F32),
            pltpu.VMEM((2, ROWS, COLS + 16, LANES), F32),
            pltpu.VMEM((2, CORE_R, CORE_C, LANES), F32),
            pltpu.VMEM((UNROLL, 2, COLS + 8, LANES), F32),
            pltpu.SemaphoreType.DMA((5,)),
        ],
        compiler_params=params(42),
        cost_estimate=pl.CostEstimate(flops=100_000_000, bytes_accessed=30_000_000, transcendentals=0),
        name="solve",
    )(*in_hbm(received, *faces))


def basis_kernel(gram_ref, y_ref, o_ref, factor_ref, *, cells):
    lanes = lane_iota()
    sublanes = lax.broadcasted_iota(jnp.int32, (8, LANES), 0)
    total = gram_ref[0:8, :]
    for i in range(1, LANES // 8):
        total = total + gram_ref[8 * i : 8 * i + 8, :]
    row = jnp.broadcast_to(jnp.sum(total, axis=0, keepdims=True), (8, LANES)) / cells

    def entry(i, j):
        at = j * NS + i
        return jnp.broadcast_to(row[:, at : at + 1], (8, LANES))

    lower = {}
    inv_diag = []
    for j in range(NP):
        pivot = entry(j, j)
        for m in range(j):
            pivot = pivot - lower[j, m] * lower[j, m]
        lower[j, j] = jnp.sqrt(pivot)
        inv_diag.append(1.0 / lower[j, j])
        for i in range(j + 1, NP):
            value = entry(i, j)
            for m in range(j):
                value = value - lower[i, m] * lower[j, m]
            lower[i, j] = value * inv_diag[j]
    inverse = {}
    for i in range(NP):
        inverse[i, i] = inv_diag[i]
        for j in range(i):
            carried = lower[i, j] * inverse[j, j]
            for m in range(j + 1, i):
                carried = carried + lower[i, m] * inverse[m, j]
            inverse[i, j] = -carried * inv_diag[i]

    factor = jnp.zeros((8, LANES), F32)
    for (i, j), value in lower.items():
        factor = jnp.where((sublanes == j) & (lanes == i), value, factor)
    factor_ref[...] = factor

    probe = lax.shift_right_logical(lanes, 4)
    mix = []
    for i in range(NP):
        coef = jnp.zeros((8, LANES), F32)
        for j in range(i + 1):
            coef = jnp.where(probe == j, inverse[i, j], coef)
        for half in range(2):
            mix.append(jnp.where((lanes & (NS - 1)) == sublanes + 8 * half, coef, 0.0))
    mix = jnp.concatenate(mix, axis=0)
    high = mix.astype(BF16)
    low = (mix - high.astype(F32)).astype(BF16)
    twice = jnp.concatenate([high, high], axis=1)

    def units(ur, carry):
        for uc in range(8):
            at = pl.ds(pl.multiple_of((ur * 8 + uc) * LANES, LANES), LANES)
            o_ref[pl.ds(ur * 8 + uc, LANES, stride=32), :] = jnp.dot(
                twice, y_ref[:, at], preferred_element_type=F32
            ) + jnp.dot(low, y_ref[0:LANES, at], preferred_element_type=F32)
        return carry

    lax.fori_loop(0, 4, units, 0)


def make_basis(grams, products):
    cells = float(2 * NS * NY * NZ)
    return pl.pallas_call(
        functools.partial(basis_kernel, cells=cells),
        in_specs=[pl.BlockSpec(memory_space=VMEM)] * 2,
        out_specs=[pl.BlockSpec(memory_space=VMEM)] * 2,
        out_shape=[
            jax.ShapeDtypeStruct((128 * 32, LANES), F32),
            jax.ShapeDtypeStruct((8, LANES), F32),
        ],
        compiler_params=params(10),
        cost_estimate=pl.CostEstimate(flops=10_000_000, bytes_accessed=4_000_000, transcendentals=0),
        name="make_basis",
    )(grams, products)


def unpack_kernel(r_ref, o_ref):
    def group(g, carry):
        parts = [
            r_ref[pl.ds(b * 512 + g * 64 + uc, 8, stride=8), :] for b in range(2) for uc in range(8)
        ]
        turned = gather_groups(parts)
        for p in range(2):
            for r in range(8):
                o_ref[0, p, pl.ds(g * 64 + r, 8, stride=8), :] = turned[p * 8 + r]
        return carry

    lax.fori_loop(0, 8, group, 0, unroll=2)


def unpack_basis(received):
    return pl.pallas_call(
        unpack_kernel,
        grid=(4,),
        in_specs=[pl.BlockSpec((1024, LANES), lambda j: (j, 0))],
        out_specs=pl.BlockSpec((1, 2, NY, LANES), lambda j: (0, 0, 0, j)),
        out_shape=jax.ShapeDtypeStruct((1, 2, NY, NZ), F32),
        compiler_params=params(10),
        cost_estimate=pl.CostEstimate(flops=8_000_000, bytes_accessed=4_000_000, transcendentals=0),
        name="unpack_basis",
    )(received)


def exchange(rows, axes):
    return lax.all_to_all(rows, axes, split_axis=0, concat_axis=0, tiled=True)


def on_device(probes, ply_labels, conductivity, sensors, sensor_weight):
    every = ("sketch", "pde")
    fields = exchange(pack_fields(conductivity, ply_labels, sensors, sensor_weight), "pde")
    tiles = exchange(pack_probes(probes).reshape(LANES, BLOCK // 4, 4, LANES), every).reshape(-1, LANES)
    products, gram = solve(tiles, make_fields(fields))
    grams = exchange(gram, every)
    columns, factor = make_basis(grams, products)
    basis = unpack_basis(exchange(columns, every))
    return (basis, factor[:, :NP])


def solution(mesh):
    placed = (P("sketch", "pde", None, None), P("pde", None, None), P(), P("pde"), P("pde"))
    return jax.shard_map(
        on_device,
        mesh=mesh,
        in_specs=placed,
        out_specs=(P("sketch", "pde", None, None), P()),
        check_vma=False,
    )
```

```python
import functools

import jax
import jax.numpy as jnp
from jax import lax
from jax.experimental import pallas as pl
from jax.experimental.pallas import tpu as pltpu
from jax.sharding import PartitionSpec as P

STEPS = 4
TIME_STEP = 0.15
PRIOR_WEIGHT = 0.1

F32 = jnp.float32
BF16 = jnp.bfloat16
LANES = 128
NP = 8
NS = 16
NY = 512
NZ = 512
NU = 64
HALO = 8
ROWS = 48
COLS = 80
CORE_R = 32
CORE_C = 64
BLOCK = 60
FIELD_BLOCK = 64
LIST_ROWS = 16
SLAB_BLOCK = FIELD_BLOCK + 2 * LIST_ROWS
VMEM = pltpu.MemorySpace.VMEM
UNROLL = 4
WIDTH = 10
VIA_SCRATCH = False


def params(mebibytes):
    return pltpu.CompilerParams(vmem_limit_bytes=mebibytes * 1024 * 1024)


def in_hbm(*arrays):
    return [pltpu.with_memory_space_constraint(array, pltpu.HBM) for array in arrays]


def lane_iota(shape=(8, LANES)):
    return lax.broadcasted_iota(jnp.int32, shape, len(shape) - 1)


def scatter_groups(parts):
    group = lax.shift_right_logical(lane_iota(), 3)
    parts = [pltpu.roll(part, 8 * m, 1) if m else part for m, part in enumerate(parts)]
    for bit in range(4):
        ahead = (group & (1 << bit)) != 0
        parts = [jnp.where(ahead, parts[(i + (1 << bit)) % 16], parts[i]) for i in range(16)]
    return [parts[(-u) % 16] for u in range(16)]


def gather_groups(parts):
    group = lax.shift_right_logical(lane_iota(), 3)
    parts = [parts[(-i) % 16] for i in range(16)]
    for bit in range(4):
        behind = (group & (1 << bit)) != 0
        parts = [jnp.where(behind, parts[(i - (1 << bit)) % 16], parts[i]) for i in range(16)]
    return [pltpu.roll(part, LANES - 8 * m, 1) if m else part for m, part in enumerate(parts)]


def pack_probes_kernel(x_ref, o_hbm, o_ref, u_ref, sems):
    step = pl.program_id(0)
    cols = NU

    @pl.when(step == 0)
    def _():
        u_ref[0:cols, :] = jnp.zeros((cols, LANES), F32)
        u_ref[cols * (NU + 1) : cols * (NU + 4), :] = jnp.zeros((3 * cols, LANES), F32)

    def part(b):
        at = pl.ds(b * NS * BLOCK, NS * BLOCK)
        return pltpu.make_async_copy(o_ref.at[at, :], o_hbm.at[at, :], sems.at[b])

    def group(g, carry):
        parts = [
            x_ref[0, p, pl.ds(g * 64 + r, 8, stride=8), :] for p in range(2) for r in range(8)
        ]
        for uc, part in enumerate(scatter_groups(parts)):
            u_ref[pl.ds((1 + 8 * g) * cols + 16 * step + uc, 8, stride=cols), :] = part
        return carry

    lax.fori_loop(0, 8, group, 0)

    @pl.when(step == 3)
    def _():
        for b in range(8):

            def tile(a, carry, b=b):
                out = (b * NS + a) * BLOCK
                for i in range(6):
                    o_ref[pl.ds(out + 8 * i, 8), :] = u_ref[
                        pl.ds(pl.multiple_of((4 * a + i) * cols + 8 * b, 8), 8), :
                    ]
                if b > 0:
                    left = u_ref[pl.ds(4 * a * cols + 8 * b - 1, 6, stride=cols), :]
                else:
                    left = jnp.zeros((6, LANES), F32)
                o_ref[pl.ds(out + 48, 6), :] = left
                if b < 7:
                    right = u_ref[pl.ds(4 * a * cols + 8 * b + 8, 6, stride=cols), :]
                else:
                    right = jnp.zeros((6, LANES), F32)
                o_ref[pl.ds(out + 54, 6), :] = right
                return carry

            lax.fori_loop(0, NS, tile, 0)
            part(b).start()
        for b in range(8):
            part(b).wait()


def pack_probes(probes):
    return pl.pallas_call(
        pack_probes_kernel,
        grid=(4,),
        in_specs=[pl.BlockSpec((1, 2, NY, LANES), lambda j: (0, 0, 0, j))],
        out_specs=pl.BlockSpec(memory_space=pltpu.HBM),
        out_shape=pltpu.HBM((128 * BLOCK, LANES), F32),
        scratch_shapes=[
            pltpu.VMEM((128 * BLOCK, LANES), F32),
            pltpu.VMEM((NU * (NU + 4), LANES), F32),
            pltpu.SemaphoreType.DMA((8,)),
        ],
        compiler_params=params(14),
        cost_estimate=pl.CostEstimate(flops=8_000_000, bytes_accessed=12_000_000, transcendentals=0),
        name="pack_probes",
    )(probes)


def pack_fields_kernel(
    kinds_hbm, label_hbm, sensor_hbm, weight_hbm, o_ref, kinds_ref, sensor_ref, weight_ref, label_ref, cond_ref, u_ref, sems
):
    k = lax.axis_index("sketch")
    lanes = lane_iota()
    shift = 8 + 64 * lax.rem(k, 2)
    first = lax.div(k + 1, 2) - 1
    start = jnp.clip(first, 0, 2)
    window_hbm = label_hbm.at[:, :, pl.ds(pl.multiple_of(start * LANES, LANES), 2 * LANES)]
    copies = [
        pltpu.make_async_copy(src, dst, sems.at[i])
        for i, (src, dst) in enumerate(
            (
                (window_hbm, label_ref),
                (kinds_hbm, kinds_ref),
                (sensor_hbm, sensor_ref),
                (weight_hbm, weight_ref),
            )
        )
    ]
    for copy in copies:
        copy.start()
    cols = 16
    u_ref[0:cols, :] = jnp.zeros((cols, LANES), F32)
    u_ref[cols * (NU + 1) :, :] = jnp.zeros((3 * cols, LANES), F32)
    for copy in copies:
        copy.wait()
    place = first - start
    first_at = pl.multiple_of(jnp.maximum(place, 0) * LANES, LANES)
    second_at = pl.multiple_of(jnp.minimum(place + 1, 1) * LANES, LANES)
    from_first = lanes < shift
    outside = (from_first & (first < 0)) | ((lanes >= shift) & (first + 1 > 3))

    def window(i, carry):
        for q in range(4):
            rows = pl.ds(pl.multiple_of(i * 32 + q * 8, 8), 8)
            for p in range(2):
                a = label_ref[p, rows, pl.ds(first_at, LANES)]
                b = label_ref[p, rows, pl.ds(second_at, LANES)]
                label = jnp.where(from_first, pltpu.roll(a, shift, 1), pltpu.roll(b, shift, 1))
                cond = jnp.zeros((8, LANES), F32)
                for kind in range(8):
                    cond = jnp.where(label == kind, kinds_ref[kind], cond)
                cond_ref[p, rows, :] = jnp.where(outside, 0.0, cond)
        return carry

    lax.fori_loop(0, NU // 4, window, 0)

    def group(g, carry):
        parts = [cond_ref[p, pl.ds(g * 64 + r, 8, stride=8), :] for p in range(2) for r in range(8)]
        for uc, part in enumerate(scatter_groups(parts)):
            if uc < 10:
                slot = (uc - 1) % 16
                u_ref[pl.ds((1 + 8 * g) * cols + slot, 8, stride=cols), :] = part
        return carry

    lax.fori_loop(0, 8, group, 0, unroll=2)

    cells = sensor_ref[...].astype(F32)
    weights = weight_ref[...]

    def tile(a, carry):
        out = a * SLAB_BLOCK
        at = 4 * a * cols
        for i in range(6):
            o_ref[pl.ds(out + 8 * i, 8), :] = u_ref[pl.ds(pl.multiple_of(at + i * cols, 8), 8), :]
        o_ref[pl.ds(out + 48, 8), :] = u_ref[pl.ds(at + 15, 8, stride=cols), :]
        o_ref[pl.ds(out + 56, 8), :] = u_ref[pl.ds(at + 8, 8, stride=cols), :]
        o_ref[pl.ds(out + FIELD_BLOCK, LIST_ROWS), :] = cells
        o_ref[pl.ds(out + FIELD_BLOCK + LIST_ROWS, LIST_ROWS), :] = weights
        return carry

    lax.fori_loop(0, NS, tile, 0)


def pack_fields(conductivity, labels, sensors, weights):
    return pl.pallas_call(
        pack_fields_kernel,
        in_specs=[pl.BlockSpec(memory_space=pltpu.HBM)] * 4,
        out_specs=pl.BlockSpec(memory_space=VMEM),
        out_shape=jax.ShapeDtypeStruct((NS * SLAB_BLOCK, LANES), F32),
        scratch_shapes=[
            pltpu.SMEM((8,), F32),
            pltpu.VMEM((LIST_ROWS, LANES), jnp.int32),
            pltpu.VMEM((LIST_ROWS, LANES), F32),
            pltpu.VMEM((2, NY, 2 * LANES), jnp.int32),
            pltpu.VMEM((2, NY, LANES), F32),
            pltpu.VMEM((16 * (NU + 4), LANES), F32),
            pltpu.SemaphoreType.DMA((4,)),
        ],
        compiler_params=params(10),
        cost_estimate=pl.CostEstimate(flops=8_000_000, bytes_accessed=12_000_000, transcendentals=0),
        name="pack_fields",
    )(*in_hbm(conductivity, labels, sensors.reshape(LIST_ROWS, LANES), weights.reshape(LIST_ROWS, LANES)))


def harmonic(left, right):
    total = jnp.maximum(left + right, 1e-30)
    return (2.0 * TIME_STEP) * left * right / total


FACE_ROWS = 12


def fields_kernel(r_ref, *refs):
    outs, refs = refs[:4], refs[4:]
    fr_ref, fc_ref, fp_ref, d_ref, cond_ref, unit_ref, place_ref, dense_ref, out_sems = refs
    row_0 = 32 * lax.axis_index("pde") - HALO
    col_0 = 64 * lax.axis_index("sketch") - HALO

    def slab(n, carry):
        at = pl.multiple_of(n * SLAB_BLOCK + FIELD_BLOCK, 8)
        cell = r_ref[pl.ds(at, LIST_ROWS), :].astype(jnp.int32)
        weight = r_ref[pl.ds(at + LIST_ROWS, LIST_ROWS), :]
        high = weight.astype(BF16).astype(F32)
        rest = weight - high
        row = (lax.shift_right_logical(cell, 9) & (NY - 1)) - row_0
        col = (cell & (NZ - 1)) - col_0
        inside = (row >= 0) & (row < ROWS) & (col >= 0) & (col < COLS)
        ur = lax.shift_right_arithmetic(row, 3)
        uc = lax.shift_right_arithmetic(col, 3)
        unit = jnp.where(uc == 0, 48 + ur, jnp.where(uc == 9, 56 + ur, 8 * ur + uc - 1))
        unit = jnp.where(inside, unit, -1)
        place = 64 * lax.shift_right_logical(cell, 18) + 8 * (row & 7) + (col & 7)
        unit_index = lax.broadcasted_iota(jnp.int32, (FIELD_BLOCK, LANES), 0)
        place_index = lax.broadcasted_iota(jnp.int32, (LANES, LANES), 0)
        for j in range(LIST_ROWS):
            span = pl.ds(j * LANES, LANES)
            unit_ref[:, span] = jnp.where(unit_index == unit[j : j + 1], 1.0, 0.0).astype(BF16)
            hit = place_index == place[j : j + 1]
            place_ref[0:LANES, span] = jnp.where(hit, high[j : j + 1], 0.0).astype(BF16)
            place_ref[LANES:, span] = jnp.where(hit, rest[j : j + 1], 0.0).astype(BF16)
        got = lax.dot_general(
            unit_ref[...], place_ref[...], (((1,), (1,)), ((), ())), preferred_element_type=F32
        )
        dense_ref[pl.ds(pl.multiple_of(n * FIELD_BLOCK, 8), FIELD_BLOCK), :] = got[:, :LANES] + got[:, LANES:]
        return carry

    lax.fori_loop(0, NS, slab, 0)
    zero8 = jnp.zeros((8, LANES), F32)
    for p in range(2):

        def clear(i, carry, p=p):
            cond_ref[p, i, COLS : COLS + 8, :] = zero8
            fc_ref[p, i, 0:8, :] = zero8
            return carry

        lax.fori_loop(0, ROWS, clear, 0)

    def unpack(src, stride, turn, ref, row, ur, col):
        block = src[pl.ds(row, NS, stride=stride), :]
        turned = jnp.concatenate([block] * NP, axis=0).T
        for g in range(16):
            m = (g - turn * (col // 8)) % 16
            ref[m // 8, ur * 8 + m % 8, pl.ds(col, 8), :] = turned[8 * g : 8 * g + 8]

    for what in ((dense_ref, FIELD_BLOCK, 0, d_ref), (r_ref, SLAB_BLOCK, 1, cond_ref)):

        def rows(ur, carry, what=what):
            for uc in range(8):
                unpack(*what, ur * 8 + uc, ur, HALO + 8 * uc)
            unpack(*what, 48 + ur, ur, 0)
            unpack(*what, 56 + ur, ur, HALO + CORE_C)
            return carry

        lax.fori_loop(0, 6, rows, 0)

    last_slab = (lane_iota() & (NS - 1)) == NS - 1

    def faces(i, carry):
        nxt = jnp.minimum(i + 1, ROWS - 1)
        for cb in range(10):
            at = pl.ds(8 * cb, 8)
            c0, c1 = cond_ref[0, i, at, :], cond_ref[1, i, at, :]
            fr_ref[0, i, at, :] = harmonic(c0, cond_ref[0, nxt, at, :])
            fr_ref[1, i, at, :] = harmonic(c1, cond_ref[1, nxt, at, :])
            aside = pl.ds(8 * cb + 1, 8)
            fc_ref[0, i, pl.ds(8 + 8 * cb, 8), :] = harmonic(c0, cond_ref[0, i, aside, :])
            fc_ref[1, i, pl.ds(8 + 8 * cb, 8), :] = harmonic(c1, cond_ref[1, i, aside, :])
            fp_ref[0, i, at, :] = harmonic(c0, c1)
            beyond = pltpu.roll(c0, LANES - 1, 1)
            outer = jnp.where(last_slab, 0.0, harmonic(c1, beyond))
            fp_ref[1, i, at, :] = outer
            fp_ref[2, i, at, :] = pltpu.roll(outer, 1, 1)
        return carry

    copies = [pltpu.make_async_copy(d_ref, outs[3], out_sems.at[0])]
    copies[0].start()
    for first in range(0, ROWS, FACE_ROWS):
        lax.fori_loop(first, first + FACE_ROWS, faces, 0)
        for ref, out in zip((fr_ref, fc_ref, fp_ref), outs):
            at = pl.ds(first, FACE_ROWS)
            copy = pltpu.make_async_copy(ref.at[:, at], out.at[:, at], out_sems.at[len(copies)])
            copy.start()
            copies.append(copy)
    for copy in copies:
        copy.wait()


def make_fields(received):
    shapes = [(2, ROWS, COLS, LANES), (2, ROWS, COLS + 8, LANES), (3, ROWS, COLS, LANES), (2, ROWS, COLS, LANES)]
    return pl.pallas_call(
        fields_kernel,
        in_specs=[pl.BlockSpec(memory_space=VMEM)],
        out_specs=[pl.BlockSpec(memory_space=pltpu.HBM)] * 4,
        out_shape=[pltpu.HBM(shape, F32) for shape in shapes],
        scratch_shapes=[
            *[pltpu.VMEM(shape, F32) for shape in shapes],
            pltpu.VMEM((2, ROWS, COLS + 8, LANES), F32),
            pltpu.VMEM((FIELD_BLOCK, 2048), BF16),
            pltpu.VMEM((2 * LANES, 2048), BF16),
            pltpu.VMEM((NS * FIELD_BLOCK, LANES), F32),
            pltpu.SemaphoreType.DMA((1 + 3 * ROWS // FACE_ROWS,)),
        ],
        compiler_params=params(32),
        cost_estimate=pl.CostEstimate(flops=40_000_000, bytes_accessed=30_000_000, transcendentals=0),
        name="make_fields",
    )(received)


def solve_kernel(
    r_hbm,
    fr_hbm,
    fc_hbm,
    fp_hbm,
    d_hbm,
    y_ref,
    gram_ref,
    r_ref,
    fr_ref,
    fc_ref,
    fp_ref,
    d_ref,
    ua_ref,
    ub_ref,
    prod_ref,
    side_ref,
    sems,
):
    copies = [
        pltpu.make_async_copy(src, dst, sems.at[i])
        for i, (src, dst) in enumerate(
            ((r_hbm, r_ref), (fr_hbm, fr_ref), (fc_hbm, fc_ref), (fp_hbm, fp_ref), (d_hbm, d_ref))
        )
    ]
    for copy in copies:
        copy.start()
    odd = lax.rem(lax.axis_index("sketch"), 2)
    zero8 = jnp.zeros((8, LANES), F32)
    for ref in (ua_ref, ub_ref):
        for p in range(2):

            def clear(i, carry, p=p, ref=ref):
                ref[p, i, 0:8, :] = zero8
                ref[p, i, 8 + COLS : 16 + COLS, :] = zero8
                return carry

            lax.fori_loop(0, ROWS, clear, 0)
    copies[0].wait()

    def unpack(row, ur, col):
        turned = r_ref[pl.ds(row, LANES, stride=BLOCK), :].T
        for g in range(16):
            m = (g - (col // 8 - 1)) % 16
            ua_ref[lax.rem(m // 8 + odd, 2), ur * 8 + m % 8, pl.ds(8 + col, 8), :] = turned[8 * g : 8 * g + 8]

    def rows(ur, carry):
        for uc in range(8):
            unpack(ur * 8 + uc, ur, HALO + 8 * uc)
        unpack(48 + ur, ur, 0)
        unpack(54 + ur, ur, HALO + CORE_C)
        return carry

    lax.fori_loop(0, 6, rows, 0)

    def keep(i, carry):
        for p in range(2):
            for cb in range(8):
                prod_ref[p, i, pl.ds(8 * cb, 8), :] = (
                    PRIOR_WEIGHT * ua_ref[p, i + HALO, pl.ds(8 + HALO + 8 * cb, 8), :]
                )
        return carry

    lax.fori_loop(0, CORE_R, keep, 0)
    for copy in copies[1:4]:
        copy.wait()

    def advance(src, dst, step, blocks):
        last = step == 2 * STEPS

        def flow(p, i, cb):
            at = pl.ds(8 + 8 * cb, 8)
            return fr_ref[p, i, pl.ds(8 * cb, 8), :] * (src[p, i + 1, at, :] - src[p, i, at, :])

        mids = [pl.ds(8 + 8 * cb, 8) for cb in blocks]

        def beside(n, i):
            return (
                pltpu.roll(src[0, i, mids[n], :], LANES - 1, 1),
                pltpu.roll(src[1, i, mids[n], :], 1, 1),
            )

        def some_rows(first, count, carry):
            flows, beyond = carry
            for slot in range(count):
                i = first + slot
                new_flows = []
                new_beyond = []
                for n, (cb, mid) in enumerate(zip(blocks, mids)):
                    at = pl.ds(8 * cb, 8)
                    right = pl.ds(9 + 8 * cb, 8)
                    left = pl.ds(7 + 8 * cb, 8)
                    u = [src[p, i, mid, :] for p in range(2)]
                    new = []
                    for p in range(2):
                        row_flow = fr_ref[p, i, at, :] * (src[p, i + 1, mid, :] - u[p])
                        change = row_flow - flows[2 * n + p]
                        new_flows.append(row_flow)
                        to_right = fc_ref[p, i, mid, :] * (src[p, i, right, :] - u[p])
                        if VIA_SCRATCH:
                            side_ref[slot, p, mid, :] = to_right
                            if n == 0:
                                from_left = fc_ref[p, i, left, :] * (u[p] - src[p, i, left, :])
                            else:
                                from_left = side_ref[slot, p, left, :]
                            change += to_right - from_left
                        else:
                            change += to_right
                            change += fc_ref[p, i, left, :] * (src[p, i, left, :] - u[p])
                        new.append(u[p] + change)
                    new_beyond.append(beside(n, i + 1))
                    inner = fp_ref[0, i, at, :] * (u[1] - u[0])
                    below = fp_ref[2, i, at, :] * (beyond[n][1] - u[0])
                    above = fp_ref[1, i, at, :] * (beyond[n][0] - u[1])
                    both = [new[0] + (below + inner), new[1] + (above - inner)]
                    for p in range(2):
                        if step == STEPS:
                            both[p] = both[p] * d_ref[p, i, at, :]
                        if last:
                            core = pl.ds(8 * (cb - 1), 8)
                            prod_ref[p, i - HALO, core, :] += both[p]
                        else:
                            dst[p, i, mid, :] = both[p]
                flows, beyond = tuple(new_flows), tuple(new_beyond)
            return flows, beyond

        flows = tuple(flow(p, step - 1, cb) for cb in blocks for p in range(2))
        carry = (flows, tuple(beside(n, step) for n in range(len(blocks))))
        count = ROWS - 2 * step
        rest = count % UNROLL
        carry = lax.fori_loop(
            0, count // UNROLL, lambda t, carry: some_rows(step + t * UNROLL, UNROLL, carry), carry
        )
        if rest:
            some_rows(ROWS - step - rest, rest, carry)

    refs = (ua_ref, ub_ref)
    for step in range(1, 2 * STEPS + 1):
        if step == STEPS:
            copies[4].wait()
        first, end = (1, 9) if step == 2 * STEPS else (0, 10)
        for at in range(first, end, WIDTH):
            blocks = list(range(at, min(at + WIDTH, end)))
            advance(refs[(step - 1) % 2], refs[step % 2], step, blocks)

    def units(ur, carry):
        for uc in range(8):
            parts = []
            for g in range(16):
                m = (g - uc) % 16
                parts.append(prod_ref[lax.rem(m // 8 + odd, 2), ur * 8 + m % 8, pl.ds(8 * uc, 8), :])
            turned = jnp.concatenate(parts, axis=0).T
            high = turned.astype(BF16)
            at = pl.ds(pl.multiple_of((ur * 8 + uc) * LANES, LANES), LANES)
            y_ref[0:LANES, at] = high
            y_ref[LANES:, at] = (turned - high.astype(F32)).astype(BF16)
        return carry

    lax.fori_loop(0, 4, units, 0)
    both = lax.dot_general(y_ref[0:LANES, :], y_ref[...], (((1,), (1,)), ((), ())), preferred_element_type=F32)
    mixed = both[:, LANES:]
    gram = both[:, :LANES] + (mixed + mixed.T)
    slab_of_row = lax.broadcasted_iota(jnp.int32, (LANES, LANES), 0) & (NS - 1)
    slab_of_lane = lax.broadcasted_iota(jnp.int32, (LANES, LANES), 1) & (NS - 1)
    gram = jnp.where(slab_of_row == slab_of_lane, gram, 0.0)
    by_probe = jnp.sum(gram.reshape(NP, NS, LANES), axis=1)
    same = (
        lax.shift_right_logical(lax.broadcasted_iota(jnp.int32, (LANES, LANES), 0), 4)
        == lax.shift_right_logical(lax.broadcasted_iota(jnp.int32, (LANES, LANES), 1), 4)
    ).astype(F32)
    by_probe = jnp.dot(by_probe, same, precision=lax.Precision.HIGHEST, preferred_element_type=F32)
    own = (lane_iota() & (NS - 1)) == lax.broadcasted_iota(jnp.int32, (8, LANES), 0)
    row = jnp.sum(jnp.where(own, by_probe, 0.0), axis=0, keepdims=True)
    gram_ref[...] = jnp.broadcast_to(row, (LANES, LANES))


def solve(received, faces):
    vmem = pl.BlockSpec(memory_space=VMEM)
    return pl.pallas_call(
        solve_kernel,
        in_specs=[pl.BlockSpec(memory_space=pltpu.HBM)] * 5,
        out_specs=[vmem] * 2,
        out_shape=[
            jax.ShapeDtypeStruct((2 * LANES, 32 * LANES), BF16),
            jax.ShapeDtypeStruct((LANES, LANES), F32),
        ],
        scratch_shapes=[
            pltpu.VMEM((128 * BLOCK, LANES), F32),
            pltpu.VMEM((2, ROWS, COLS, LANES), F32),
            pltpu.VMEM((2, ROWS, COLS + 8, LANES), F32),
            pltpu.VMEM((3, ROWS, COLS, LANES), F32),
            pltpu.VMEM((2, ROWS, COLS, LANES), F32),
            pltpu.VMEM((2, ROWS, COLS + 16, LANES), F32),
            pltpu.VMEM((2, ROWS, COLS + 16, LANES), F32),
            pltpu.VMEM((2, CORE_R, CORE_C, LANES), F32),
            pltpu.VMEM((UNROLL, 2, COLS + 8, LANES), F32),
            pltpu.SemaphoreType.DMA((5,)),
        ],
        compiler_params=params(42),
        cost_estimate=pl.CostEstimate(flops=100_000_000, bytes_accessed=30_000_000, transcendentals=0),
        name="solve",
    )(*in_hbm(received, *faces))


def basis_kernel(gram_ref, y_ref, o_ref, factor_ref, *, cells):
    lanes = lane_iota()
    sublanes = lax.broadcasted_iota(jnp.int32, (8, LANES), 0)
    total = gram_ref[0:8, :]
    for i in range(1, LANES // 8):
        total = total + gram_ref[8 * i : 8 * i + 8, :]
    row = jnp.broadcast_to(jnp.sum(total, axis=0, keepdims=True), (8, LANES)) / cells

    def entry(i, j):
        at = j * NS + i
        return jnp.broadcast_to(row[:, at : at + 1], (8, LANES))

    lower = {}
    inv_diag = []
    for j in range(NP):
        pivot = entry(j, j)
        for m in range(j):
            pivot = pivot - lower[j, m] * lower[j, m]
        lower[j, j] = jnp.sqrt(pivot)
        inv_diag.append(1.0 / lower[j, j])
        for i in range(j + 1, NP):
            value = entry(i, j)
            for m in range(j):
                value = value - lower[i, m] * lower[j, m]
            lower[i, j] = value * inv_diag[j]
    inverse = {}
    for i in range(NP):
        inverse[i, i] = inv_diag[i]
        for j in range(i):
            carried = lower[i, j] * inverse[j, j]
            for m in range(j + 1, i):
                carried = carried + lower[i, m] * inverse[m, j]
            inverse[i, j] = -carried * inv_diag[i]

    factor = jnp.zeros((8, LANES), F32)
    for (i, j), value in lower.items():
        factor = jnp.where((sublanes == j) & (lanes == i), value, factor)
    factor_ref[...] = factor

    probe = lax.shift_right_logical(lanes, 4)
    mix = []
    for i in range(NP):
        coef = jnp.zeros((8, LANES), F32)
        for j in range(i + 1):
            coef = jnp.where(probe == j, inverse[i, j], coef)
        for half in range(2):
            mix.append(jnp.where((lanes & (NS - 1)) == sublanes + 8 * half, coef, 0.0))
    mix = jnp.concatenate(mix, axis=0)
    high = mix.astype(BF16)
    low = (mix - high.astype(F32)).astype(BF16)
    twice = jnp.concatenate([high, high], axis=1)

    def units(ur, carry):
        for uc in range(8):
            at = pl.ds(pl.multiple_of((ur * 8 + uc) * LANES, LANES), LANES)
            o_ref[pl.ds(ur * 8 + uc, LANES, stride=32), :] = jnp.dot(
                twice, y_ref[:, at], preferred_element_type=F32
            ) + jnp.dot(low, y_ref[0:LANES, at], preferred_element_type=F32)
        return carry

    lax.fori_loop(0, 4, units, 0)


def make_basis(grams, products):
    cells = float(2 * NS * NY * NZ)
    return pl.pallas_call(
        functools.partial(basis_kernel, cells=cells),
        in_specs=[pl.BlockSpec(memory_space=VMEM)] * 2,
        out_specs=[pl.BlockSpec(memory_space=VMEM)] * 2,
        out_shape=[
            jax.ShapeDtypeStruct((128 * 32, LANES), F32),
            jax.ShapeDtypeStruct((8, LANES), F32),
        ],
        compiler_params=params(10),
        cost_estimate=pl.CostEstimate(flops=10_000_000, bytes_accessed=4_000_000, transcendentals=0),
        name="make_basis",
    )(grams, products)


def unpack_kernel(r_ref, o_ref):
    def group(g, carry):
        parts = [
            r_ref[pl.ds(b * 512 + g * 64 + uc, 8, stride=8), :] for b in range(2) for uc in range(8)
        ]
        turned = gather_groups(parts)
        for p in range(2):
            for r in range(8):
                o_ref[0, p, pl.ds(g * 64 + r, 8, stride=8), :] = turned[p * 8 + r]
        return carry

    lax.fori_loop(0, 8, group, 0, unroll=2)


def unpack_basis(received):
    return pl.pallas_call(
        unpack_kernel,
        grid=(4,),
        in_specs=[pl.BlockSpec((1024, LANES), lambda j: (j, 0))],
        out_specs=pl.BlockSpec((1, 2, NY, LANES), lambda j: (0, 0, 0, j)),
        out_shape=jax.ShapeDtypeStruct((1, 2, NY, NZ), F32),
        compiler_params=params(10),
        cost_estimate=pl.CostEstimate(flops=8_000_000, bytes_accessed=4_000_000, transcendentals=0),
        name="unpack_basis",
    )(received)


def exchange(rows, axes):
    return lax.all_to_all(rows, axes, split_axis=0, concat_axis=0, tiled=True)


def on_device(probes, ply_labels, conductivity, sensors, sensor_weight):
    every = ("sketch", "pde")
    fields = exchange(pack_fields(conductivity, ply_labels, sensors, sensor_weight), "pde")
    tiles = exchange(pack_probes(probes).reshape(LANES, BLOCK // 4, 4, LANES), every).reshape(-1, LANES)
    products, gram = solve(tiles, make_fields(fields))
    grams = exchange(gram, every)
    columns, factor = make_basis(grams, products)
    basis = unpack_basis(exchange(columns, every))
    return (basis, factor[:, :NP])


def solution(mesh):
    placed = (P("sketch", "pde", None, None), P("pde", None, None), P(), P("pde"), P("pde"))
    return jax.shard_map(
        on_device,
        mesh=mesh,
        in_specs=placed,
        out_specs=(P("sketch", "pde", None, None), P()),
        check_vma=False,
    )
```

```python
import functools

import jax
import jax.numpy as jnp
from jax import lax
from jax.experimental import pallas as pl
from jax.experimental.pallas import tpu as pltpu
from jax.sharding import PartitionSpec as P

STEPS = 4
TIME_STEP = 0.15
PRIOR_WEIGHT = 0.1

F32 = jnp.float32
BF16 = jnp.bfloat16
LANES = 128
NP = 8
NS = 16
NY = 512
NZ = 512
NU = 64
HALO = 8
ROWS = 48
COLS = 80
CORE_R = 32
CORE_C = 64
BLOCK = 50
EDGE = 10
FIELD_BLOCK = 64
LIST_ROWS = 16
SLAB_BLOCK = FIELD_BLOCK + 2 * LIST_ROWS
VMEM = pltpu.MemorySpace.VMEM
UNROLL = 4
WIDTH = 10
VIA_SCRATCH = False


def params(mebibytes):
    return pltpu.CompilerParams(vmem_limit_bytes=mebibytes * 1024 * 1024)


def in_hbm(*arrays):
    return [pltpu.with_memory_space_constraint(array, pltpu.HBM) for array in arrays]


def lane_iota(shape=(8, LANES)):
    return lax.broadcasted_iota(jnp.int32, shape, len(shape) - 1)


def scatter_groups(parts):
    group = lax.shift_right_logical(lane_iota(), 3)
    parts = [pltpu.roll(part, 8 * m, 1) if m else part for m, part in enumerate(parts)]
    for bit in range(4):
        ahead = (group & (1 << bit)) != 0
        parts = [jnp.where(ahead, parts[(i + (1 << bit)) % 16], parts[i]) for i in range(16)]
    return [parts[(-u) % 16] for u in range(16)]


def gather_groups(parts):
    group = lax.shift_right_logical(lane_iota(), 3)
    parts = [parts[(-i) % 16] for i in range(16)]
    for bit in range(4):
        behind = (group & (1 << bit)) != 0
        parts = [jnp.where(behind, parts[(i - (1 << bit)) % 16], parts[i]) for i in range(16)]
    return [pltpu.roll(part, LANES - 8 * m, 1) if m else part for m, part in enumerate(parts)]


def pack_probes_kernel(x_ref, o_hbm, o_ref, u_ref, sems):
    step = pl.program_id(0)
    cols = NU

    @pl.when(step == 0)
    def _():
        u_ref[0:cols, :] = jnp.zeros((cols, LANES), F32)
        u_ref[cols * (NU + 1) : cols * (NU + 4), :] = jnp.zeros((3 * cols, LANES), F32)

    def part(b):
        at = pl.ds(b * NS * BLOCK, NS * BLOCK)
        return pltpu.make_async_copy(o_ref.at[at, :], o_hbm.at[at, :], sems.at[b])

    def group(g, carry):
        parts = [
            x_ref[0, p, pl.ds(g * 64 + r, 8, stride=8), :] for p in range(2) for r in range(8)
        ]
        for uc, part in enumerate(scatter_groups(parts)):
            u_ref[pl.ds((1 + 8 * g) * cols + 16 * step + uc, 8, stride=cols), :] = part
        return carry

    lax.fori_loop(0, 8, group, 0)

    @pl.when(step == 3)
    def _():
        for b in range(8):

            def tile(a, carry, b=b):
                out = (b * NS + a) * BLOCK
                core = lax.rem(a, 2)
                edge = (4 * a + 4 - 3 * core) * cols + 8 * b
                inner = (4 * a + 2 * core) * cols + 8 * b
                o_ref[pl.ds(out, 8), :] = u_ref[pl.ds(pl.multiple_of(edge, 8), 8), :]
                for q in range(4):
                    o_ref[pl.ds(out + EDGE + 8 * q, 8), :] = u_ref[
                        pl.ds(pl.multiple_of(inner + q * cols, 8), 8), :
                    ]
                for side, offset in enumerate((-1, 8)):
                    if 0 <= 8 * b + offset < cols:
                        one = u_ref[pl.ds(edge + offset, 1), :]
                        four = u_ref[pl.ds(inner + offset, 4, stride=cols), :]
                    else:
                        one = jnp.zeros((1, LANES), F32)
                        four = jnp.zeros((4, LANES), F32)
                    o_ref[pl.ds(out + 8 + side, 1), :] = one
                    o_ref[pl.ds(out + EDGE + 32 + 4 * side, 4), :] = four
                return carry

            lax.fori_loop(0, NS, tile, 0)
            part(b).start()
        for b in range(8):
            part(b).wait()


def pack_probes(probes):
    return pl.pallas_call(
        pack_probes_kernel,
        grid=(4,),
        in_specs=[pl.BlockSpec((1, 2, NY, LANES), lambda j: (0, 0, 0, j))],
        out_specs=pl.BlockSpec(memory_space=pltpu.HBM),
        out_shape=pltpu.HBM((128 * BLOCK, LANES), F32),
        scratch_shapes=[
            pltpu.VMEM((128 * BLOCK, LANES), F32),
            pltpu.VMEM((NU * (NU + 4), LANES), F32),
            pltpu.SemaphoreType.DMA((8,)),
        ],
        compiler_params=params(14),
        cost_estimate=pl.CostEstimate(flops=8_000_000, bytes_accessed=12_000_000, transcendentals=0),
        name="pack_probes",
    )(probes)


def pack_fields_kernel(
    kinds_hbm, label_hbm, sensor_hbm, weight_hbm, o_ref, kinds_ref, sensor_ref, weight_ref, label_ref, cond_ref, u_ref, sems
):
    k = lax.axis_index("sketch")
    lanes = lane_iota()
    shift = 8 + 64 * lax.rem(k, 2)
    first = lax.div(k + 1, 2) - 1
    start = jnp.clip(first, 0, 2)
    window_hbm = label_hbm.at[:, :, pl.ds(pl.multiple_of(start * LANES, LANES), 2 * LANES)]
    copies = [
        pltpu.make_async_copy(src, dst, sems.at[i])
        for i, (src, dst) in enumerate(
            (
                (window_hbm, label_ref),
                (kinds_hbm, kinds_ref),
                (sensor_hbm, sensor_ref),
                (weight_hbm, weight_ref),
            )
        )
    ]
    for copy in copies:
        copy.start()
    cols = 16
    u_ref[0:cols, :] = jnp.zeros((cols, LANES), F32)
    u_ref[cols * (NU + 1) :, :] = jnp.zeros((3 * cols, LANES), F32)
    for copy in copies:
        copy.wait()
    place = first - start
    first_at = pl.multiple_of(jnp.maximum(place, 0) * LANES, LANES)
    second_at = pl.multiple_of(jnp.minimum(place + 1, 1) * LANES, LANES)
    from_first = lanes < shift
    outside = (from_first & (first < 0)) | ((lanes >= shift) & (first + 1 > 3))

    def window(i, carry):
        for q in range(8):
            rows = pl.ds(pl.multiple_of(i * 64 + q * 8, 8), 8)
            for p in range(2):
                a = label_ref[p, rows, pl.ds(first_at, LANES)]
                b = label_ref[p, rows, pl.ds(second_at, LANES)]
                label = jnp.where(from_first, pltpu.roll(a, shift, 1), pltpu.roll(b, shift, 1))
                cond = jnp.zeros((8, LANES), F32)
                for kind in range(8):
                    cond = jnp.where(label == kind, kinds_ref[kind], cond)
                cond_ref[p, rows, :] = jnp.where(outside, 0.0, cond)
        return carry

    lax.fori_loop(0, NU // 8, window, 0)

    def group(g, carry):
        parts = [cond_ref[p, pl.ds(g * 64 + r, 8, stride=8), :] for p in range(2) for r in range(8)]
        for uc, part in enumerate(scatter_groups(parts)):
            if uc < 10:
                slot = (uc - 1) % 16
                u_ref[pl.ds((1 + 8 * g) * cols + slot, 8, stride=cols), :] = part
        return carry

    lax.fori_loop(0, 8, group, 0, unroll=2)

    cells = sensor_ref[...].astype(F32)
    weights = weight_ref[...]

    def tile(a, carry):
        out = a * SLAB_BLOCK
        at = 4 * a * cols
        for i in range(6):
            o_ref[pl.ds(out + 8 * i, 8), :] = u_ref[pl.ds(pl.multiple_of(at + i * cols, 8), 8), :]
        o_ref[pl.ds(out + 48, 8), :] = u_ref[pl.ds(at + 15, 8, stride=cols), :]
        o_ref[pl.ds(out + 56, 8), :] = u_ref[pl.ds(at + 8, 8, stride=cols), :]
        o_ref[pl.ds(out + FIELD_BLOCK, LIST_ROWS), :] = cells
        o_ref[pl.ds(out + FIELD_BLOCK + LIST_ROWS, LIST_ROWS), :] = weights
        return carry

    lax.fori_loop(0, NS, tile, 0)


def pack_fields(conductivity, labels, sensors, weights):
    return pl.pallas_call(
        pack_fields_kernel,
        in_specs=[pl.BlockSpec(memory_space=pltpu.HBM)] * 4,
        out_specs=pl.BlockSpec(memory_space=VMEM),
        out_shape=jax.ShapeDtypeStruct((NS * SLAB_BLOCK, LANES), F32),
        scratch_shapes=[
            pltpu.SMEM((8,), F32),
            pltpu.VMEM((LIST_ROWS, LANES), jnp.int32),
            pltpu.VMEM((LIST_ROWS, LANES), F32),
            pltpu.VMEM((2, NY, 2 * LANES), jnp.int32),
            pltpu.VMEM((2, NY, LANES), F32),
            pltpu.VMEM((16 * (NU + 4), LANES), F32),
            pltpu.SemaphoreType.DMA((4,)),
        ],
        compiler_params=params(10),
        cost_estimate=pl.CostEstimate(flops=8_000_000, bytes_accessed=12_000_000, transcendentals=0),
        name="pack_fields",
    )(*in_hbm(conductivity, labels, sensors.reshape(LIST_ROWS, LANES), weights.reshape(LIST_ROWS, LANES)))


def harmonic(left, right):
    total = jnp.maximum(left + right, 1e-30)
    return (2.0 * TIME_STEP) * left * right / total


FACE_ROWS = 12


def fields_kernel(r_ref, *refs):
    outs, refs = refs[:4], refs[4:]
    fr_ref, fc_ref, fp_ref, d_ref, cond_ref, unit_ref, place_ref, dense_ref, out_sems = refs
    row_0 = 32 * lax.axis_index("pde") - HALO
    col_0 = 64 * lax.axis_index("sketch") - HALO

    def slab(n, carry):
        at = pl.multiple_of(n * SLAB_BLOCK + FIELD_BLOCK, 8)
        cell = r_ref[pl.ds(at, LIST_ROWS), :].astype(jnp.int32)
        weight = r_ref[pl.ds(at + LIST_ROWS, LIST_ROWS), :]
        high = weight.astype(BF16).astype(F32)
        rest = weight - high
        row = (lax.shift_right_logical(cell, 9) & (NY - 1)) - row_0
        col = (cell & (NZ - 1)) - col_0
        inside = (row >= 0) & (row < ROWS) & (col >= 0) & (col < COLS)
        ur = lax.shift_right_arithmetic(row, 3)
        uc = lax.shift_right_arithmetic(col, 3)
        unit = jnp.where(uc == 0, 48 + ur, jnp.where(uc == 9, 56 + ur, 8 * ur + uc - 1))
        unit = jnp.where(inside, unit, -1)
        place = 64 * lax.shift_right_logical(cell, 18) + 8 * (row & 7) + (col & 7)
        unit_index = lax.broadcasted_iota(jnp.int32, (FIELD_BLOCK, LANES), 0)
        place_index = lax.broadcasted_iota(jnp.int32, (LANES, LANES), 0)
        for j in range(LIST_ROWS):
            span = pl.ds(j * LANES, LANES)
            unit_ref[:, span] = jnp.where(unit_index == unit[j : j + 1], 1.0, 0.0).astype(BF16)
            hit = place_index == place[j : j + 1]
            place_ref[0:LANES, span] = jnp.where(hit, high[j : j + 1], 0.0).astype(BF16)
            place_ref[LANES:, span] = jnp.where(hit, rest[j : j + 1], 0.0).astype(BF16)
        got = lax.dot_general(
            unit_ref[...], place_ref[...], (((1,), (1,)), ((), ())), preferred_element_type=F32
        )
        dense_ref[pl.ds(pl.multiple_of(n * FIELD_BLOCK, 8), FIELD_BLOCK), :] = got[:, :LANES] + got[:, LANES:]
        return carry

    lax.fori_loop(0, NS, slab, 0)
    zero8 = jnp.zeros((8, LANES), F32)
    for p in range(2):

        def clear(i, carry, p=p):
            cond_ref[p, i, COLS : COLS + 8, :] = zero8
            fc_ref[p, i, 0:8, :] = zero8
            return carry

        lax.fori_loop(0, ROWS, clear, 0)

    def unpack(src, stride, turn, ref, row, ur, col):
        block = src[pl.ds(row, NS, stride=stride), :]
        turned = jnp.concatenate([block] * NP, axis=0).T
        for g in range(16):
            m = (g - turn * (col // 8)) % 16
            ref[m // 8, ur * 8 + m % 8, pl.ds(col, 8), :] = turned[8 * g : 8 * g + 8]

    for what in ((dense_ref, FIELD_BLOCK, 0, d_ref), (r_ref, SLAB_BLOCK, 1, cond_ref)):

        def rows(ur, carry, what=what):
            for uc in range(8):
                unpack(*what, ur * 8 + uc, ur, HALO + 8 * uc)
            unpack(*what, 48 + ur, ur, 0)
            unpack(*what, 56 + ur, ur, HALO + CORE_C)
            return carry

        lax.fori_loop(0, 6, rows, 0)

    last_slab = (lane_iota() & (NS - 1)) == NS - 1

    def faces(i, carry):
        nxt = jnp.minimum(i + 1, ROWS - 1)
        for cb in range(10):
            at = pl.ds(8 * cb, 8)
            c0, c1 = cond_ref[0, i, at, :], cond_ref[1, i, at, :]
            fr_ref[0, i, at, :] = harmonic(c0, cond_ref[0, nxt, at, :])
            fr_ref[1, i, at, :] = harmonic(c1, cond_ref[1, nxt, at, :])
            aside = pl.ds(8 * cb + 1, 8)
            fc_ref[0, i, pl.ds(8 + 8 * cb, 8), :] = harmonic(c0, cond_ref[0, i, aside, :])
            fc_ref[1, i, pl.ds(8 + 8 * cb, 8), :] = harmonic(c1, cond_ref[1, i, aside, :])
            fp_ref[0, i, at, :] = harmonic(c0, c1)
            beyond = pltpu.roll(c0, LANES - 1, 1)
            outer = jnp.where(last_slab, 0.0, harmonic(c1, beyond))
            fp_ref[1, i, at, :] = outer
            fp_ref[2, i, at, :] = pltpu.roll(outer, 1, 1)
        return carry

    copies = [pltpu.make_async_copy(d_ref, outs[3], out_sems.at[0])]
    copies[0].start()
    for first in range(0, ROWS, FACE_ROWS):
        lax.fori_loop(first, first + FACE_ROWS, faces, 0)
        for ref, out in zip((fr_ref, fc_ref, fp_ref), outs):
            at = pl.ds(first, FACE_ROWS)
            copy = pltpu.make_async_copy(ref.at[:, at], out.at[:, at], out_sems.at[len(copies)])
            copy.start()
            copies.append(copy)
    for copy in copies:
        copy.wait()


def make_fields(received):
    shapes = [(2, ROWS, COLS, LANES), (2, ROWS, COLS + 8, LANES), (3, ROWS, COLS, LANES), (2, ROWS, COLS, LANES)]
    return pl.pallas_call(
        fields_kernel,
        in_specs=[pl.BlockSpec(memory_space=VMEM)],
        out_specs=[pl.BlockSpec(memory_space=pltpu.HBM)] * 4,
        out_shape=[pltpu.HBM(shape, F32) for shape in shapes],
        scratch_shapes=[
            *[pltpu.VMEM(shape, F32) for shape in shapes],
            pltpu.VMEM((2, ROWS, COLS + 8, LANES), F32),
            pltpu.VMEM((FIELD_BLOCK, 2048), BF16),
            pltpu.VMEM((2 * LANES, 2048), BF16),
            pltpu.VMEM((NS * FIELD_BLOCK, LANES), F32),
            pltpu.SemaphoreType.DMA((1 + 3 * ROWS // FACE_ROWS,)),
        ],
        compiler_params=params(32),
        cost_estimate=pl.CostEstimate(flops=40_000_000, bytes_accessed=30_000_000, transcendentals=0),
        name="make_fields",
    )(received)


def solve_kernel(
    r_hbm,
    near_ref,
    fr_hbm,
    fc_hbm,
    fp_hbm,
    d_hbm,
    y_ref,
    gram_ref,
    r_ref,
    fr_ref,
    fc_ref,
    fp_ref,
    d_ref,
    ua_ref,
    ub_ref,
    prod_ref,
    side_ref,
    sems,
):
    tiles_copy = pltpu.make_async_copy(r_hbm, r_ref, sems.at[0])
    tiles_copy.start()
    face_copies = []
    for c in range(ROWS // FACE_ROWS):
        at = pl.ds(c * FACE_ROWS, FACE_ROWS)
        face_copies.append(
            [
                pltpu.make_async_copy(src.at[:, at], dst.at[:, at], sems.at[2 + 3 * c + n])
                for n, (src, dst) in enumerate(((fr_hbm, fr_ref), (fc_hbm, fc_ref), (fp_hbm, fp_ref)))
            ]
        )
    dense_copy = pltpu.make_async_copy(d_hbm, d_ref, sems.at[1])
    odd = lax.rem(lax.axis_index("sketch"), 2)
    zero8 = jnp.zeros((8, LANES), F32)
    for ref in (ua_ref, ub_ref):
        for p in range(2):

            def clear(i, carry, p=p, ref=ref):
                ref[p, i, 0:8, :] = zero8
                ref[p, i, 8 + COLS : 16 + COLS, :] = zero8
                return carry

            lax.fori_loop(0, ROWS, clear, 0)
    tiles_copy.wait()
    core = lax.rem(lax.axis_index("pde"), 2)

    def fetch(n):
        for copy in (face_copies + [[dense_copy]])[n]:
            copy.start()

    fetch(0)
    fetch(1)

    def unpack(ref, stride, row, ur, col):
        turned = ref[pl.ds(row, LANES, stride=stride), :].T
        for g in range(16):
            m = (g - (col // 8 - 1)) % 16
            ua_ref[lax.rem(m // 8 + odd, 2), ur * 8 + m % 8, pl.ds(8 + col, 8), :] = turned[8 * g : 8 * g + 8]

    for ref, stride, ur in ((r_ref, BLOCK, 4 - 3 * core), (near_ref, EDGE, 5 - 5 * core)):
        for uc in range(8):
            unpack(ref, stride, uc, ur, HALO + 8 * uc)
        unpack(ref, stride, 8, ur, 0)
        unpack(ref, stride, 9, ur, HALO + CORE_C)

    def rows(q, carry):
        ur = q + 2 * core
        for uc in range(8):
            unpack(r_ref, BLOCK, EDGE + 8 * q + uc, ur, HALO + 8 * uc)
        unpack(r_ref, BLOCK, EDGE + 32 + q, ur, 0)
        unpack(r_ref, BLOCK, EDGE + 36 + q, ur, HALO + CORE_C)
        return carry

    lax.fori_loop(0, 2, rows, 0)
    fetch(2)
    lax.fori_loop(2, 4, rows, 0)

    def keep(i, carry):
        for p in range(2):
            for cb in range(8):
                prod_ref[p, i, pl.ds(8 * cb, 8), :] = (
                    PRIOR_WEIGHT * ua_ref[p, i + HALO, pl.ds(8 + HALO + 8 * cb, 8), :]
                )
        return carry

    lax.fori_loop(0, CORE_R, keep, 0)

    def advance(src, dst, step, blocks):
        last = step == 2 * STEPS

        def flow(p, i, cb):
            at = pl.ds(8 + 8 * cb, 8)
            return fr_ref[p, i, pl.ds(8 * cb, 8), :] * (src[p, i + 1, at, :] - src[p, i, at, :])

        mids = [pl.ds(8 + 8 * cb, 8) for cb in blocks]

        def beside(n, i):
            return (
                pltpu.roll(src[0, i, mids[n], :], LANES - 1, 1),
                pltpu.roll(src[1, i, mids[n], :], 1, 1),
            )

        def some_rows(first, count, carry):
            flows, beyond = carry
            for slot in range(count):
                i = first + slot
                new_flows = []
                new_beyond = []
                for n, (cb, mid) in enumerate(zip(blocks, mids)):
                    at = pl.ds(8 * cb, 8)
                    right = pl.ds(9 + 8 * cb, 8)
                    left = pl.ds(7 + 8 * cb, 8)
                    u = [src[p, i, mid, :] for p in range(2)]
                    new = []
                    for p in range(2):
                        row_flow = fr_ref[p, i, at, :] * (src[p, i + 1, mid, :] - u[p])
                        change = row_flow - flows[2 * n + p]
                        new_flows.append(row_flow)
                        to_right = fc_ref[p, i, mid, :] * (src[p, i, right, :] - u[p])
                        if VIA_SCRATCH:
                            side_ref[slot, p, mid, :] = to_right
                            if n == 0:
                                from_left = fc_ref[p, i, left, :] * (u[p] - src[p, i, left, :])
                            else:
                                from_left = side_ref[slot, p, left, :]
                            change += to_right - from_left
                        else:
                            change += to_right
                            change += fc_ref[p, i, left, :] * (src[p, i, left, :] - u[p])
                        new.append(u[p] + change)
                    new_beyond.append(beside(n, i + 1))
                    inner = fp_ref[0, i, at, :] * (u[1] - u[0])
                    below = fp_ref[2, i, at, :] * (beyond[n][1] - u[0])
                    above = fp_ref[1, i, at, :] * (beyond[n][0] - u[1])
                    both = [new[0] + (below + inner), new[1] + (above - inner)]
                    for p in range(2):
                        if step == STEPS:
                            both[p] = both[p] * d_ref[p, i, at, :]
                        if last:
                            core = pl.ds(8 * (cb - 1), 8)
                            prod_ref[p, i - HALO, core, :] += both[p]
                        else:
                            dst[p, i, mid, :] = both[p]
                flows, beyond = tuple(new_flows), tuple(new_beyond)
            return flows, beyond

        end = ROWS - step
        if step == 1:
            cuts = [step] + [FACE_ROWS * (c + 1) - 3 for c in range(ROWS // FACE_ROWS - 1)] + [end]
        else:
            cuts = [step, end]
        carry = None
        for c, (low, high) in enumerate(zip(cuts[:-1], cuts[1:])):
            if step == 1:
                for copy in face_copies[c]:
                    copy.wait()
                if c < 2:
                    fetch(3 + c)
            if carry is None:
                flows = tuple(flow(p, step - 1, cb) for cb in blocks for p in range(2))
                carry = (flows, tuple(beside(n, step) for n in range(len(blocks))))
            carry = lax.fori_loop(
                0,
                (high - low) // UNROLL,
                lambda t, carry, low=low: some_rows(low + t * UNROLL, UNROLL, carry),
                carry,
            )
            rest = (high - low) % UNROLL
            if rest:
                carry = some_rows(high - rest, rest, carry)

    refs = (ua_ref, ub_ref)
    for step in range(1, 2 * STEPS + 1):
        if step == STEPS:
            dense_copy.wait()
        first, end = (1, 9) if step == 2 * STEPS else (0, 10)
        for at in range(first, end, WIDTH):
            blocks = list(range(at, min(at + WIDTH, end)))
            advance(refs[(step - 1) % 2], refs[step % 2], step, blocks)

    def units(ur, carry):
        for uc in range(8):
            parts = []
            for g in range(16):
                m = (g - uc) % 16
                parts.append(prod_ref[lax.rem(m // 8 + odd, 2), ur * 8 + m % 8, pl.ds(8 * uc, 8), :])
            turned = jnp.concatenate(parts, axis=0).T
            high = turned.astype(BF16)
            at = pl.ds(pl.multiple_of((ur * 8 + uc) * LANES, LANES), LANES)
            y_ref[0:LANES, at] = high
            y_ref[LANES:, at] = (turned - high.astype(F32)).astype(BF16)
        return carry

    lax.fori_loop(0, 4, units, 0)
    both = lax.dot_general(y_ref[0:LANES, :], y_ref[...], (((1,), (1,)), ((), ())), preferred_element_type=F32)
    mixed = both[:, LANES:]
    gram = both[:, :LANES] + (mixed + mixed.T)
    slab_of_row = lax.broadcasted_iota(jnp.int32, (LANES, LANES), 0) & (NS - 1)
    slab_of_lane = lax.broadcasted_iota(jnp.int32, (LANES, LANES), 1) & (NS - 1)
    gram = jnp.where(slab_of_row == slab_of_lane, gram, 0.0)
    by_probe = jnp.sum(gram.reshape(NP, NS, LANES), axis=1)
    same = (
        lax.shift_right_logical(lax.broadcasted_iota(jnp.int32, (LANES, LANES), 0), 4)
        == lax.shift_right_logical(lax.broadcasted_iota(jnp.int32, (LANES, LANES), 1), 4)
    ).astype(F32)
    by_probe = jnp.dot(by_probe, same, precision=lax.Precision.HIGHEST, preferred_element_type=F32)
    own = (lane_iota() & (NS - 1)) == lax.broadcasted_iota(jnp.int32, (8, LANES), 0)
    row = jnp.sum(jnp.where(own, by_probe, 0.0), axis=0, keepdims=True)
    gram_ref[...] = jnp.broadcast_to(row, (LANES, LANES))


def solve(received, near, faces):
    vmem = pl.BlockSpec(memory_space=VMEM)
    hbm = pl.BlockSpec(memory_space=pltpu.HBM)
    received, *faces = in_hbm(received, *faces)
    return pl.pallas_call(
        solve_kernel,
        in_specs=[hbm, vmem] + [hbm] * 4,
        out_specs=[vmem] * 2,
        out_shape=[
            jax.ShapeDtypeStruct((2 * LANES, 32 * LANES), BF16),
            jax.ShapeDtypeStruct((LANES, LANES), F32),
        ],
        scratch_shapes=[
            pltpu.VMEM((128 * BLOCK, LANES), F32),
            pltpu.VMEM((2, ROWS, COLS, LANES), F32),
            pltpu.VMEM((2, ROWS, COLS + 8, LANES), F32),
            pltpu.VMEM((3, ROWS, COLS, LANES), F32),
            pltpu.VMEM((2, ROWS, COLS, LANES), F32),
            pltpu.VMEM((2, ROWS, COLS + 16, LANES), F32),
            pltpu.VMEM((2, ROWS, COLS + 16, LANES), F32),
            pltpu.VMEM((2, CORE_R, CORE_C, LANES), F32),
            pltpu.VMEM((UNROLL, 2, COLS + 8, LANES), F32),
            pltpu.SemaphoreType.DMA((2 + 3 * ROWS // FACE_ROWS,)),
        ],
        compiler_params=params(42),
        cost_estimate=pl.CostEstimate(flops=100_000_000, bytes_accessed=30_000_000, transcendentals=0),
        name="solve",
    )(received, near, *faces)


def basis_kernel(gram_ref, y_ref, o_ref, factor_ref, *, cells):
    lanes = lane_iota()
    sublanes = lax.broadcasted_iota(jnp.int32, (8, LANES), 0)
    total = gram_ref[0:8, :]
    for i in range(1, LANES // 8):
        total = total + gram_ref[8 * i : 8 * i + 8, :]
    row = jnp.broadcast_to(jnp.sum(total, axis=0, keepdims=True), (8, LANES)) / cells

    def entry(i, j):
        at = j * NS + i
        return jnp.broadcast_to(row[:, at : at + 1], (8, LANES))

    lower = {}
    inv_diag = []
    for j in range(NP):
        pivot = entry(j, j)
        for m in range(j):
            pivot = pivot - lower[j, m] * lower[j, m]
        lower[j, j] = jnp.sqrt(pivot)
        inv_diag.append(1.0 / lower[j, j])
        for i in range(j + 1, NP):
            value = entry(i, j)
            for m in range(j):
                value = value - lower[i, m] * lower[j, m]
            lower[i, j] = value * inv_diag[j]
    inverse = {}
    for i in range(NP):
        inverse[i, i] = inv_diag[i]
        for j in range(i):
            carried = lower[i, j] * inverse[j, j]
            for m in range(j + 1, i):
                carried = carried + lower[i, m] * inverse[m, j]
            inverse[i, j] = -carried * inv_diag[i]

    factor = jnp.zeros((8, LANES), F32)
    for (i, j), value in lower.items():
        factor = jnp.where((sublanes == j) & (lanes == i), value, factor)
    factor_ref[...] = factor

    probe = lax.shift_right_logical(lanes, 4)
    mix = []
    for i in range(NP):
        coef = jnp.zeros((8, LANES), F32)
        for j in range(i + 1):
            coef = jnp.where(probe == j, inverse[i, j], coef)
        for half in range(2):
            mix.append(jnp.where((lanes & (NS - 1)) == sublanes + 8 * half, coef, 0.0))
    mix = jnp.concatenate(mix, axis=0)
    high = mix.astype(BF16)
    low = (mix - high.astype(F32)).astype(BF16)
    twice = jnp.concatenate([high, high], axis=1)

    def units(ur, carry):
        for uc in range(8):
            at = pl.ds(pl.multiple_of((ur * 8 + uc) * LANES, LANES), LANES)
            o_ref[pl.ds(ur * 8 + uc, LANES, stride=32), :] = jnp.dot(
                twice, y_ref[:, at], preferred_element_type=F32
            ) + jnp.dot(low, y_ref[0:LANES, at], preferred_element_type=F32)
        return carry

    lax.fori_loop(0, 4, units, 0)


def make_basis(grams, products):
    cells = float(2 * NS * NY * NZ)
    return pl.pallas_call(
        functools.partial(basis_kernel, cells=cells),
        in_specs=[pl.BlockSpec(memory_space=VMEM)] * 2,
        out_specs=[pl.BlockSpec(memory_space=VMEM)] * 2,
        out_shape=[
            jax.ShapeDtypeStruct((128 * 32, LANES), F32),
            jax.ShapeDtypeStruct((8, LANES), F32),
        ],
        compiler_params=params(10),
        cost_estimate=pl.CostEstimate(flops=10_000_000, bytes_accessed=4_000_000, transcendentals=0),
        name="make_basis",
    )(grams, products)


def unpack_kernel(r_ref, o_ref):
    def group(g, carry):
        parts = [
            r_ref[pl.ds(b * 512 + g * 64 + uc, 8, stride=8), :] for b in range(2) for uc in range(8)
        ]
        turned = gather_groups(parts)
        for p in range(2):
            for r in range(8):
                o_ref[0, p, pl.ds(g * 64 + r, 8, stride=8), :] = turned[p * 8 + r]
        return carry

    lax.fori_loop(0, 8, group, 0, unroll=2)


def unpack_basis(received):
    return pl.pallas_call(
        unpack_kernel,
        grid=(4,),
        in_specs=[pl.BlockSpec((1024, LANES), lambda j: (j, 0))],
        out_specs=pl.BlockSpec((1, 2, NY, LANES), lambda j: (0, 0, 0, j)),
        out_shape=jax.ShapeDtypeStruct((1, 2, NY, NZ), F32),
        compiler_params=params(10),
        cost_estimate=pl.CostEstimate(flops=8_000_000, bytes_accessed=4_000_000, transcendentals=0),
        name="unpack_basis",
    )(received)


def exchange(rows, axes):
    return lax.all_to_all(rows, axes, split_axis=0, concat_axis=0, tiled=True)


def on_device(probes, ply_labels, conductivity, sensors, sensor_weight):
    every = ("sketch", "pde")
    fields = pack_fields(conductivity, ply_labels, sensors, sensor_weight)
    fields, probes = lax.optimization_barrier((fields, probes))
    fields, packed = lax.optimization_barrier((exchange(fields, "pde"), pack_probes(probes)))
    tiles = exchange(packed.reshape(LANES, BLOCK // 2, 2, LANES), every)
    tiles, faces = lax.optimization_barrier((tiles, make_fields(fields)))
    near = lax.ppermute(tiles[:, : EDGE // 2], "pde", [(i, i ^ 1) for i in range(NS)])
    products, gram = solve(tiles.reshape(-1, LANES), near.reshape(-1, LANES), faces)
    grams = exchange(gram, every)
    columns, factor = make_basis(grams, products)
    basis = unpack_basis(exchange(columns, every))
    return (basis, factor[:, :NP])


def solution(mesh):
    placed = (P("sketch", "pde", None, None), P("pde", None, None), P(), P("pde"), P("pde"))
    return jax.shard_map(
        on_device,
        mesh=mesh,
        in_specs=placed,
        out_specs=(P("sketch", "pde", None, None), P()),
        check_vma=False,
    )
```

```python
import functools

import jax
import jax.numpy as jnp
from jax import lax
from jax.experimental import pallas as pl
from jax.experimental.pallas import tpu as pltpu
from jax.sharding import PartitionSpec as P

STEPS = 4
TIME_STEP = 0.15
PRIOR_WEIGHT = 0.1

F32 = jnp.float32
BF16 = jnp.bfloat16
LANES = 128
NP = 8
NS = 16
NY = 512
NZ = 512
NU = 64
HALO = 8
ROWS = 48
COLS = 80
CORE_R = 32
CORE_C = 64
BLOCK = 50
EDGE = 10
FIELD_BLOCK = 64
LIST_ROWS = 16
SLAB_BLOCK = FIELD_BLOCK + 2 * LIST_ROWS
VMEM = pltpu.MemorySpace.VMEM
UNROLL = 4
WIDTH = 10
VIA_SCRATCH = False


def params(mebibytes):
    return pltpu.CompilerParams(vmem_limit_bytes=mebibytes * 1024 * 1024)


def in_hbm(*arrays):
    return [pltpu.with_memory_space_constraint(array, pltpu.HBM) for array in arrays]


def lane_iota(shape=(8, LANES)):
    return lax.broadcasted_iota(jnp.int32, shape, len(shape) - 1)


def scatter_groups(parts):
    group = lax.shift_right_logical(lane_iota(), 3)
    parts = [pltpu.roll(part, 8 * m, 1) if m else part for m, part in enumerate(parts)]
    for bit in range(4):
        ahead = (group & (1 << bit)) != 0
        parts = [jnp.where(ahead, parts[(i + (1 << bit)) % 16], parts[i]) for i in range(16)]
    return [parts[(-u) % 16] for u in range(16)]


def gather_groups(parts):
    group = lax.shift_right_logical(lane_iota(), 3)
    parts = [parts[(-i) % 16] for i in range(16)]
    for bit in range(4):
        behind = (group & (1 << bit)) != 0
        parts = [jnp.where(behind, parts[(i - (1 << bit)) % 16], parts[i]) for i in range(16)]
    return [pltpu.roll(part, LANES - 8 * m, 1) if m else part for m, part in enumerate(parts)]


def pack_probes_kernel(x_ref, o_hbm, o_ref, u_ref, sems):
    step = pl.program_id(0)
    cols = NU

    @pl.when(step == 0)
    def _():
        u_ref[0:cols, :] = jnp.zeros((cols, LANES), F32)
        u_ref[cols * (NU + 1) : cols * (NU + 4), :] = jnp.zeros((3 * cols, LANES), F32)

    def part(b):
        at = pl.ds(b * NS * BLOCK, NS * BLOCK)
        return pltpu.make_async_copy(o_ref.at[at, :], o_hbm.at[at, :], sems.at[b])

    def group(g, carry):
        parts = [
            x_ref[0, p, pl.ds(g * 64 + r, 8, stride=8), :] for p in range(2) for r in range(8)
        ]
        for uc, part in enumerate(scatter_groups(parts)):
            u_ref[pl.ds((1 + 8 * g) * cols + 16 * step + uc, 8, stride=cols), :] = part
        return carry

    lax.fori_loop(0, 8, group, 0)

    @pl.when(step == 3)
    def _():
        for b in range(8):

            def tile(a, carry, b=b):
                out = (b * NS + a) * BLOCK
                core = lax.rem(a, 2)
                edge = (4 * a + 4 - 3 * core) * cols + 8 * b
                inner = (4 * a + 2 * core) * cols + 8 * b
                o_ref[pl.ds(out, 8), :] = u_ref[pl.ds(pl.multiple_of(edge, 8), 8), :]
                for q in range(4):
                    o_ref[pl.ds(out + EDGE + 8 * q, 8), :] = u_ref[
                        pl.ds(pl.multiple_of(inner + q * cols, 8), 8), :
                    ]
                for side, offset in enumerate((-1, 8)):
                    if 0 <= 8 * b + offset < cols:
                        one = u_ref[pl.ds(edge + offset, 1), :]
                        four = u_ref[pl.ds(inner + offset, 4, stride=cols), :]
                    else:
                        one = jnp.zeros((1, LANES), F32)
                        four = jnp.zeros((4, LANES), F32)
                    o_ref[pl.ds(out + 8 + side, 1), :] = one
                    o_ref[pl.ds(out + EDGE + 32 + 4 * side, 4), :] = four
                return carry

            lax.fori_loop(0, NS, tile, 0)
            part(b).start()
        for b in range(8):
            part(b).wait()


def pack_probes(probes):
    return pl.pallas_call(
        pack_probes_kernel,
        grid=(4,),
        in_specs=[pl.BlockSpec((1, 2, NY, LANES), lambda j: (0, 0, 0, j))],
        out_specs=pl.BlockSpec(memory_space=pltpu.HBM),
        out_shape=pltpu.HBM((128 * BLOCK, LANES), F32),
        scratch_shapes=[
            pltpu.VMEM((128 * BLOCK, LANES), F32),
            pltpu.VMEM((NU * (NU + 4), LANES), F32),
            pltpu.SemaphoreType.DMA((8,)),
        ],
        compiler_params=params(14),
        cost_estimate=pl.CostEstimate(flops=8_000_000, bytes_accessed=12_000_000, transcendentals=0),
        name="pack_probes",
    )(probes)


def pack_fields_kernel(
    kinds_hbm, label_hbm, sensor_hbm, weight_hbm, o_ref, kinds_ref, sensor_ref, weight_ref, label_ref, cond_ref, u_ref, sems
):
    k = lax.axis_index("sketch")
    lanes = lane_iota()
    shift = 8 + 64 * lax.rem(k, 2)
    first = lax.div(k + 1, 2) - 1
    start = jnp.clip(first, 0, 2)
    window_hbm = label_hbm.at[:, :, pl.ds(pl.multiple_of(start * LANES, LANES), 2 * LANES)]
    upper, lower = pl.ds(0, NY // 2), pl.ds(NY // 2, NY // 2)
    copies = [
        pltpu.make_async_copy(src, dst, sems.at[i])
        for i, (src, dst) in enumerate(
            (
                (window_hbm.at[:, upper], label_ref.at[:, upper]),
                (window_hbm.at[:, lower], label_ref.at[:, lower]),
                (kinds_hbm, kinds_ref),
                (sensor_hbm, sensor_ref),
                (weight_hbm, weight_ref),
            )
        )
    ]
    for copy in copies:
        copy.start()
    cols = 16
    u_ref[0:cols, :] = jnp.zeros((cols, LANES), F32)
    u_ref[cols * (NU + 1) :, :] = jnp.zeros((3 * cols, LANES), F32)
    copies[0].wait()
    copies[2].wait()
    place = first - start
    first_at = pl.multiple_of(jnp.maximum(place, 0) * LANES, LANES)
    second_at = pl.multiple_of(jnp.minimum(place + 1, 1) * LANES, LANES)
    from_first = lanes < shift
    outside = (from_first & (first < 0)) | ((lanes >= shift) & (first + 1 > 3))

    def window(i, carry):
        for q in range(8):
            rows = pl.ds(pl.multiple_of(i * 64 + q * 8, 8), 8)
            for p in range(2):
                a = label_ref[p, rows, pl.ds(first_at, LANES)]
                b = label_ref[p, rows, pl.ds(second_at, LANES)]
                label = jnp.where(from_first, pltpu.roll(a, shift, 1), pltpu.roll(b, shift, 1))
                cond = jnp.zeros((8, LANES), F32)
                for kind in range(8):
                    cond = jnp.where(label == kind, kinds_ref[kind], cond)
                cond_ref[p, rows, :] = jnp.where(outside, 0.0, cond)
        return carry

    lax.fori_loop(0, NU // 16, window, 0)
    copies[1].wait()
    lax.fori_loop(NU // 16, NU // 8, window, 0)

    def group(g, carry):
        parts = [cond_ref[p, pl.ds(g * 64 + r, 8, stride=8), :] for p in range(2) for r in range(8)]
        for uc, part in enumerate(scatter_groups(parts)):
            if uc < 10:
                slot = (uc - 1) % 16
                u_ref[pl.ds((1 + 8 * g) * cols + slot, 8, stride=cols), :] = part
        return carry

    lax.fori_loop(0, 8, group, 0, unroll=2)

    copies[3].wait()
    copies[4].wait()
    cells = sensor_ref[...].astype(F32)
    weights = weight_ref[...]

    def tile(a, carry):
        out = a * SLAB_BLOCK
        at = 4 * a * cols
        for i in range(6):
            o_ref[pl.ds(out + 8 * i, 8), :] = u_ref[pl.ds(pl.multiple_of(at + i * cols, 8), 8), :]
        o_ref[pl.ds(out + 48, 8), :] = u_ref[pl.ds(at + 15, 8, stride=cols), :]
        o_ref[pl.ds(out + 56, 8), :] = u_ref[pl.ds(at + 8, 8, stride=cols), :]
        o_ref[pl.ds(out + FIELD_BLOCK, LIST_ROWS), :] = cells
        o_ref[pl.ds(out + FIELD_BLOCK + LIST_ROWS, LIST_ROWS), :] = weights
        return carry

    lax.fori_loop(0, NS, tile, 0)


def pack_fields(conductivity, labels, sensors, weights):
    return pl.pallas_call(
        pack_fields_kernel,
        in_specs=[pl.BlockSpec(memory_space=pltpu.HBM)] * 4,
        out_specs=pl.BlockSpec(memory_space=VMEM),
        out_shape=jax.ShapeDtypeStruct((NS * SLAB_BLOCK, LANES), F32),
        scratch_shapes=[
            pltpu.SMEM((8,), F32),
            pltpu.VMEM((LIST_ROWS, LANES), jnp.int32),
            pltpu.VMEM((LIST_ROWS, LANES), F32),
            pltpu.VMEM((2, NY, 2 * LANES), jnp.int32),
            pltpu.VMEM((2, NY, LANES), F32),
            pltpu.VMEM((16 * (NU + 4), LANES), F32),
            pltpu.SemaphoreType.DMA((5,)),
        ],
        compiler_params=params(10),
        cost_estimate=pl.CostEstimate(flops=8_000_000, bytes_accessed=12_000_000, transcendentals=0),
        name="pack_fields",
    )(*in_hbm(conductivity, labels, sensors.reshape(LIST_ROWS, LANES), weights.reshape(LIST_ROWS, LANES)))


def harmonic(left, right):
    total = jnp.maximum(left + right, 1e-30)
    return (2.0 * TIME_STEP) * left * right / total


FACE_ROWS = 12


def fields_kernel(r_ref, *refs):
    outs, refs = refs[:4], refs[4:]
    fr_ref, fc_ref, fp_ref, d_ref, cond_ref, unit_ref, place_ref, dense_ref, out_sems = refs
    row_0 = 32 * lax.axis_index("pde") - HALO
    col_0 = 64 * lax.axis_index("sketch") - HALO

    def slab(n, carry):
        at = pl.multiple_of(n * SLAB_BLOCK + FIELD_BLOCK, 8)
        cell = r_ref[pl.ds(at, LIST_ROWS), :].astype(jnp.int32)
        weight = r_ref[pl.ds(at + LIST_ROWS, LIST_ROWS), :]
        high = weight.astype(BF16).astype(F32)
        rest = weight - high
        row = (lax.shift_right_logical(cell, 9) & (NY - 1)) - row_0
        col = (cell & (NZ - 1)) - col_0
        inside = (row >= 0) & (row < ROWS) & (col >= 0) & (col < COLS)
        ur = lax.shift_right_arithmetic(row, 3)
        uc = lax.shift_right_arithmetic(col, 3)
        unit = jnp.where(uc == 0, 48 + ur, jnp.where(uc == 9, 56 + ur, 8 * ur + uc - 1))
        unit = jnp.where(inside, unit, -1)
        place = 64 * lax.shift_right_logical(cell, 18) + 8 * (row & 7) + (col & 7)
        unit_index = lax.broadcasted_iota(jnp.int32, (FIELD_BLOCK, LANES), 0)
        place_index = lax.broadcasted_iota(jnp.int32, (LANES, LANES), 0)
        for j in range(LIST_ROWS):
            span = pl.ds(j * LANES, LANES)
            unit_ref[:, span] = jnp.where(unit_index == unit[j : j + 1], 1.0, 0.0).astype(BF16)
            hit = place_index == place[j : j + 1]
            place_ref[0:LANES, span] = jnp.where(hit, high[j : j + 1], 0.0).astype(BF16)
            place_ref[LANES:, span] = jnp.where(hit, rest[j : j + 1], 0.0).astype(BF16)
        got = lax.dot_general(
            unit_ref[...], place_ref[...], (((1,), (1,)), ((), ())), preferred_element_type=F32
        )
        dense_ref[pl.ds(pl.multiple_of(n * FIELD_BLOCK, 8), FIELD_BLOCK), :] = got[:, :LANES] + got[:, LANES:]
        return carry

    lax.fori_loop(0, NS, slab, 0)
    zero8 = jnp.zeros((8, LANES), F32)
    for p in range(2):

        def clear(i, carry, p=p):
            cond_ref[p, i, COLS : COLS + 8, :] = zero8
            fc_ref[p, i, 0:8, :] = zero8
            return carry

        lax.fori_loop(0, ROWS, clear, 0)

    def unpack(src, stride, turn, ref, row, ur, col):
        block = src[pl.ds(row, NS, stride=stride), :]
        turned = jnp.concatenate([block] * NP, axis=0).T
        for g in range(16):
            m = (g - turn * (col // 8)) % 16
            ref[m // 8, ur * 8 + m % 8, pl.ds(col, 8), :] = turned[8 * g : 8 * g + 8]

    for what in ((dense_ref, FIELD_BLOCK, 0, d_ref), (r_ref, SLAB_BLOCK, 1, cond_ref)):

        def rows(ur, carry, what=what):
            for uc in range(8):
                unpack(*what, ur * 8 + uc, ur, HALO + 8 * uc)
            unpack(*what, 48 + ur, ur, 0)
            unpack(*what, 56 + ur, ur, HALO + CORE_C)
            return carry

        lax.fori_loop(0, 6, rows, 0)

    last_slab = (lane_iota() & (NS - 1)) == NS - 1

    def faces(i, carry):
        nxt = jnp.minimum(i + 1, ROWS - 1)
        for cb in range(10):
            at = pl.ds(8 * cb, 8)
            c0, c1 = cond_ref[0, i, at, :], cond_ref[1, i, at, :]
            fr_ref[0, i, at, :] = harmonic(c0, cond_ref[0, nxt, at, :])
            fr_ref[1, i, at, :] = harmonic(c1, cond_ref[1, nxt, at, :])
            aside = pl.ds(8 * cb + 1, 8)
            fc_ref[0, i, pl.ds(8 + 8 * cb, 8), :] = harmonic(c0, cond_ref[0, i, aside, :])
            fc_ref[1, i, pl.ds(8 + 8 * cb, 8), :] = harmonic(c1, cond_ref[1, i, aside, :])
            fp_ref[0, i, at, :] = harmonic(c0, c1)
            beyond = pltpu.roll(c0, LANES - 1, 1)
            outer = jnp.where(last_slab, 0.0, harmonic(c1, beyond))
            fp_ref[1, i, at, :] = outer
            fp_ref[2, i, at, :] = pltpu.roll(outer, 1, 1)
        return carry

    copies = [pltpu.make_async_copy(d_ref, outs[3], out_sems.at[0])]
    copies[0].start()
    for first in range(0, ROWS, FACE_ROWS):
        lax.fori_loop(first, first + FACE_ROWS, faces, 0)
        for ref, out in zip((fr_ref, fc_ref, fp_ref), outs):
            at = pl.ds(first, FACE_ROWS)
            copy = pltpu.make_async_copy(ref.at[:, at], out.at[:, at], out_sems.at[len(copies)])
            copy.start()
            copies.append(copy)
    for copy in copies:
        copy.wait()


def make_fields(received):
    shapes = [(2, ROWS, COLS, LANES), (2, ROWS, COLS + 8, LANES), (3, ROWS, COLS, LANES), (2, ROWS, COLS, LANES)]
    return pl.pallas_call(
        fields_kernel,
        in_specs=[pl.BlockSpec(memory_space=VMEM)],
        out_specs=[pl.BlockSpec(memory_space=pltpu.HBM)] * 4,
        out_shape=[pltpu.HBM(shape, F32) for shape in shapes],
        scratch_shapes=[
            *[pltpu.VMEM(shape, F32) for shape in shapes],
            pltpu.VMEM((2, ROWS, COLS + 8, LANES), F32),
            pltpu.VMEM((FIELD_BLOCK, 2048), BF16),
            pltpu.VMEM((2 * LANES, 2048), BF16),
            pltpu.VMEM((NS * FIELD_BLOCK, LANES), F32),
            pltpu.SemaphoreType.DMA((1 + 3 * ROWS // FACE_ROWS,)),
        ],
        compiler_params=params(32),
        cost_estimate=pl.CostEstimate(flops=40_000_000, bytes_accessed=30_000_000, transcendentals=0),
        name="make_fields",
    )(received)


def solve_kernel(
    r_hbm,
    near_ref,
    fr_hbm,
    fc_hbm,
    fp_hbm,
    d_hbm,
    y_ref,
    gram_ref,
    r_ref,
    fr_ref,
    fc_ref,
    fp_ref,
    d_ref,
    ua_ref,
    ub_ref,
    prod_ref,
    side_ref,
    sems,
):
    tiles_copy = pltpu.make_async_copy(r_hbm, r_ref, sems.at[0])
    tiles_copy.start()
    face_copies = []
    for c in range(ROWS // FACE_ROWS):
        at = pl.ds(c * FACE_ROWS, FACE_ROWS)
        face_copies.append(
            [
                pltpu.make_async_copy(src.at[:, at], dst.at[:, at], sems.at[2 + 3 * c + n])
                for n, (src, dst) in enumerate(((fr_hbm, fr_ref), (fc_hbm, fc_ref), (fp_hbm, fp_ref)))
            ]
        )
    dense_copy = pltpu.make_async_copy(d_hbm, d_ref, sems.at[1])
    odd = lax.rem(lax.axis_index("sketch"), 2)
    zero8 = jnp.zeros((8, LANES), F32)
    for ref in (ua_ref, ub_ref):
        for p in range(2):

            def clear(i, carry, p=p, ref=ref):
                ref[p, i, 0:8, :] = zero8
                ref[p, i, 8 + COLS : 16 + COLS, :] = zero8
                return carry

            lax.fori_loop(0, ROWS, clear, 0)
    tiles_copy.wait()
    core = lax.rem(lax.axis_index("pde"), 2)

    def fetch(n):
        for copy in (face_copies + [[dense_copy]])[n]:
            copy.start()

    fetch(0)
    fetch(1)

    def unpack(ref, stride, row, ur, col):
        turned = ref[pl.ds(row, LANES, stride=stride), :].T
        for g in range(16):
            m = (g - (col // 8 - 1)) % 16
            ua_ref[lax.rem(m // 8 + odd, 2), ur * 8 + m % 8, pl.ds(8 + col, 8), :] = turned[8 * g : 8 * g + 8]

    for ref, stride, ur in ((r_ref, BLOCK, 4 - 3 * core), (near_ref, EDGE, 5 - 5 * core)):
        for uc in range(8):
            unpack(ref, stride, uc, ur, HALO + 8 * uc)
        unpack(ref, stride, 8, ur, 0)
        unpack(ref, stride, 9, ur, HALO + CORE_C)

    def rows(q, carry):
        ur = q + 2 * core
        for uc in range(8):
            unpack(r_ref, BLOCK, EDGE + 8 * q + uc, ur, HALO + 8 * uc)
        unpack(r_ref, BLOCK, EDGE + 32 + q, ur, 0)
        unpack(r_ref, BLOCK, EDGE + 36 + q, ur, HALO + CORE_C)
        return carry

    lax.fori_loop(0, 2, rows, 0)
    fetch(2)
    lax.fori_loop(2, 4, rows, 0)

    def keep(i, carry):
        for p in range(2):
            for cb in range(8):
                prod_ref[p, i, pl.ds(8 * cb, 8), :] = (
                    PRIOR_WEIGHT * ua_ref[p, i + HALO, pl.ds(8 + HALO + 8 * cb, 8), :]
                )
        return carry

    lax.fori_loop(0, CORE_R, keep, 0)

    def advance(src, dst, step, blocks):
        last = step == 2 * STEPS

        def flow(p, i, cb):
            at = pl.ds(8 + 8 * cb, 8)
            return fr_ref[p, i, pl.ds(8 * cb, 8), :] * (src[p, i + 1, at, :] - src[p, i, at, :])

        mids = [pl.ds(8 + 8 * cb, 8) for cb in blocks]

        def beside(n, i):
            return (
                pltpu.roll(src[0, i, mids[n], :], LANES - 1, 1),
                pltpu.roll(src[1, i, mids[n], :], 1, 1),
            )

        def some_rows(first, count, carry):
            flows, beyond = carry
            for slot in range(count):
                i = first + slot
                new_flows = []
                new_beyond = []
                for n, (cb, mid) in enumerate(zip(blocks, mids)):
                    at = pl.ds(8 * cb, 8)
                    right = pl.ds(9 + 8 * cb, 8)
                    left = pl.ds(7 + 8 * cb, 8)
                    u = [src[p, i, mid, :] for p in range(2)]
                    new = []
                    for p in range(2):
                        row_flow = fr_ref[p, i, at, :] * (src[p, i + 1, mid, :] - u[p])
                        change = row_flow - flows[2 * n + p]
                        new_flows.append(row_flow)
                        to_right = fc_ref[p, i, mid, :] * (src[p, i, right, :] - u[p])
                        if VIA_SCRATCH:
                            side_ref[slot, p, mid, :] = to_right
                            if n == 0:
                                from_left = fc_ref[p, i, left, :] * (u[p] - src[p, i, left, :])
                            else:
                                from_left = side_ref[slot, p, left, :]
                            change += to_right - from_left
                        else:
                            change += to_right
                            change += fc_ref[p, i, left, :] * (src[p, i, left, :] - u[p])
                        new.append(u[p] + change)
                    new_beyond.append(beside(n, i + 1))
                    inner = fp_ref[0, i, at, :] * (u[1] - u[0])
                    below = fp_ref[2, i, at, :] * (beyond[n][1] - u[0])
                    above = fp_ref[1, i, at, :] * (beyond[n][0] - u[1])
                    both = [new[0] + (below + inner), new[1] + (above - inner)]
                    for p in range(2):
                        if step == STEPS:
                            both[p] = both[p] * d_ref[p, i, at, :]
                        if last:
                            core = pl.ds(8 * (cb - 1), 8)
                            prod_ref[p, i - HALO, core, :] += both[p]
                        else:
                            dst[p, i, mid, :] = both[p]
                flows, beyond = tuple(new_flows), tuple(new_beyond)
            return flows, beyond

        end = ROWS - step
        if step == 1:
            cuts = [step] + [FACE_ROWS * (c + 1) - 3 for c in range(ROWS // FACE_ROWS - 1)] + [end]
        else:
            cuts = [step, end]
        carry = None
        for c, (low, high) in enumerate(zip(cuts[:-1], cuts[1:])):
            if step == 1:
                for copy in face_copies[c]:
                    copy.wait()
                if c < 2:
                    fetch(3 + c)
            if carry is None:
                flows = tuple(flow(p, step - 1, cb) for cb in blocks for p in range(2))
                carry = (flows, tuple(beside(n, step) for n in range(len(blocks))))
            carry = lax.fori_loop(
                0,
                (high - low) // UNROLL,
                lambda t, carry, low=low: some_rows(low + t * UNROLL, UNROLL, carry),
                carry,
            )
            rest = (high - low) % UNROLL
            if rest:
                carry = some_rows(high - rest, rest, carry)

    refs = (ua_ref, ub_ref)
    for step in range(1, 2 * STEPS + 1):
        if step == STEPS:
            dense_copy.wait()
        first, end = (1, 9) if step == 2 * STEPS else (0, 10)
        for at in range(first, end, WIDTH):
            blocks = list(range(at, min(at + WIDTH, end)))
            advance(refs[(step - 1) % 2], refs[step % 2], step, blocks)

    def units(ur, carry):
        for uc in range(8):
            parts = []
            for g in range(16):
                m = (g - uc) % 16
                parts.append(prod_ref[lax.rem(m // 8 + odd, 2), ur * 8 + m % 8, pl.ds(8 * uc, 8), :])
            turned = jnp.concatenate(parts, axis=0).T
            high = turned.astype(BF16)
            at = pl.ds(pl.multiple_of((ur * 8 + uc) * LANES, LANES), LANES)
            y_ref[0:LANES, at] = high
            y_ref[LANES:, at] = (turned - high.astype(F32)).astype(BF16)
        return carry

    lax.fori_loop(0, 4, units, 0)
    both = lax.dot_general(y_ref[0:LANES, :], y_ref[...], (((1,), (1,)), ((), ())), preferred_element_type=F32)
    mixed = both[:, LANES:]
    gram = both[:, :LANES] + (mixed + mixed.T)
    slab_of_row = lax.broadcasted_iota(jnp.int32, (LANES, LANES), 0) & (NS - 1)
    slab_of_lane = lax.broadcasted_iota(jnp.int32, (LANES, LANES), 1) & (NS - 1)
    gram = jnp.where(slab_of_row == slab_of_lane, gram, 0.0)
    by_probe = jnp.sum(gram.reshape(NP, NS, LANES), axis=1)
    same = (
        lax.shift_right_logical(lax.broadcasted_iota(jnp.int32, (LANES, LANES), 0), 4)
        == lax.shift_right_logical(lax.broadcasted_iota(jnp.int32, (LANES, LANES), 1), 4)
    ).astype(F32)
    by_probe = jnp.dot(by_probe, same, precision=lax.Precision.HIGHEST, preferred_element_type=F32)
    own = (lane_iota() & (NS - 1)) == lax.broadcasted_iota(jnp.int32, (8, LANES), 0)
    row = jnp.sum(jnp.where(own, by_probe, 0.0), axis=0, keepdims=True)
    gram_ref[...] = jnp.broadcast_to(row, (LANES, LANES))


def solve(received, near, faces):
    vmem = pl.BlockSpec(memory_space=VMEM)
    hbm = pl.BlockSpec(memory_space=pltpu.HBM)
    received, *faces = in_hbm(received, *faces)
    return pl.pallas_call(
        solve_kernel,
        in_specs=[hbm, vmem] + [hbm] * 4,
        out_specs=[vmem] * 2,
        out_shape=[
            jax.ShapeDtypeStruct((2 * LANES, 32 * LANES), BF16),
            jax.ShapeDtypeStruct((LANES, LANES), F32),
        ],
        scratch_shapes=[
            pltpu.VMEM((128 * BLOCK, LANES), F32),
            pltpu.VMEM((2, ROWS, COLS, LANES), F32),
            pltpu.VMEM((2, ROWS, COLS + 8, LANES), F32),
            pltpu.VMEM((3, ROWS, COLS, LANES), F32),
            pltpu.VMEM((2, ROWS, COLS, LANES), F32),
            pltpu.VMEM((2, ROWS, COLS + 16, LANES), F32),
            pltpu.VMEM((2, ROWS, COLS + 16, LANES), F32),
            pltpu.VMEM((2, CORE_R, CORE_C, LANES), F32),
            pltpu.VMEM((UNROLL, 2, COLS + 8, LANES), F32),
            pltpu.SemaphoreType.DMA((2 + 3 * ROWS // FACE_ROWS,)),
        ],
        compiler_params=params(42),
        cost_estimate=pl.CostEstimate(flops=100_000_000, bytes_accessed=30_000_000, transcendentals=0),
        name="solve",
    )(received, near, *faces)


def basis_kernel(gram_ref, y_ref, o_ref, factor_ref, *, cells):
    lanes = lane_iota()
    sublanes = lax.broadcasted_iota(jnp.int32, (8, LANES), 0)
    total = gram_ref[0:8, :]
    for i in range(1, LANES // 8):
        total = total + gram_ref[8 * i : 8 * i + 8, :]
    row = jnp.broadcast_to(jnp.sum(total, axis=0, keepdims=True), (8, LANES)) / cells

    def entry(i, j):
        at = j * NS + i
        return jnp.broadcast_to(row[:, at : at + 1], (8, LANES))

    lower = {}
    inv_diag = []
    for j in range(NP):
        pivot = entry(j, j)
        for m in range(j):
            pivot = pivot - lower[j, m] * lower[j, m]
        lower[j, j] = jnp.sqrt(pivot)
        inv_diag.append(1.0 / lower[j, j])
        for i in range(j + 1, NP):
            value = entry(i, j)
            for m in range(j):
                value = value - lower[i, m] * lower[j, m]
            lower[i, j] = value * inv_diag[j]
    inverse = {}
    for i in range(NP):
        inverse[i, i] = inv_diag[i]
        for j in range(i):
            carried = lower[i, j] * inverse[j, j]
            for m in range(j + 1, i):
                carried = carried + lower[i, m] * inverse[m, j]
            inverse[i, j] = -carried * inv_diag[i]

    factor = jnp.zeros((8, LANES), F32)
    for (i, j), value in lower.items():
        factor = jnp.where((sublanes == j) & (lanes == i), value, factor)
    factor_ref[...] = factor

    probe = lax.shift_right_logical(lanes, 4)
    mix = []
    for i in range(NP):
        coef = jnp.zeros((8, LANES), F32)
        for j in range(i + 1):
            coef = jnp.where(probe == j, inverse[i, j], coef)
        for half in range(2):
            mix.append(jnp.where((lanes & (NS - 1)) == sublanes + 8 * half, coef, 0.0))
    mix = jnp.concatenate(mix, axis=0)
    high = mix.astype(BF16)
    low = (mix - high.astype(F32)).astype(BF16)
    twice = jnp.concatenate([high, high], axis=1)

    def units(ur, carry):
        for uc in range(8):
            at = pl.ds(pl.multiple_of((ur * 8 + uc) * LANES, LANES), LANES)
            o_ref[pl.ds(ur * 8 + uc, LANES, stride=32), :] = jnp.dot(
                twice, y_ref[:, at], preferred_element_type=F32
            ) + jnp.dot(low, y_ref[0:LANES, at], preferred_element_type=F32)
        return carry

    lax.fori_loop(0, 4, units, 0)


def make_basis(grams, products):
    cells = float(2 * NS * NY * NZ)
    return pl.pallas_call(
        functools.partial(basis_kernel, cells=cells),
        in_specs=[pl.BlockSpec(memory_space=VMEM)] * 2,
        out_specs=[pl.BlockSpec(memory_space=VMEM)] * 2,
        out_shape=[
            jax.ShapeDtypeStruct((128 * 32, LANES), F32),
            jax.ShapeDtypeStruct((8, LANES), F32),
        ],
        compiler_params=params(10),
        cost_estimate=pl.CostEstimate(flops=10_000_000, bytes_accessed=4_000_000, transcendentals=0),
        name="make_basis",
    )(grams, products)


def unpack_kernel(r_ref, o_ref):
    def group(g, carry):
        parts = [
            r_ref[pl.ds(b * 512 + g * 64 + uc, 8, stride=8), :] for b in range(2) for uc in range(8)
        ]
        turned = gather_groups(parts)
        for p in range(2):
            for r in range(8):
                o_ref[0, p, pl.ds(g * 64 + r, 8, stride=8), :] = turned[p * 8 + r]
        return carry

    lax.fori_loop(0, 8, group, 0, unroll=4)


def unpack_basis(received):
    return pl.pallas_call(
        unpack_kernel,
        grid=(4,),
        in_specs=[pl.BlockSpec((1024, LANES), lambda j: (j, 0))],
        out_specs=pl.BlockSpec((1, 2, NY, LANES), lambda j: (0, 0, 0, j)),
        out_shape=jax.ShapeDtypeStruct((1, 2, NY, NZ), F32),
        compiler_params=params(10),
        cost_estimate=pl.CostEstimate(flops=8_000_000, bytes_accessed=4_000_000, transcendentals=0),
        name="unpack_basis",
    )(received)


def exchange(rows, axes):
    return lax.all_to_all(rows, axes, split_axis=0, concat_axis=0, tiled=True)


def on_device(probes, ply_labels, conductivity, sensors, sensor_weight):
    every = ("sketch", "pde")
    fields = pack_fields(conductivity, ply_labels, sensors, sensor_weight)
    fields, probes = lax.optimization_barrier((fields, probes))
    fields, packed = lax.optimization_barrier((exchange(fields, "pde"), pack_probes(probes)))
    tiles = exchange(packed.reshape(LANES, BLOCK // 2, 2, LANES), every)
    tiles, faces = lax.optimization_barrier((tiles, make_fields(fields)))
    near = lax.ppermute(tiles[:, : EDGE // 2], "pde", [(i, i ^ 1) for i in range(NS)])
    products, gram = solve(tiles.reshape(-1, LANES), near.reshape(-1, LANES), faces)
    grams = exchange(gram, every)
    columns, factor = make_basis(grams, products)
    basis = unpack_basis(exchange(columns, every))
    return (basis, factor[:, :NP])


def solution(mesh):
    placed = (P("sketch", "pde", None, None), P("pde", None, None), P(), P("pde"), P("pde"))
    return jax.shard_map(
        on_device,
        mesh=mesh,
        in_specs=placed,
        out_specs=(P("sketch", "pde", None, None), P()),
        check_vma=False,
    )
```

```python
import functools

import jax
import jax.numpy as jnp
from jax import lax
from jax.experimental import pallas as pl
from jax.experimental.pallas import tpu as pltpu
from jax.sharding import PartitionSpec as P

STEPS = 4
TIME_STEP = 0.15
PRIOR_WEIGHT = 0.1

F32 = jnp.float32
BF16 = jnp.bfloat16
LANES = 128
NP = 8
NS = 16
NY = 512
NZ = 512
NU = 64
HALO = 8
ROWS = 48
COLS = 80
CORE_R = 32
CORE_C = 64
BLOCK = 50
EDGE = 10
FIELD_BLOCK = 64
LIST_ROWS = 16
SLAB_BLOCK = FIELD_BLOCK + 2 * LIST_ROWS
VMEM = pltpu.MemorySpace.VMEM
UNROLL = 4
WIDTH = 10
VIA_SCRATCH = False


def params(mebibytes):
    return pltpu.CompilerParams(vmem_limit_bytes=mebibytes * 1024 * 1024)


def in_hbm(*arrays):
    return [pltpu.with_memory_space_constraint(array, pltpu.HBM) for array in arrays]


def lane_iota(shape=(8, LANES)):
    return lax.broadcasted_iota(jnp.int32, shape, len(shape) - 1)


def scatter_groups(parts):
    group = lax.shift_right_logical(lane_iota(), 3)
    parts = [pltpu.roll(part, 8 * m, 1) if m else part for m, part in enumerate(parts)]
    for bit in range(4):
        ahead = (group & (1 << bit)) != 0
        parts = [jnp.where(ahead, parts[(i + (1 << bit)) % 16], parts[i]) for i in range(16)]
    return [parts[(-u) % 16] for u in range(16)]


def gather_groups(parts):
    group = lax.shift_right_logical(lane_iota(), 3)
    parts = [parts[(-i) % 16] for i in range(16)]
    for bit in range(4):
        behind = (group & (1 << bit)) != 0
        parts = [jnp.where(behind, parts[(i - (1 << bit)) % 16], parts[i]) for i in range(16)]
    return [pltpu.roll(part, LANES - 8 * m, 1) if m else part for m, part in enumerate(parts)]


def pack_probes_kernel(x_ref, o_hbm, o_ref, u_ref, sems):
    step = pl.program_id(0)
    cols = NU

    @pl.when(step == 0)
    def _():
        u_ref[0:cols, :] = jnp.zeros((cols, LANES), F32)
        u_ref[cols * (NU + 1) : cols * (NU + 4), :] = jnp.zeros((3 * cols, LANES), F32)

    def part(b):
        at = pl.ds(b * NS * BLOCK, NS * BLOCK)
        return pltpu.make_async_copy(o_ref.at[at, :], o_hbm.at[at, :], sems.at[b])

    def group(g, carry):
        parts = [
            x_ref[0, p, pl.ds(g * 64 + r, 8, stride=8), :] for p in range(2) for r in range(8)
        ]
        for uc, part in enumerate(scatter_groups(parts)):
            u_ref[pl.ds((1 + 8 * g) * cols + 16 * step + uc, 8, stride=cols), :] = part
        return carry

    lax.fori_loop(0, 8, group, 0)

    @pl.when(step == 3)
    def _():
        for b in range(8):

            def tile(a, carry, b=b):
                out = (b * NS + a) * BLOCK
                core = lax.rem(a, 2)
                edge = (4 * a + 4 - 3 * core) * cols + 8 * b
                inner = (4 * a + 2 * core) * cols + 8 * b
                o_ref[pl.ds(out, 8), :] = u_ref[pl.ds(pl.multiple_of(edge, 8), 8), :]
                for q in range(4):
                    o_ref[pl.ds(out + EDGE + 8 * q, 8), :] = u_ref[
                        pl.ds(pl.multiple_of(inner + q * cols, 8), 8), :
                    ]
                for side, offset in enumerate((-1, 8)):
                    if 0 <= 8 * b + offset < cols:
                        one = u_ref[pl.ds(edge + offset, 1), :]
                        four = u_ref[pl.ds(inner + offset, 4, stride=cols), :]
                    else:
                        one = jnp.zeros((1, LANES), F32)
                        four = jnp.zeros((4, LANES), F32)
                    o_ref[pl.ds(out + 8 + side, 1), :] = one
                    o_ref[pl.ds(out + EDGE + 32 + 4 * side, 4), :] = four
                return carry

            lax.fori_loop(0, NS, tile, 0)
            part(b).start()
        for b in range(8):
            part(b).wait()


def pack_probes(probes):
    return pl.pallas_call(
        pack_probes_kernel,
        grid=(4,),
        in_specs=[pl.BlockSpec((1, 2, NY, LANES), lambda j: (0, 0, 0, j))],
        out_specs=pl.BlockSpec(memory_space=pltpu.HBM),
        out_shape=pltpu.HBM((128 * BLOCK, LANES), F32),
        scratch_shapes=[
            pltpu.VMEM((128 * BLOCK, LANES), F32),
            pltpu.VMEM((NU * (NU + 4), LANES), F32),
            pltpu.SemaphoreType.DMA((8,)),
        ],
        compiler_params=params(14),
        cost_estimate=pl.CostEstimate(flops=8_000_000, bytes_accessed=12_000_000, transcendentals=0),
        name="pack_probes",
    )(probes)


def pack_fields_kernel(
    kinds_hbm, label_hbm, sensor_hbm, weight_hbm, o_ref, kinds_ref, sensor_ref, weight_ref, label_ref, cond_ref, u_ref, sems
):
    k = lax.axis_index("sketch")
    lanes = lane_iota()
    shift = 8 + 64 * lax.rem(k, 2)
    first = lax.div(k + 1, 2) - 1
    start = jnp.clip(first, 0, 2)
    window_hbm = label_hbm.at[:, :, pl.ds(pl.multiple_of(start * LANES, LANES), 2 * LANES)]
    upper, lower = pl.ds(0, NY // 2), pl.ds(NY // 2, NY // 2)
    copies = [
        pltpu.make_async_copy(src, dst, sems.at[i])
        for i, (src, dst) in enumerate(
            (
                (window_hbm.at[:, upper], label_ref.at[:, upper]),
                (window_hbm.at[:, lower], label_ref.at[:, lower]),
                (kinds_hbm, kinds_ref),
                (sensor_hbm, sensor_ref),
                (weight_hbm, weight_ref),
            )
        )
    ]
    for copy in copies:
        copy.start()
    cols = 16
    u_ref[0:cols, :] = jnp.zeros((cols, LANES), F32)
    u_ref[cols * (NU + 1) :, :] = jnp.zeros((3 * cols, LANES), F32)
    copies[0].wait()
    copies[2].wait()
    place = first - start
    first_at = pl.multiple_of(jnp.maximum(place, 0) * LANES, LANES)
    second_at = pl.multiple_of(jnp.minimum(place + 1, 1) * LANES, LANES)
    from_first = lanes < shift
    outside = (from_first & (first < 0)) | ((lanes >= shift) & (first + 1 > 3))

    def window(i, carry):
        for q in range(8):
            rows = pl.ds(pl.multiple_of(i * 64 + q * 8, 8), 8)
            for p in range(2):
                a = label_ref[p, rows, pl.ds(first_at, LANES)]
                b = label_ref[p, rows, pl.ds(second_at, LANES)]
                label = jnp.where(from_first, pltpu.roll(a, shift, 1), pltpu.roll(b, shift, 1))
                cond = jnp.zeros((8, LANES), F32)
                for kind in range(8):
                    cond = jnp.where(label == kind, kinds_ref[kind], cond)
                cond_ref[p, rows, :] = jnp.where(outside, 0.0, cond)
        return carry

    lax.fori_loop(0, NU // 16, window, 0)
    copies[1].wait()
    lax.fori_loop(NU // 16, NU // 8, window, 0)

    def group(g, carry):
        parts = [cond_ref[p, pl.ds(g * 64 + r, 8, stride=8), :] for p in range(2) for r in range(8)]
        for uc, part in enumerate(scatter_groups(parts)):
            if uc < 10:
                slot = (uc - 1) % 16
                u_ref[pl.ds((1 + 8 * g) * cols + slot, 8, stride=cols), :] = part
        return carry

    lax.fori_loop(0, 8, group, 0, unroll=4)

    copies[3].wait()
    copies[4].wait()
    cells = sensor_ref[...].astype(F32)
    weights = weight_ref[...]

    def tile(a, carry):
        out = a * SLAB_BLOCK
        at = 4 * a * cols
        for i in range(6):
            o_ref[pl.ds(out + 8 * i, 8), :] = u_ref[pl.ds(pl.multiple_of(at + i * cols, 8), 8), :]
        o_ref[pl.ds(out + 48, 8), :] = u_ref[pl.ds(at + 15, 8, stride=cols), :]
        o_ref[pl.ds(out + 56, 8), :] = u_ref[pl.ds(at + 8, 8, stride=cols), :]
        o_ref[pl.ds(out + FIELD_BLOCK, LIST_ROWS), :] = cells
        o_ref[pl.ds(out + FIELD_BLOCK + LIST_ROWS, LIST_ROWS), :] = weights
        return carry

    lax.fori_loop(0, NS, tile, 0)


def pack_fields(conductivity, labels, sensors, weights):
    return pl.pallas_call(
        pack_fields_kernel,
        in_specs=[pl.BlockSpec(memory_space=pltpu.HBM)] * 4,
        out_specs=pl.BlockSpec(memory_space=VMEM),
        out_shape=jax.ShapeDtypeStruct((NS * SLAB_BLOCK, LANES), F32),
        scratch_shapes=[
            pltpu.SMEM((8,), F32),
            pltpu.VMEM((LIST_ROWS, LANES), jnp.int32),
            pltpu.VMEM((LIST_ROWS, LANES), F32),
            pltpu.VMEM((2, NY, 2 * LANES), jnp.int32),
            pltpu.VMEM((2, NY, LANES), F32),
            pltpu.VMEM((16 * (NU + 4), LANES), F32),
            pltpu.SemaphoreType.DMA((5,)),
        ],
        compiler_params=params(10),
        cost_estimate=pl.CostEstimate(flops=8_000_000, bytes_accessed=12_000_000, transcendentals=0),
        name="pack_fields",
    )(*in_hbm(conductivity, labels, sensors.reshape(LIST_ROWS, LANES), weights.reshape(LIST_ROWS, LANES)))


def harmonic(left, right):
    total = jnp.maximum(left + right, 1e-30)
    return (2.0 * TIME_STEP) * left * right / total


FACE_ROWS = 12


def fields_kernel(r_ref, *refs):
    outs, refs = refs[:4], refs[4:]
    fr_ref, fc_ref, fp_ref, d_ref, cond_ref, unit_ref, place_ref, dense_ref, out_sems = refs
    row_0 = 32 * lax.axis_index("pde") - HALO
    col_0 = 64 * lax.axis_index("sketch") - HALO

    def slab(n, carry):
        at = pl.multiple_of(n * SLAB_BLOCK + FIELD_BLOCK, 8)
        cell = r_ref[pl.ds(at, LIST_ROWS), :].astype(jnp.int32)
        weight = r_ref[pl.ds(at + LIST_ROWS, LIST_ROWS), :]
        high = weight.astype(BF16).astype(F32)
        rest = weight - high
        row = (lax.shift_right_logical(cell, 9) & (NY - 1)) - row_0
        col = (cell & (NZ - 1)) - col_0
        inside = (row >= 0) & (row < ROWS) & (col >= 0) & (col < COLS)
        ur = lax.shift_right_arithmetic(row, 3)
        uc = lax.shift_right_arithmetic(col, 3)
        unit = jnp.where(uc == 0, 48 + ur, jnp.where(uc == 9, 56 + ur, 8 * ur + uc - 1))
        unit = jnp.where(inside, unit, -1)
        place = 64 * lax.shift_right_logical(cell, 18) + 8 * (row & 7) + (col & 7)
        unit_index = lax.broadcasted_iota(jnp.int32, (FIELD_BLOCK, LANES), 0)
        place_index = lax.broadcasted_iota(jnp.int32, (LANES, LANES), 0)
        for j in range(LIST_ROWS):
            span = pl.ds(j * LANES, LANES)
            unit_ref[:, span] = jnp.where(unit_index == unit[j : j + 1], 1.0, 0.0).astype(BF16)
            hit = place_index == place[j : j + 1]
            place_ref[0:LANES, span] = jnp.where(hit, high[j : j + 1], 0.0).astype(BF16)
            place_ref[LANES:, span] = jnp.where(hit, rest[j : j + 1], 0.0).astype(BF16)
        got = lax.dot_general(
            unit_ref[...], place_ref[...], (((1,), (1,)), ((), ())), preferred_element_type=F32
        )
        dense_ref[pl.ds(pl.multiple_of(n * FIELD_BLOCK, 8), FIELD_BLOCK), :] = got[:, :LANES] + got[:, LANES:]
        return carry

    lax.fori_loop(0, NS, slab, 0)
    zero8 = jnp.zeros((8, LANES), F32)
    for p in range(2):

        def clear(i, carry, p=p):
            cond_ref[p, i, COLS : COLS + 8, :] = zero8
            fc_ref[p, i, 0:8, :] = zero8
            return carry

        lax.fori_loop(0, ROWS, clear, 0)

    def unpack(src, stride, turn, ref, row, ur, col):
        block = src[pl.ds(row, NS, stride=stride), :]
        turned = jnp.concatenate([block] * NP, axis=0).T
        for g in range(16):
            m = (g - turn * (col // 8)) % 16
            ref[m // 8, ur * 8 + m % 8, pl.ds(col, 8), :] = turned[8 * g : 8 * g + 8]

    for what in ((dense_ref, FIELD_BLOCK, 0, d_ref), (r_ref, SLAB_BLOCK, 1, cond_ref)):

        def rows(ur, carry, what=what):
            for uc in range(8):
                unpack(*what, ur * 8 + uc, ur, HALO + 8 * uc)
            unpack(*what, 48 + ur, ur, 0)
            unpack(*what, 56 + ur, ur, HALO + CORE_C)
            return carry

        lax.fori_loop(0, 6, rows, 0)

    last_slab = (lane_iota() & (NS - 1)) == NS - 1

    def faces(i, carry):
        nxt = jnp.minimum(i + 1, ROWS - 1)
        for cb in range(10):
            at = pl.ds(8 * cb, 8)
            c0, c1 = cond_ref[0, i, at, :], cond_ref[1, i, at, :]
            fr_ref[0, i, at, :] = harmonic(c0, cond_ref[0, nxt, at, :])
            fr_ref[1, i, at, :] = harmonic(c1, cond_ref[1, nxt, at, :])
            aside = pl.ds(8 * cb + 1, 8)
            fc_ref[0, i, pl.ds(8 + 8 * cb, 8), :] = harmonic(c0, cond_ref[0, i, aside, :])
            fc_ref[1, i, pl.ds(8 + 8 * cb, 8), :] = harmonic(c1, cond_ref[1, i, aside, :])
            fp_ref[0, i, at, :] = harmonic(c0, c1)
            beyond = pltpu.roll(c0, LANES - 1, 1)
            outer = jnp.where(last_slab, 0.0, harmonic(c1, beyond))
            fp_ref[1, i, at, :] = outer
            fp_ref[2, i, at, :] = pltpu.roll(outer, 1, 1)
        return carry

    copies = [pltpu.make_async_copy(d_ref, outs[3], out_sems.at[0])]
    copies[0].start()
    for first in range(0, ROWS, FACE_ROWS):
        lax.fori_loop(first, first + FACE_ROWS, faces, 0)
        for ref, out in zip((fr_ref, fc_ref, fp_ref), outs):
            at = pl.ds(first, FACE_ROWS)
            copy = pltpu.make_async_copy(ref.at[:, at], out.at[:, at], out_sems.at[len(copies)])
            copy.start()
            copies.append(copy)
    for copy in copies:
        copy.wait()


def make_fields(received):
    shapes = [(2, ROWS, COLS, LANES), (2, ROWS, COLS + 8, LANES), (3, ROWS, COLS, LANES), (2, ROWS, COLS, LANES)]
    return pl.pallas_call(
        fields_kernel,
        in_specs=[pl.BlockSpec(memory_space=VMEM)],
        out_specs=[pl.BlockSpec(memory_space=pltpu.HBM)] * 4,
        out_shape=[pltpu.HBM(shape, F32) for shape in shapes],
        scratch_shapes=[
            *[pltpu.VMEM(shape, F32) for shape in shapes],
            pltpu.VMEM((2, ROWS, COLS + 8, LANES), F32),
            pltpu.VMEM((FIELD_BLOCK, 2048), BF16),
            pltpu.VMEM((2 * LANES, 2048), BF16),
            pltpu.VMEM((NS * FIELD_BLOCK, LANES), F32),
            pltpu.SemaphoreType.DMA((1 + 3 * ROWS // FACE_ROWS,)),
        ],
        compiler_params=params(32),
        cost_estimate=pl.CostEstimate(flops=40_000_000, bytes_accessed=30_000_000, transcendentals=0),
        name="make_fields",
    )(received)


def solve_kernel(
    r_hbm,
    near_ref,
    fr_hbm,
    fc_hbm,
    fp_hbm,
    d_hbm,
    y_ref,
    gram_ref,
    r_ref,
    fr_ref,
    fc_ref,
    fp_ref,
    d_ref,
    ua_ref,
    ub_ref,
    prod_ref,
    side_ref,
    sems,
):
    tiles_copy = pltpu.make_async_copy(r_hbm, r_ref, sems.at[0])
    tiles_copy.start()
    face_copies = []
    for c in range(ROWS // FACE_ROWS):
        at = pl.ds(c * FACE_ROWS, FACE_ROWS)
        face_copies.append(
            [
                pltpu.make_async_copy(src.at[:, at], dst.at[:, at], sems.at[2 + 3 * c + n])
                for n, (src, dst) in enumerate(((fr_hbm, fr_ref), (fc_hbm, fc_ref), (fp_hbm, fp_ref)))
            ]
        )
    dense_copy = pltpu.make_async_copy(d_hbm, d_ref, sems.at[1])
    odd = lax.rem(lax.axis_index("sketch"), 2)
    zero8 = jnp.zeros((8, LANES), F32)
    for ref in (ua_ref, ub_ref):
        for p in range(2):

            def clear(i, carry, p=p, ref=ref):
                ref[p, i, 0:8, :] = zero8
                ref[p, i, 8 + COLS : 16 + COLS, :] = zero8
                return carry

            lax.fori_loop(0, ROWS, clear, 0)
    tiles_copy.wait()
    core = lax.rem(lax.axis_index("pde"), 2)

    def fetch(n):
        for copy in (face_copies + [[dense_copy]])[n]:
            copy.start()

    fetch(0)
    fetch(1)

    def unpack(ref, stride, row, ur, col):
        turned = ref[pl.ds(row, LANES, stride=stride), :].T
        for g in range(16):
            m = (g - (col // 8 - 1)) % 16
            ua_ref[lax.rem(m // 8 + odd, 2), ur * 8 + m % 8, pl.ds(8 + col, 8), :] = turned[8 * g : 8 * g + 8]

    for ref, stride, ur in ((r_ref, BLOCK, 4 - 3 * core), (near_ref, EDGE, 5 - 5 * core)):
        for uc in range(8):
            unpack(ref, stride, uc, ur, HALO + 8 * uc)
        unpack(ref, stride, 8, ur, 0)
        unpack(ref, stride, 9, ur, HALO + CORE_C)

    def rows(q, carry):
        ur = q + 2 * core
        for uc in range(8):
            unpack(r_ref, BLOCK, EDGE + 8 * q + uc, ur, HALO + 8 * uc)
        unpack(r_ref, BLOCK, EDGE + 32 + q, ur, 0)
        unpack(r_ref, BLOCK, EDGE + 36 + q, ur, HALO + CORE_C)
        return carry

    lax.fori_loop(0, 2, rows, 0, unroll=2)
    fetch(2)
    lax.fori_loop(2, 4, rows, 0, unroll=2)

    def keep(i, carry):
        for p in range(2):
            for cb in range(8):
                prod_ref[p, i, pl.ds(8 * cb, 8), :] = (
                    PRIOR_WEIGHT * ua_ref[p, i + HALO, pl.ds(8 + HALO + 8 * cb, 8), :]
                )
        return carry

    lax.fori_loop(0, CORE_R, keep, 0)

    def advance(src, dst, step, blocks):
        last = step == 2 * STEPS

        def flow(p, i, cb):
            at = pl.ds(8 + 8 * cb, 8)
            return fr_ref[p, i, pl.ds(8 * cb, 8), :] * (src[p, i + 1, at, :] - src[p, i, at, :])

        mids = [pl.ds(8 + 8 * cb, 8) for cb in blocks]

        def beside(n, i):
            return (
                pltpu.roll(src[0, i, mids[n], :], LANES - 1, 1),
                pltpu.roll(src[1, i, mids[n], :], 1, 1),
            )

        def some_rows(first, count, carry):
            flows, beyond = carry
            for slot in range(count):
                i = first + slot
                new_flows = []
                new_beyond = []
                for n, (cb, mid) in enumerate(zip(blocks, mids)):
                    at = pl.ds(8 * cb, 8)
                    right = pl.ds(9 + 8 * cb, 8)
                    left = pl.ds(7 + 8 * cb, 8)
                    u = [src[p, i, mid, :] for p in range(2)]
                    new = []
                    for p in range(2):
                        row_flow = fr_ref[p, i, at, :] * (src[p, i + 1, mid, :] - u[p])
                        change = row_flow - flows[2 * n + p]
                        new_flows.append(row_flow)
                        to_right = fc_ref[p, i, mid, :] * (src[p, i, right, :] - u[p])
                        if VIA_SCRATCH:
                            side_ref[slot, p, mid, :] = to_right
                            if n == 0:
                                from_left = fc_ref[p, i, left, :] * (u[p] - src[p, i, left, :])
                            else:
                                from_left = side_ref[slot, p, left, :]
                            change += to_right - from_left
                        else:
                            change += to_right
                            change += fc_ref[p, i, left, :] * (src[p, i, left, :] - u[p])
                        new.append(u[p] + change)
                    new_beyond.append(beside(n, i + 1))
                    inner = fp_ref[0, i, at, :] * (u[1] - u[0])
                    below = fp_ref[2, i, at, :] * (beyond[n][1] - u[0])
                    above = fp_ref[1, i, at, :] * (beyond[n][0] - u[1])
                    both = [new[0] + (below + inner), new[1] + (above - inner)]
                    for p in range(2):
                        if step == STEPS:
                            both[p] = both[p] * d_ref[p, i, at, :]
                        if last:
                            core = pl.ds(8 * (cb - 1), 8)
                            prod_ref[p, i - HALO, core, :] += both[p]
                        else:
                            dst[p, i, mid, :] = both[p]
                flows, beyond = tuple(new_flows), tuple(new_beyond)
            return flows, beyond

        end = ROWS - step
        if step == 1:
            cuts = [step] + [FACE_ROWS * (c + 1) - 3 for c in range(ROWS // FACE_ROWS - 1)] + [end]
        else:
            cuts = [step, end]
        carry = None
        for c, (low, high) in enumerate(zip(cuts[:-1], cuts[1:])):
            if step == 1:
                for copy in face_copies[c]:
                    copy.wait()
                if c < 2:
                    fetch(3 + c)
            if carry is None:
                flows = tuple(flow(p, step - 1, cb) for cb in blocks for p in range(2))
                carry = (flows, tuple(beside(n, step) for n in range(len(blocks))))
            carry = lax.fori_loop(
                0,
                (high - low) // UNROLL,
                lambda t, carry, low=low: some_rows(low + t * UNROLL, UNROLL, carry),
                carry,
            )
            rest = (high - low) % UNROLL
            if rest:
                carry = some_rows(high - rest, rest, carry)

    refs = (ua_ref, ub_ref)
    for step in range(1, 2 * STEPS + 1):
        if step == STEPS:
            dense_copy.wait()
        first, end = (1, 9) if step == 2 * STEPS else (0, 10)
        for at in range(first, end, WIDTH):
            blocks = list(range(at, min(at + WIDTH, end)))
            advance(refs[(step - 1) % 2], refs[step % 2], step, blocks)

    def units(ur, carry):
        for uc in range(8):
            parts = []
            for g in range(16):
                m = (g - uc) % 16
                parts.append(prod_ref[lax.rem(m // 8 + odd, 2), ur * 8 + m % 8, pl.ds(8 * uc, 8), :])
            turned = jnp.concatenate(parts, axis=0).T
            high = turned.astype(BF16)
            at = pl.ds(pl.multiple_of((ur * 8 + uc) * LANES, LANES), LANES)
            y_ref[0:LANES, at] = high
            y_ref[LANES:, at] = (turned - high.astype(F32)).astype(BF16)
        return carry

    lax.fori_loop(0, 4, units, 0, unroll=2)
    both = lax.dot_general(y_ref[0:LANES, :], y_ref[...], (((1,), (1,)), ((), ())), preferred_element_type=F32)
    mixed = both[:, LANES:]
    gram = both[:, :LANES] + (mixed + mixed.T)
    slab_of_row = lax.broadcasted_iota(jnp.int32, (LANES, LANES), 0) & (NS - 1)
    slab_of_lane = lax.broadcasted_iota(jnp.int32, (LANES, LANES), 1) & (NS - 1)
    gram = jnp.where(slab_of_row == slab_of_lane, gram, 0.0)
    by_probe = jnp.sum(gram.reshape(NP, NS, LANES), axis=1)
    same = (
        lax.shift_right_logical(lax.broadcasted_iota(jnp.int32, (LANES, LANES), 0), 4)
        == lax.shift_right_logical(lax.broadcasted_iota(jnp.int32, (LANES, LANES), 1), 4)
    ).astype(F32)
    by_probe = jnp.dot(by_probe, same, precision=lax.Precision.HIGHEST, preferred_element_type=F32)
    own = (lane_iota() & (NS - 1)) == lax.broadcasted_iota(jnp.int32, (8, LANES), 0)
    row = jnp.sum(jnp.where(own, by_probe, 0.0), axis=0, keepdims=True)
    gram_ref[...] = jnp.broadcast_to(row, (LANES, LANES))


def solve(received, near, faces):
    vmem = pl.BlockSpec(memory_space=VMEM)
    hbm = pl.BlockSpec(memory_space=pltpu.HBM)
    received, *faces = in_hbm(received, *faces)
    return pl.pallas_call(
        solve_kernel,
        in_specs=[hbm, vmem] + [hbm] * 4,
        out_specs=[vmem] * 2,
        out_shape=[
            jax.ShapeDtypeStruct((2 * LANES, 32 * LANES), BF16),
            jax.ShapeDtypeStruct((LANES, LANES), F32),
        ],
        scratch_shapes=[
            pltpu.VMEM((128 * BLOCK, LANES), F32),
            pltpu.VMEM((2, ROWS, COLS, LANES), F32),
            pltpu.VMEM((2, ROWS, COLS + 8, LANES), F32),
            pltpu.VMEM((3, ROWS, COLS, LANES), F32),
            pltpu.VMEM((2, ROWS, COLS, LANES), F32),
            pltpu.VMEM((2, ROWS, COLS + 16, LANES), F32),
            pltpu.VMEM((2, ROWS, COLS + 16, LANES), F32),
            pltpu.VMEM((2, CORE_R, CORE_C, LANES), F32),
            pltpu.VMEM((UNROLL, 2, COLS + 8, LANES), F32),
            pltpu.SemaphoreType.DMA((2 + 3 * ROWS // FACE_ROWS,)),
        ],
        compiler_params=params(42),
        cost_estimate=pl.CostEstimate(flops=100_000_000, bytes_accessed=30_000_000, transcendentals=0),
        name="solve",
    )(received, near, *faces)


def basis_kernel(gram_ref, y_ref, o_ref, factor_ref, *, cells):
    lanes = lane_iota()
    sublanes = lax.broadcasted_iota(jnp.int32, (8, LANES), 0)
    total = gram_ref[0:8, :]
    for i in range(1, LANES // 8):
        total = total + gram_ref[8 * i : 8 * i + 8, :]
    row = jnp.broadcast_to(jnp.sum(total, axis=0, keepdims=True), (8, LANES)) / cells

    def entry(i, j):
        at = j * NS + i
        return jnp.broadcast_to(row[:, at : at + 1], (8, LANES))

    lower = {}
    inv_diag = []
    for j in range(NP):
        pivot = entry(j, j)
        for m in range(j):
            pivot = pivot - lower[j, m] * lower[j, m]
        lower[j, j] = jnp.sqrt(pivot)
        inv_diag.append(1.0 / lower[j, j])
        for i in range(j + 1, NP):
            value = entry(i, j)
            for m in range(j):
                value = value - lower[i, m] * lower[j, m]
            lower[i, j] = value * inv_diag[j]
    inverse = {}
    for i in range(NP):
        inverse[i, i] = inv_diag[i]
        for j in range(i):
            carried = lower[i, j] * inverse[j, j]
            for m in range(j + 1, i):
                carried = carried + lower[i, m] * inverse[m, j]
            inverse[i, j] = -carried * inv_diag[i]

    factor = jnp.zeros((8, LANES), F32)
    for (i, j), value in lower.items():
        factor = jnp.where((sublanes == j) & (lanes == i), value, factor)
    factor_ref[...] = factor

    probe = lax.shift_right_logical(lanes, 4)
    mix = []
    for i in range(NP):
        coef = jnp.zeros((8, LANES), F32)
        for j in range(i + 1):
            coef = jnp.where(probe == j, inverse[i, j], coef)
        for half in range(2):
            mix.append(jnp.where((lanes & (NS - 1)) == sublanes + 8 * half, coef, 0.0))
    mix = jnp.concatenate(mix, axis=0)
    high = mix.astype(BF16)
    low = (mix - high.astype(F32)).astype(BF16)
    twice = jnp.concatenate([high, high], axis=1)

    def units(ur, carry):
        for uc in range(8):
            at = pl.ds(pl.multiple_of((ur * 8 + uc) * LANES, LANES), LANES)
            o_ref[pl.ds(ur * 8 + uc, LANES, stride=32), :] = jnp.dot(
                twice, y_ref[:, at], preferred_element_type=F32
            ) + jnp.dot(low, y_ref[0:LANES, at], preferred_element_type=F32)
        return carry

    lax.fori_loop(0, 4, units, 0)


def make_basis(grams, products):
    cells = float(2 * NS * NY * NZ)
    return pl.pallas_call(
        functools.partial(basis_kernel, cells=cells),
        in_specs=[pl.BlockSpec(memory_space=VMEM)] * 2,
        out_specs=[pl.BlockSpec(memory_space=VMEM)] * 2,
        out_shape=[
            jax.ShapeDtypeStruct((128 * 32, LANES), F32),
            jax.ShapeDtypeStruct((8, LANES), F32),
        ],
        compiler_params=params(10),
        cost_estimate=pl.CostEstimate(flops=10_000_000, bytes_accessed=4_000_000, transcendentals=0),
        name="make_basis",
    )(grams, products)


def unpack_kernel(r_ref, o_ref):
    def group(g, carry):
        parts = [
            r_ref[pl.ds(b * 512 + g * 64 + uc, 8, stride=8), :] for b in range(2) for uc in range(8)
        ]
        turned = gather_groups(parts)
        for p in range(2):
            for r in range(8):
                o_ref[0, p, pl.ds(g * 64 + r, 8, stride=8), :] = turned[p * 8 + r]
        return carry

    lax.fori_loop(0, 8, group, 0, unroll=4)


def unpack_basis(received):
    return pl.pallas_call(
        unpack_kernel,
        grid=(4,),
        in_specs=[pl.BlockSpec((1024, LANES), lambda j: (j, 0))],
        out_specs=pl.BlockSpec((1, 2, NY, LANES), lambda j: (0, 0, 0, j)),
        out_shape=jax.ShapeDtypeStruct((1, 2, NY, NZ), F32),
        compiler_params=params(10),
        cost_estimate=pl.CostEstimate(flops=8_000_000, bytes_accessed=4_000_000, transcendentals=0),
        name="unpack_basis",
    )(received)


def exchange(rows, axes):
    return lax.all_to_all(rows, axes, split_axis=0, concat_axis=0, tiled=True)


def on_device(probes, ply_labels, conductivity, sensors, sensor_weight):
    every = ("sketch", "pde")
    fields = pack_fields(conductivity, ply_labels, sensors, sensor_weight)
    fields, probes = lax.optimization_barrier((fields, probes))
    fields, packed = lax.optimization_barrier((exchange(fields, "pde"), pack_probes(probes)))
    tiles = exchange(packed.reshape(LANES, BLOCK // 2, 2, LANES), every)
    tiles, faces = lax.optimization_barrier((tiles, make_fields(fields)))
    near = lax.ppermute(tiles[:, : EDGE // 2], "pde", [(i, i ^ 1) for i in range(NS)])
    products, gram = solve(tiles.reshape(-1, LANES), near.reshape(-1, LANES), faces)
    grams = exchange(gram, every)
    columns, factor = make_basis(grams, products)
    basis = unpack_basis(exchange(columns, every))
    return (basis, factor[:, :NP])


def solution(mesh):
    placed = (P("sketch", "pde", None, None), P("pde", None, None), P(), P("pde"), P("pde"))
    return jax.shard_map(
        on_device,
        mesh=mesh,
        in_specs=placed,
        out_specs=(P("sketch", "pde", None, None), P()),
        check_vma=False,
    )
```
